32 devices in a mesh: tower: 2 (over x), dp: 16 (over z, y, core).
Axes of the slice: x: 2, y: 2, z: 4, core: 2. Of those that a mesh axis runs over, the one named last changes fastest.
Arguments:
- tokens: bfloat16 [2, 6144, 768], P('tower', 'dp'), may hold values from -6 to 6
- lengths: int32 [2, 64], P('tower', 'dp'), may hold values from 1 to 381, as said below
- pos_doc: int32 [64], replicated, may hold values from 0 to 63, each once
- w_qkv: bfloat16 [768, 2304], P('dp'), may hold values from -0.21875 to 0.21875
- w_out: bfloat16 [768, 768], P('dp'), may hold values from -1.75 to 1.75
- w_gate: bfloat16 [768, 3072], P('dp'), may hold values from -0.21875 to 0.21875
- w_up: bfloat16 [768, 3072], P('dp'), may hold values from -0.21875 to 0.21875
- w_down: bfloat16 [3072, 768], P('dp'), may hold values from -0.109375 to 0.109375
- ln1_gain: bfloat16 [768], P('dp'), may hold values from 0.5 to 1.5
- ln1_bias: bfloat16 [768], P('dp'), may hold values from -1.5 to 1.5
- ln2_gain: bfloat16 [768], P('dp'), may hold values from 0.5 to 1.5
- ln2_bias: bfloat16 [768], P('dp'), may hold values from -0.5 to 0.5
Outputs:
- loss: float32 [], replicated
- embeddings: float32 [2, 64, 768], P('tower', 'dp')
- grad_tokens: float32 [2, 6144, 768], P('tower', 'dp')
- grad_w_qkv: float32 [768, 2304], P('dp')
- grad_w_out: float32 [768, 768], P('dp')
- grad_w_gate: float32 [768, 3072], P('dp')
- grad_w_up: float32 [768, 3072], P('dp')
- grad_w_down: float32 [3072, 768], P('dp')
- grad_ln1_gain: float32 [768], P('dp')
- grad_ln1_bias: float32 [768], P('dp')
- grad_ln2_gain: float32 [768], P('dp')
- grad_ln2_bias: float32 [768], P('dp')
The draws below stay inside these ranges and needn't reach their ends.
Inputs may be any that keep to these rules, and one draw needn't show every extreme that they name: Each device's 4 lengths are its sequences in token order and sum to 384; in every draw some device holds a sequence of 381 tokens. A permutation: query i's positive document is document pos_doc[i] of tower 1.
All inputs are finite; a program needn't handle non-finite values.
Results may differ from the reference program's by a relative error of at most 0.012.
Values may be sent and summed in bfloat16 or wider, within the bound.
No kernel may reach another device: no remote copies, remote signals or barrier semaphores. Data moves between devices by JAX's collectives and lax.ppermute only.
A program may use at most 192 MiB of HBM per device.

```python
import jax
import jax.numpy as jnp
from jax import lax

HD = 64
D = 768
FF = 3072
TOK_DEV = 384
SEQ_DEV = 4
NSEQ = 64
TOKENS_T = 6144


def draw_lengths(key, part):
    key = jax.random.fold_in(key, 11)
    groups = 2 * NSEQ // SEQ_DEV
    cut_keys = jax.random.split(key, groups + 1)

    def cuts_for(one_key):
        picked = jax.random.permutation(one_key, TOK_DEV - 1)[:SEQ_DEV - 1].astype(jnp.int32) + 1
        edge_marks = jnp.concatenate([jnp.zeros((1,), jnp.int32), jnp.sort(picked), jnp.full((1,), TOK_DEV, jnp.int32)])
        return edge_marks[1:] - edge_marks[:-1]
    seq_spans = jax.vmap(cuts_for)(cut_keys[1:])
    chosen = jax.random.randint(cut_keys[0], (), 0, groups)
    longest = jnp.concatenate([jnp.full((1,), TOK_DEV - SEQ_DEV + 1, jnp.int32), jnp.ones((SEQ_DEV - 1,), jnp.int32)])
    seq_spans = jnp.where((jnp.arange(groups) == chosen)[:, None], longest[None, :], seq_spans)
    return seq_spans.reshape(2, NSEQ).astype(jnp.int32)


def levels(key, extent, cuts, least, largest):
    def one(dim, shards_of):
        draws = jax.random.uniform(jax.random.fold_in(jax.random.fold_in(key, 6), dim), (shards_of,), jnp.float32, least / len(cuts), largest / len(cuts))
        return jnp.repeat(jnp.exp(draws), extent[dim] // shards_of).reshape((-1,) + (1,) * (len(extent) - dim - 1))

    factor_of = one(*cuts[0])
    for cut in cuts[1:]:
        factor_of = factor_of * one(*cut)
    return factor_of


def bell_draw(stream_key, shape, width, most, cuts=(), kind=jnp.bfloat16):
    array = jax.random.normal(stream_key, shape, jnp.float32) * width
    if len(cuts) > 0:
        array = levels(stream_key, shape, cuts, -0.22, 0.18) * array
    return jnp.clip(array, min=-most, max=most).astype(kind)


def setup_inputs(seed: int = 0) -> dict:
    key_of = jax.random.split(jax.random.key(seed), 13)
    return {
        "tokens": bell_draw(key_of[0], (2, TOKENS_T, D), 1.0, 6.0, ((0, 2), (1, 16))),
        "lengths": draw_lengths(jax.random.fold_in(key_of[12], 71), 0),
        "pos_doc": jax.random.permutation(key_of[2], NSEQ).astype(jnp.int32),
        "w_qkv": bell_draw(key_of[3], (D, 3 * D), D ** -0.5, 0.21875, ((0, 16),)),
        "w_out": bell_draw(key_of[4], (D, D), (D // 64) ** -0.5, 1.75, ((0, 16),)),
        "w_gate": bell_draw(key_of[5], (D, FF), D ** -0.5, 0.21875, ((0, 16),)),
        "w_up": bell_draw(key_of[6], (D, FF), D ** -0.5, 0.21875, ((0, 16),)),
        "w_down": bell_draw(key_of[7], (FF, D), FF ** -0.5, 0.109375, ((0, 16),)),
        "ln1_gain": jnp.clip(1.0 + 0.1 * jax.random.normal(key_of[8], (D,), jnp.float32), 0.5, 1.5).astype(jnp.bfloat16),
        "ln1_bias": bell_draw(key_of[9], (D,), 0.3, 1.5, ((0, 16),)),
        "ln2_gain": jnp.clip(1.0 + 0.1 * jax.random.normal(key_of[10], (D,), jnp.float32), 0.5, 1.5).astype(jnp.bfloat16),
        "ln2_bias": bell_draw(key_of[11], (D,), 0.1, 0.5, ((0, 16),)),
    }


TEMPER = 0.05
EPS_NORM = 1e-05
EPS_UNIT = 1e-06
MASKED = -1e+30

@jax.custom_vjp
def low(v):
    return lax.optimization_barrier(v.astype(jnp.bfloat16)).astype(jnp.float32)

@jax.custom_vjp
def low_back(v):
    return v

def low_keep(v):
    return (low(v), None)

def low_pass(kept, grad):
    return (grad,)

def back_keep(v):
    return (v, None)

def back_low(kept, grad):
    return (low(grad),)
low.defvjp(low_keep, low_pass)
low_back.defvjp(back_keep, back_low)

def matmul_high(left_arr, right_arr):
    return jnp.dot(left_arr, right_arr, precision=lax.Precision.HIGHEST)

def layout(seq_spans, row_count):
    seq_total = seq_spans.shape[0]
    starts = (jnp.cumsum(seq_spans) - seq_spans).astype(jnp.int32)
    places = jnp.arange(row_count, dtype=jnp.int32)
    member = ((places[None, :] >= starts[:, None]) & (places[None, :] < (starts + seq_spans)[:, None])).astype(jnp.int32)
    labels = lax.optimization_barrier(jnp.sum(member * jnp.arange(seq_total, dtype=jnp.int32)[:, None], axis=0))
    offsets = places - lax.optimization_barrier(jnp.sum(member * starts[:, None], axis=0))
    pooling = member.astype(jnp.float32) / seq_spans.astype(jnp.float32)[:, None]
    return (pooling, labels, offsets)

def rotary(offsets, half_size):
    frequency = 1000.0 ** (-jnp.arange(half_size, dtype=jnp.float32) / half_size)
    angles = offsets.astype(jnp.float32)[:, None] * frequency[None, :]
    cosine = jnp.concatenate([jnp.cos(angles), jnp.cos(angles)], axis=-1)[:, None, :]
    sine_table = jnp.concatenate([jnp.sin(angles), jnp.sin(angles)], axis=-1)[:, None, :]
    return (cosine, sine_table)

def turn_rows(values, cosine, sine_table, half_size):
    rolled = jnp.concatenate([-values[..., half_size:], values[..., :half_size]], axis=-1)
    return values * cosine + rolled * sine_table

def layer_norm(values, gain_vec, bias_vec):
    centered = values - lax.optimization_barrier(jnp.mean(values, axis=-1, keepdims=True))
    scaling = lax.rsqrt(lax.optimization_barrier(jnp.mean(centered * centered, axis=-1, keepdims=True)) + EPS_NORM)
    return centered * scaling * gain_vec + bias_vec

def encode(rows_in, seq_spans, params):
    mat_qkv, mat_out, mat_gate, mat_up, mat_down, gain_one, bias_one, gain_two, bias_two = params
    row_count = rows_in.shape[0]
    model_width = mat_out.shape[0]
    head_count = model_width // HD
    half_size = HD // 2
    pooling, labels, offsets = layout(seq_spans, row_count)
    cosine, sine_table = rotary(offsets, half_size)
    mixed_rows = low_back(matmul_high(rows_in, mat_qkv))
    query_rows = low(turn_rows(mixed_rows[:, :model_width].reshape(row_count, head_count, HD), cosine, sine_table, half_size))
    key_rows = low(turn_rows(mixed_rows[:, model_width:2 * model_width].reshape(row_count, head_count, HD), cosine, sine_table, half_size))
    value_rows = low(mixed_rows[:, 2 * model_width:].reshape(row_count, head_count, HD))
    scores = jnp.einsum('thd,uhd->htu', query_rows, key_rows, precision=lax.Precision.HIGHEST) * HD ** (-0.5)
    scores = low_back(scores)
    same_seq = labels[:, None] == labels[None, :]
    scores = jnp.where(same_seq[None], scores, MASKED)
    weights_low = low(jax.nn.softmax(scores, axis=-1))
    attended = jnp.einsum('htu,uhd->thd', weights_low, value_rows, precision=lax.Precision.HIGHEST).reshape(row_count, model_width)
    attended = low(low_back(attended))
    hidden = rows_in + low_back(matmul_high(attended, mat_out))
    first_norm = layer_norm(hidden, gain_one, bias_one)
    first_low = low(first_norm)
    gate_value = low_back(matmul_high(first_low, mat_gate))
    up_value = low_back(matmul_high(first_low, mat_up))
    active = low(jax.nn.silu(gate_value) * up_value)
    second = layer_norm(first_norm + low_back(matmul_high(active, mat_down)), gain_two, bias_two)
    pooled = matmul_high(pooling, second)
    return pooled * lax.rsqrt(lax.optimization_barrier(jnp.sum(pooled * pooled, axis=-1, keepdims=True)) + EPS_UNIT)

def contrast(queries, documents, pos_doc):
    seq_count = queries.shape[0]
    similar = matmul_high(queries, documents.T) / TEMPER
    positive = (pos_doc[:, None] == jnp.arange(seq_count, dtype=jnp.int32)[None, :]).astype(jnp.float32)
    row_logsum = jax.nn.logsumexp(similar, axis=1)
    col_logsum = jax.nn.logsumexp(similar, axis=0)
    return (0.5 * (jnp.sum(row_logsum) + jnp.sum(col_logsum)) - jnp.sum(similar * positive)) / seq_count

def reference(tokens, lengths, pos_doc, w_qkv, w_out, w_gate, w_up, w_down, ln1_gain, ln1_bias, ln2_gain, ln2_bias):
    block_count = 2 * NSEQ // SEQ_DEV
    rows_all = tokens.astype(jnp.float32).reshape(block_count, TOK_DEV, D)
    span_rows = lengths.reshape(block_count, SEQ_DEV)
    params = tuple((weight.astype(jnp.float32) for weight in (w_qkv, w_out, w_gate, w_up, w_down, ln1_gain, ln1_bias, ln2_gain, ln2_bias)))
    checked = jax.checkpoint(encode)

    def forward(rows_all, params):

        def one_block(item_parts):
            return checked(item_parts[0], item_parts[1], params)
        pooled = lax.map(one_block, (rows_all, span_rows)).reshape(2, NSEQ, D)
        return (contrast(pooled[0], pooled[1], pos_doc), pooled)
    loss_value, pull_back, pooled = jax.vjp(forward, rows_all, params, has_aux=True)
    grad_rows, grads = pull_back(jnp.ones_like(loss_value))
    return (loss_value, pooled, grad_rows.reshape(2, TOKENS_T, D), grads[0], grads[1], grads[2], grads[3], grads[4], grads[5], grads[6], grads[7], grads[8])
```

```python
import math

import jax
import jax.numpy as jnp
from jax import lax
from jax.sharding import PartitionSpec as P

HD = 64


TEMPER = 0.05
EPS_NORM = 1e-05
EPS_UNIT = 1e-06
MASKED = -1e30


def joined(left_arr, right_arr, left_dim, right_dim):
    return lax.dot_general(
        left_arr,
        right_arr,
        (((left_dim,), (right_dim,)), ((), ())),
        preferred_element_type=jnp.float32,
    )


def joined_high(left_arr, right_arr, left_dim, right_dim):
    return lax.dot_general(
        left_arr,
        right_arr,
        (((left_dim,), (right_dim,)), ((), ())),
        precision=lax.Precision.HIGHEST,
        preferred_element_type=jnp.float32,
    )


def layout(seq_spans, row_count):
    seq_total = seq_spans.shape[0]
    starts = jnp.cumsum(seq_spans) - seq_spans
    places = jnp.arange(row_count, dtype=jnp.int32)
    member = (
        (places[None, :] >= starts[:, None]) & (places[None, :] < (starts + seq_spans)[:, None])
    ).astype(jnp.int32)
    labels = jnp.sum(member * jnp.arange(seq_total, dtype=jnp.int32)[:, None], axis=0)
    offsets = places - jnp.sum(member * starts[:, None], axis=0)
    pooling = member.astype(jnp.float32) / seq_spans.astype(jnp.float32)[:, None]
    return (pooling, labels, offsets)


def rotary(offsets, half_size):
    frequency = 1000.0 ** (-jnp.arange(half_size, dtype=jnp.float32) / half_size)
    angles = offsets.astype(jnp.float32)[:, None] * frequency[None, :]
    cosine = jnp.concatenate([jnp.cos(angles), jnp.cos(angles)], axis=-1)[:, None, :]
    sine_table = jnp.concatenate([jnp.sin(angles), jnp.sin(angles)], axis=-1)[:, None, :]
    return (cosine, sine_table)


def turn_rows(values, cosine, sine_table, half_size):
    rolled = jnp.concatenate([-values[..., half_size:], values[..., :half_size]], axis=-1)
    return values * cosine + rolled * sine_table


def turn_back(values, cosine, sine_table, half_size):
    turned = values * sine_table
    return values * cosine + jnp.concatenate(
        [turned[..., half_size:], -turned[..., :half_size]], axis=-1
    )


def norm_rows(values, gain_vec, bias_vec):
    centered = values - jnp.mean(values, axis=-1, keepdims=True)
    scaling = lax.rsqrt(jnp.mean(centered * centered, axis=-1, keepdims=True) + EPS_NORM)
    unit_rows = centered * scaling
    return (unit_rows * gain_vec + bias_vec, unit_rows, scaling)


def norm_back(grad_rows, unit_rows, scaling, gain_vec):
    along = grad_rows * gain_vec
    back_rows = scaling * (
        along
        - jnp.mean(along, axis=-1, keepdims=True)
        - unit_rows * jnp.mean(along * unit_rows, axis=-1, keepdims=True)
    )
    return (back_rows, jnp.sum(grad_rows * unit_rows, axis=0), jnp.sum(grad_rows, axis=0))


def split_dp(count):
    sizes = [2] if count % 2 == 0 else []
    rest = count // 2 if sizes else count
    front = []
    while rest > 1:
        step = 4 if rest % 4 == 0 else (2 if rest % 2 == 0 else rest)
        front.append(step)
        rest //= step
    return front + sizes


def digit_shift(sizes, place, shift):
    stride = math.prod(sizes[place + 1 :])
    size = sizes[place]
    pairs = []
    for index in range(math.prod(sizes)):
        digit = index // stride % size
        pairs.append((index, index + ((digit + shift) % size - digit) * stride))
    return pairs


def digits_of(index, sizes):
    found = []
    for size in reversed(sizes):
        found.append(index % size)
        index = index // size
    return found[::-1]


def pick(array, axis, place):
    return lax.dynamic_index_in_dim(array, place, axis, keepdims=False)


def reduce_digit(parts, sizes, place, digit):
    size = sizes[place]
    total = pick(parts, 0, digit).astype(jnp.float32)
    for shift in range(1, size):
        sent = pick(parts, 0, (digit + shift) % size).astype(jnp.bfloat16)
        total += lax.ppermute(sent, "dp", digit_shift(sizes, place, shift)).astype(jnp.float32)
    return total


def shared_sum(grad, sizes, digits, tower_index):
    rows, columns = grad.shape
    count = math.prod(sizes)
    per = rows // count
    tiles = columns // 128
    side = max(1, round(tiles * 0.3)) * 128
    middle = columns - 2 * side
    last = len(sizes) - 1
    blocks = grad.astype(jnp.bfloat16).reshape(count // sizes[last], sizes[last], per, columns)
    chip = reduce_digit(jnp.moveaxis(blocks, 1, 0), sizes, last, digits[last]).astype(jnp.bfloat16)
    lead = chip.shape[0]
    mine = lax.dynamic_slice(
        chip, (0, 0, tower_index * (columns - side)), (lead, per, side)
    )
    other = lax.dynamic_slice(
        chip, (0, 0, (1 - tower_index) * (columns - side)), (lead, per, side)
    )
    swap = [(0, 1), (1, 0)]
    mine = mine.astype(jnp.float32) + lax.ppermute(other, "tower", swap).astype(jnp.float32)
    part = jnp.concatenate([mine.astype(jnp.bfloat16), chip[:, :, side : side + middle]], axis=2)
    for place in range(last - 1, -1, -1):
        size = sizes[place]
        part = jnp.moveaxis(
            part.reshape(part.shape[0] // size, size, per, side + middle), 1, 0
        )
        part = reduce_digit(part, sizes, place, digits[place]).astype(jnp.bfloat16)
    part = part[0]
    back = lax.ppermute(part, "tower", swap).astype(jnp.float32)
    part = part.astype(jnp.float32)
    centre = part[:, side:] + back[:, side:]
    first = tower_index == 0
    return jnp.concatenate(
        [
            jnp.where(first, part[:, :side], back[:, :side]),
            centre,
            jnp.where(first, back[:, :side], part[:, :side]),
        ],
        axis=1,
    )


def body(
    tokens,
    lengths,
    pos_doc,
    w_qkv,
    w_out,
    w_gate,
    w_up,
    w_down,
    ln1_gain,
    ln1_bias,
    ln2_gain,
    ln2_bias,
):
    dp_count = lax.axis_size("dp")
    sizes = split_dp(dp_count)
    dp_index = lax.axis_index("dp")
    tower_index = lax.axis_index("tower")
    digits = digits_of(dp_index, sizes)
    per, narrow = w_out.shape
    spread = w_down.shape[0] // per
    down_flat = w_down.reshape(spread, per, narrow).transpose(1, 0, 2).reshape(per, spread * narrow)
    packed = jnp.concatenate([w_gate, w_up, down_flat, w_out, w_qkv], axis=1)
    whole = lax.all_gather(packed, "dp", axis=0, tiled=True)
    wide = w_gate.shape[1]
    mat_gate = whole[:, :wide]
    mat_up = whole[:, wide : 2 * wide]
    mat_down = (
        whole[:, 2 * wide : 3 * wide]
        .reshape(dp_count, per, spread, narrow)
        .transpose(0, 2, 1, 3)
        .reshape(wide, narrow)
    )
    mat_out = whole[:, 3 * wide : 3 * wide + narrow]
    mat_qkv = whole[:, 3 * wide + narrow :]
    vectors_own = jnp.stack([ln1_gain, ln1_bias, ln2_gain, ln2_bias])
    vectors_all = lax.all_to_all(
        jnp.broadcast_to(vectors_own[None], (dp_count, 4, per)), "dp", 0, 0, tiled=True
    )
    gain_one, bias_one, gain_two, bias_two = (
        vectors_all[:, k].reshape(narrow).astype(jnp.float32) for k in range(4)
    )
    rows_in = tokens[0]
    seq_spans = lengths[0]
    row_count, model_width = rows_in.shape
    head_count = model_width // HD
    half_size = HD // 2
    scaling = HD ** (-0.5)
    block_rows = 128
    pooling, labels, offsets = layout(seq_spans, row_count)
    same_seq = labels[:, None] == labels[None, :]
    cosine, sine_table = rotary(offsets, half_size)
    mixed_rows = jnp.dot(rows_in, mat_qkv, preferred_element_type=jnp.float32)
    query_rows = turn_rows(
        mixed_rows[:, :model_width].reshape(row_count, head_count, HD),
        cosine,
        sine_table,
        half_size,
    ).astype(jnp.bfloat16)
    key_rows = turn_rows(
        mixed_rows[:, model_width : 2 * model_width].reshape(row_count, head_count, HD),
        cosine,
        sine_table,
        half_size,
    ).astype(jnp.bfloat16)
    value_rows = (
        mixed_rows[:, 2 * model_width :].reshape(row_count, head_count, HD).astype(jnp.bfloat16)
    )
    query_heads = query_rows.transpose(1, 0, 2)
    key_heads = key_rows.transpose(1, 0, 2)
    value_heads = value_rows.transpose(1, 0, 2)

    def attend_head(head_parts):
        query_one, key_one, value_one = head_parts
        scores = jnp.where(same_seq, joined(query_one, key_one, 1, 1) * scaling, MASKED)
        row_max = jnp.max(scores, axis=-1, keepdims=True)
        exp_scores = jnp.exp(scores - row_max)
        row_total = jnp.sum(exp_scores, axis=-1, keepdims=True)
        weights_low = (exp_scores / row_total).astype(jnp.bfloat16)
        head_out = jnp.dot(weights_low, value_one, preferred_element_type=jnp.float32).astype(
            jnp.bfloat16
        )
        return (head_out, (row_max + jnp.log(row_total))[:, 0])

    attended, log_totals = lax.map(attend_head, (query_heads, key_heads, value_heads))
    attended = attended.transpose(1, 0, 2).reshape(row_count, model_width)
    hidden = rows_in.astype(jnp.float32) + jnp.dot(
        attended, mat_out, preferred_element_type=jnp.float32
    )
    first_norm, unit_one, scale_one = norm_rows(hidden, gain_one, bias_one)
    first_low = first_norm.astype(jnp.bfloat16)
    gate_value = jnp.dot(first_low, mat_gate, preferred_element_type=jnp.float32)
    up_value = jnp.dot(first_low, mat_up, preferred_element_type=jnp.float32)
    sigmoid_gate = jax.nn.sigmoid(gate_value)
    silu_gate = gate_value * sigmoid_gate
    active_low = (silu_gate * up_value).astype(jnp.bfloat16)
    to_gate = up_value * sigmoid_gate * (1.0 + gate_value * (1.0 - sigmoid_gate))
    branch = jnp.dot(active_low, mat_down, preferred_element_type=jnp.float32)
    second, unit_two, scale_two = norm_rows(first_norm + branch, gain_two, bias_two)
    pooled = jnp.dot(pooling, second, precision=lax.Precision.HIGHEST)
    inverse = lax.rsqrt(jnp.sum(pooled * pooled, axis=-1, keepdims=True) + EPS_UNIT)
    unit_vectors = pooled * inverse
    seq_count = unit_vectors.shape[0]
    device_count = 2 * dp_count
    everyone = lax.all_to_all(
        jnp.broadcast_to(unit_vectors[None], (device_count,) + unit_vectors.shape),
        ("tower", "dp"),
        0,
        0,
        tiled=True,
    ).reshape(device_count * seq_count, narrow)
    total_seqs = everyone.shape[0] // 2
    own_start = tower_index * total_seqs + dp_index * seq_count
    queries = everyone[:total_seqs]
    documents = everyone[total_seqs:]
    similar = joined_high(queries, documents, 1, 1) / TEMPER
    positive = (pos_doc[:, None] == jnp.arange(total_seqs, dtype=jnp.int32)[None, :]).astype(
        jnp.float32
    )
    row_logsum = jax.nn.logsumexp(similar, axis=1)
    col_logsum = jax.nn.logsumexp(similar, axis=0)
    loss_value = (
        0.5 * (jnp.sum(row_logsum) + jnp.sum(col_logsum)) - jnp.sum(similar * positive)
    ) / total_seqs
    grad_similar = (
        0.5 * (jnp.exp(similar - row_logsum[:, None]) + jnp.exp(similar - col_logsum[None, :]))
        - positive
    ) / total_seqs
    grad_all = (
        jnp.concatenate(
            [joined_high(grad_similar, documents, 1, 0), joined_high(grad_similar, queries, 0, 0)],
            axis=0,
        )
        / TEMPER
    )
    grad_unit = lax.dynamic_slice_in_dim(grad_all, own_start, seq_count, 0)
    dot_along = jnp.sum(pooled * grad_unit, axis=-1, keepdims=True)
    grad_pooled = inverse * grad_unit - inverse * inverse * inverse * pooled * dot_along
    grad_second = joined_high(pooling, grad_pooled, 0, 0)
    grad_mid, grad_gain_two, grad_bias_two = norm_back(grad_second, unit_two, scale_two, gain_two)
    grad_branch = grad_mid.astype(jnp.bfloat16)

    grad_mat_down = joined(active_low, grad_branch, 0, 0)
    grad_active = joined(grad_branch, mat_down, 1, 1)
    grad_gate = (grad_active * to_gate).astype(jnp.bfloat16)
    grad_up = (grad_active * silu_gate).astype(jnp.bfloat16)
    grad_mat_gate = joined(first_low, grad_gate, 0, 0)
    grad_mat_up = joined(first_low, grad_up, 0, 0)
    grad_first = grad_mid + joined(grad_gate, mat_gate, 1, 1) + joined(grad_up, mat_up, 1, 1)
    grad_hidden, grad_gain_one, grad_bias_one = norm_back(grad_first, unit_one, scale_one, gain_one)
    grad_attn = grad_hidden.astype(jnp.bfloat16)
    grad_mat_out = joined(attended, grad_attn, 0, 0)
    grad_attended = joined(grad_attn, mat_out, 1, 1).astype(jnp.bfloat16)
    grad_heads = grad_attended.reshape(row_count, head_count, HD).transpose(1, 0, 2)

    def attend_back(head_parts):
        query_one, key_one, value_one, grad_one, log_total = head_parts
        scores = jnp.where(same_seq, joined(query_one, key_one, 1, 1) * scaling, MASKED)
        probs_full = jnp.exp(scores - log_total[:, None])
        grad_probs = joined(grad_one, value_one, 1, 1)
        delta_rows = jnp.sum(probs_full * grad_probs, axis=-1, keepdims=True)
        grad_scores = (probs_full * (grad_probs - delta_rows)).astype(jnp.bfloat16)
        grad_query = jnp.dot(grad_scores, key_one, preferred_element_type=jnp.float32) * scaling
        grad_key = joined(grad_scores, query_one, 0, 0) * scaling
        grad_value = joined(probs_full.astype(jnp.bfloat16), grad_one, 0, 0)
        return (grad_query, grad_key, grad_value)

    grad_query, grad_key, grad_value = lax.map(
        attend_back, (query_heads, key_heads, value_heads, grad_heads, log_totals)
    )
    grad_query = turn_back(grad_query.transpose(1, 0, 2), cosine, sine_table, half_size).reshape(
        row_count, model_width
    )
    grad_key = turn_back(grad_key.transpose(1, 0, 2), cosine, sine_table, half_size).reshape(
        row_count, model_width
    )
    grad_value = grad_value.transpose(1, 0, 2).reshape(row_count, model_width)
    grad_mixed = jnp.concatenate([grad_query, grad_key, grad_value], axis=1).astype(jnp.bfloat16)
    grad_mat_qkv = joined(rows_in, grad_mixed, 0, 0)
    grad_rows = grad_hidden + joined(grad_mixed, mat_qkv, 1, 1)
    vectors = jnp.stack([grad_gain_one, grad_bias_one, grad_gain_two, grad_bias_two], axis=1)
    vectors = jnp.pad(vectors, ((0, 0), (0, 124)))
    down_rows = (
        grad_mat_down.reshape(dp_count, spread, per, narrow)
        .transpose(0, 2, 1, 3)
        .reshape(narrow, wide)
    )
    sum_down = shared_sum(down_rows, sizes, digits, tower_index)
    sum_feed = shared_sum(
        jnp.concatenate([grad_mat_gate, grad_mat_up], axis=1), sizes, digits, tower_index
    )
    sum_rest = shared_sum(
        jnp.concatenate([grad_mat_out, grad_mat_qkv, vectors], axis=1), sizes, digits, tower_index
    )
    sum_down = sum_down.reshape(per, spread, narrow).transpose(1, 0, 2).reshape(per * spread, narrow)
    vector_rows = sum_rest[:, 4 * narrow : 4 * narrow + 4]
    return (
        loss_value,
        unit_vectors[None],
        grad_rows[None],
        sum_rest[:, narrow : 4 * narrow],
        sum_rest[:, :narrow],
        sum_feed[:, :wide],
        sum_feed[:, wide:],
        sum_down,
        vector_rows[:, 0],
        vector_rows[:, 1],
        vector_rows[:, 2],
        vector_rows[:, 3],
    )


def solution(mesh):
    placed = (
        P("tower", "dp", None),
        P("tower", "dp"),
        P(),
        P("dp", None),
        P("dp", None),
        P("dp", None),
        P("dp", None),
        P("dp", None),
        P("dp"),
        P("dp"),
        P("dp"),
        P("dp"),
    )
    return jax.shard_map(
        body,
        mesh=mesh,
        in_specs=placed,
        out_specs=(
            P(),
            P("tower", "dp", None),
            P("tower", "dp", None),
            P("dp", None),
            P("dp", None),
            P("dp", None),
            P("dp", None),
            P("dp", None),
            P("dp"),
            P("dp"),
            P("dp"),
            P("dp"),
        ),
        check_vma=False,
    )
```

```python
import math

import jax
import jax.numpy as jnp
from jax import lax
from jax.experimental import pallas as pl
from jax.experimental.pallas import tpu as pltpu
from jax.sharding import PartitionSpec as P

HD = 64
TEMPER = 0.05
EPS_NORM = 1e-05
EPS_UNIT = 1e-06
MASKED = -1e30
F32 = jnp.float32
BF16 = jnp.bfloat16
MIB = 1 << 20


def joined(left_arr, right_arr, left_dim, right_dim):
    return lax.dot_general(
        left_arr,
        right_arr,
        (((left_dim,), (right_dim,)), ((), ())),
        preferred_element_type=F32,
    )


def joined_high(left_arr, right_arr, left_dim, right_dim):
    return lax.dot_general(
        left_arr,
        right_arr,
        (((left_dim,), (right_dim,)), ((), ())),
        precision=lax.Precision.HIGHEST,
        preferred_element_type=F32,
    )


def split_dp(count):
    sizes = [2] if count % 2 == 0 else []
    rest = count // 2 if sizes else count
    front = []
    while rest > 1:
        step = 4 if rest % 4 == 0 else (2 if rest % 2 == 0 else rest)
        front.append(step)
        rest //= step
    return front + sizes


def digit_shift(sizes, place, shift):
    stride = math.prod(sizes[place + 1 :])
    size = sizes[place]
    pairs = []
    for index in range(math.prod(sizes)):
        digit = index // stride % size
        pairs.append((index, index + ((digit + shift) % size - digit) * stride))
    return pairs


def digits_of(index, sizes):
    found = []
    for size in reversed(sizes):
        found.append(index % size)
        index = index // size
    return found[::-1]


SWAP = [(0, 1), (1, 0)]


def pick(array, axis, place):
    return lax.dynamic_index_in_dim(array, place, axis, keepdims=False)


def layout(seq_spans, row_count):
    seq_total = seq_spans.shape[0]
    starts = jnp.cumsum(seq_spans) - seq_spans
    places = jnp.arange(row_count, dtype=jnp.int32)
    member = (
        (places[None, :] >= starts[:, None]) & (places[None, :] < (starts + seq_spans)[:, None])
    ).astype(jnp.int32)
    labels = jnp.sum(member * jnp.arange(seq_total, dtype=jnp.int32)[:, None], axis=0)
    offsets = places - jnp.sum(member * starts[:, None], axis=0)
    pooling = member.astype(F32) / seq_spans.astype(F32)[:, None]
    return (pooling, labels, offsets)


def rotary_tables(offsets):
    half_size = HD // 2
    frequency = 1000.0 ** (-jnp.arange(half_size, dtype=F32) / half_size)
    angles = offsets.astype(F32)[:, None] * frequency[None, :]
    cosine, sine = jnp.cos(angles), jnp.sin(angles)
    return (
        jnp.concatenate([cosine] * 4, axis=1),
        jnp.concatenate([-sine, sine, -sine, sine], axis=1),
    )


def partner(values):
    lane = lax.broadcasted_iota(jnp.int32, values.shape, 1)
    return jnp.where(
        lane % HD < HD // 2, pltpu.roll(values, 96, 1), pltpu.roll(values, 32, 1)
    )


def unit_rows(values):
    centered = values - jnp.mean(values, axis=-1, keepdims=True)
    scaling = lax.rsqrt(jnp.mean(centered * centered, axis=-1, keepdims=True) + EPS_NORM)
    return centered * scaling, scaling


def norm_back(grad_rows, units, scaling, gain_row):
    along = grad_rows * gain_row
    back_rows = scaling * (
        along
        - jnp.mean(along, axis=-1, keepdims=True)
        - units * jnp.mean(along * units, axis=-1, keepdims=True)
    )
    return (
        back_rows,
        jnp.sum(grad_rows * units, axis=0, keepdims=True),
        jnp.sum(grad_rows, axis=0, keepdims=True),
    )


def whole_spec():
    return pl.BlockSpec(memory_space=pltpu.VMEM)


def params(mib, **more):
    return pltpu.CompilerParams(vmem_limit_bytes=mib * MIB, **more)


def attend_kernel(
    rows_ref, wqkv_ref, wout_ref, cos_ref, sin_ref, mark_ref, markt_ref, vec_ref,
    q_ref, k_ref, v_ref, att_ref, low_ref, unit_ref, scale_ref, bias_ref,
):
    rows = rows_ref[...]
    tokens, width = rows.shape
    pair = 2 * HD
    cosine, sine = cos_ref[...], sin_ref[...]
    bias_ref[...] = jnp.where(mark_ref[...] == markt_ref[...], 0.0, MASKED)
    for part, out_ref in enumerate((q_ref, k_ref, v_ref)):
        mixed = joined(rows, wqkv_ref[:, part].reshape(width, width), 1, 0)
        if part == 2:
            out_ref[...] = mixed.astype(BF16)
        else:
            for at in range(0, width, pair):
                piece = mixed[:, at : at + pair]
                turned = piece * cosine + partner(piece) * sine
                out_ref[:, at : at + pair] = turned.astype(BF16)
    first_half = lax.broadcasted_iota(jnp.int32, (tokens, pair), 1) < HD
    for at in range(0, width, pair):
        query = q_ref[:, at : at + pair]
        key = k_ref[:, at : at + pair]
        value = v_ref[:, at : at + pair]
        outs = []
        for half in range(2):
            inside = first_half if half == 0 else jnp.logical_not(first_half)
            only = jnp.where(inside, query, jnp.zeros_like(query))
            scores = joined(only, key, 1, 1) * HD**-0.5 + bias_ref[...]
            raised = jnp.exp(scores - jnp.max(scores, axis=-1, keepdims=True))
            total = jnp.sum(raised, axis=-1, keepdims=True)
            weights = (raised * (1.0 / total)).astype(BF16)
            outs.append(joined(weights, value, 1, 0))
        att_ref[:, at : at + pair] = jnp.where(first_half, outs[0], outs[1]).astype(BF16)
    hidden = rows.astype(F32) + joined(att_ref[...], wout_ref[:, 0].reshape(width, width), 1, 0)
    units, scaling = unit_rows(hidden)
    unit_ref[...] = units
    scale_ref[...] = scaling
    low_ref[...] = (units * vec_ref[0:1, :] + vec_ref[1:2, :]).astype(BF16)


def attend(rows, pack, cosine, sine, labels, vectors):
    tokens, width = rows.shape
    lead, _, per, _ = pack.shape
    shape = jax.ShapeDtypeStruct
    full = lambda *dims: pl.BlockSpec(dims, lambda i: (0,) * len(dims))
    mark = labels.astype(F32)
    return pl.pallas_call(
        attend_kernel,
        grid=(1,),
        in_specs=[
            full(tokens, width),
            pl.BlockSpec((lead, 3, per, width), lambda i: (0, 3, 0, 0)),
            pl.BlockSpec((lead, 1, per, width), lambda i: (0, 8, 0, 0)),
            full(tokens, 2 * HD),
            full(tokens, 2 * HD),
            full(tokens, 1),
            full(1, tokens),
            full(4, width),
        ],
        out_specs=[full(tokens, width)] * 6 + [full(tokens, 1)],
        out_shape=[shape((tokens, width), BF16)] * 5
        + [shape((tokens, width), F32), shape((tokens, 1), F32)],
        scratch_shapes=[pltpu.VMEM((tokens, tokens), F32)],
        compiler_params=params(48),
        cost_estimate=pl.CostEstimate(
            flops=8 * tokens * width * width, bytes_accessed=12 * MIB, transcendentals=0
        ),
    )(rows, pack, pack, cosine, sine, mark[:, None], mark[None, :], vectors)


def feed_kernel(
    low_ref, unit1_ref, wgate_ref, wup_ref, wdown_ref, vec_ref, pool_ref,
    act_ref, togate_ref, toup_ref, unit_ref, scale_ref, pooled_ref, emb_ref, acc_ref,
):
    step = pl.program_id(0)
    tokens, width = low_ref.shape
    low = low_ref[...]
    gate = joined(low, wgate_ref[:, 0].reshape(width, width), 1, 0)
    up = joined(low, wup_ref[:, 0].reshape(width, width), 1, 0)
    sig = 1.0 / (1.0 + jnp.exp(-gate))
    silu = gate * sig
    active = (silu * up).astype(BF16)
    act_ref[...] = active
    toup_ref[...] = silu.astype(BF16)
    togate_ref[...] = (up * sig * (1.0 + gate * (1.0 - sig))).astype(BF16)
    product = joined(active, wdown_ref[...].reshape(width, width), 1, 0)

    @pl.when(step == 0)
    def _():
        acc_ref[...] = unit1_ref[...] * vec_ref[0:1, :] + vec_ref[1:2, :] + product

    @pl.when(step > 0)
    def _():
        acc_ref[...] += product

    @pl.when(step == pl.num_programs(0) - 1)
    def _():
        units, scaling = unit_rows(acc_ref[...])
        unit_ref[...] = units
        scale_ref[...] = scaling
        second = units * vec_ref[2:3, :] + vec_ref[3:4, :]
        rows = [
            jnp.sum(second * pool_ref[:, s : s + 1], axis=0, keepdims=True)
            for s in range(pool_ref.shape[1])
        ]
        pooled = jnp.concatenate(rows, axis=0)
        pooled_ref[...] = pooled
        emb_ref[...] = pooled * lax.rsqrt(
            jnp.sum(pooled * pooled, axis=-1, keepdims=True) + EPS_UNIT
        )


def feed(low, units, pack, vectors, pool_t):
    tokens, width = low.shape
    lead, _, per, _ = pack.shape
    blocks = 4
    seqs = pool_t.shape[1]
    shape = jax.ShapeDtypeStruct
    full = lambda *dims: pl.BlockSpec(dims, lambda i: (0,) * len(dims))
    column = pl.BlockSpec((tokens, width), lambda i: (0, i))
    return pl.pallas_call(
        feed_kernel,
        grid=(blocks,),
        in_specs=[
            full(tokens, width),
            full(tokens, width),
            pl.BlockSpec((lead, 1, per, width), lambda i: (0, i, 0, 0)),
            pl.BlockSpec((lead, 1, per, width), lambda i: (0, blocks + i, 0, 0)),
            down_spec(pack),
            full(4, width),
            full(tokens, seqs),
        ],
        out_specs=[column] * 3
        + [full(tokens, width), full(tokens, 1), full(seqs, width), full(seqs, width)],
        out_shape=[shape((tokens, blocks * width), BF16)] * 3
        + [
            shape((tokens, width), F32),
            shape((tokens, 1), F32),
            shape((seqs, width), F32),
            shape((seqs, width), F32),
        ],
        scratch_shapes=[pltpu.VMEM((tokens, width), F32)],
        compiler_params=params(48),
        cost_estimate=pl.CostEstimate(
            flops=6 * tokens * width * width * blocks, bytes_accessed=24 * MIB, transcendentals=0
        ),
    )(low, units, pack, pack, pack, vectors, pool_t)


def down_spec(pack):
    lead, chunks, per, width = pack.shape
    if lead == 1:
        return pl.BlockSpec((1, 1, per, width), lambda i: (0, chunks - 4 + i, 0, 0))
    return pl.BlockSpec((lead // 4, 4, per, width), lambda i: (i, 3, 0, 0))


def lse(values, axis):
    top = jnp.max(values, axis=axis, keepdims=True)
    return top + jnp.log(jnp.sum(jnp.exp(values - top), axis=axis, keepdims=True))


def loss_kernel(
    every_ref, match_ref, own_match_ref, tower_ref, emb_ref, pooled_ref, loss_ref, grad_ref
):
    total = every_ref.shape[0] // 2
    queries = every_ref[0:total, :]
    documents = every_ref[total : 2 * total, :]
    similar = joined_high(queries, documents, 1, 1) / TEMPER
    flipped = joined_high(documents, queries, 1, 1) / TEMPER
    row_log = lse(similar, 1)
    loss = (
        0.5 * (jnp.sum(row_log, keepdims=True) + jnp.sum(lse(similar, 0), keepdims=True))
        - jnp.sum(similar * match_ref[...], keepdims=True)
    ) / total
    loss_ref[...] = loss
    first = tower_ref[...] == 0
    others = jnp.where(first, documents, queries)
    other_log = jnp.where(first, lse(similar, 0), lse(flipped, 0))
    own = joined_high(emb_ref[...], others, 1, 1) / TEMPER
    grad_similar = (
        0.5 * (jnp.exp(own - lse(own, 1)) + jnp.exp(own - other_log)) - own_match_ref[...]
    ) / total
    grad_unit = joined_high(grad_similar, others, 1, 0) / TEMPER
    pooled = pooled_ref[...]
    inverse = lax.rsqrt(jnp.sum(pooled * pooled, axis=-1, keepdims=True) + EPS_UNIT)
    along = jnp.sum(pooled * grad_unit, axis=-1, keepdims=True)
    grad_ref[...] = inverse * grad_unit - inverse * inverse * inverse * pooled * along


def loss_and_grad(everyone, pos_doc, tower_index, dp_index, emb, pooled):
    total = everyone.shape[0] // 2
    seqs, width = emb.shape
    match = (pos_doc[:, None] == jnp.arange(total, dtype=jnp.int32)[None, :]).astype(F32)
    oriented = jnp.where(tower_index == 0, match, match.T)
    own_match = lax.dynamic_slice_in_dim(oriented, dp_index * seqs, seqs, 0)
    shape = jax.ShapeDtypeStruct
    return pl.pallas_call(
        loss_kernel,
        in_specs=[whole_spec()] * 6,
        out_specs=[whole_spec()] * 2,
        out_shape=[shape((1, 1), F32), shape((seqs, width), F32)],
        compiler_params=params(40),
    )(everyone, match, own_match, tower_index.reshape(1, 1), emb, pooled)


def down_kernel(gp_ref, pool_ref, unit_ref, scale_ref, vec_ref, act_ref,
                dw_ref, mid_ref, low_ref, sums_ref):
    @pl.when(pl.program_id(0) == 0)
    def _():
        grad_second = sum(
            pool_ref[:, s : s + 1] * gp_ref[s : s + 1, :] for s in range(gp_ref.shape[0])
        )
        mid, gain, bias = norm_back(grad_second, unit_ref[...], scale_ref[...], vec_ref[2:3, :])
        mid_ref[...] = mid
        low_ref[...] = mid.astype(BF16)
        sums_ref[0:1, :] = gain
        sums_ref[1:2, :] = bias

    dw_ref[...] = joined(act_ref[...], low_ref[...], 0, 0).astype(BF16)


def down_back(grad_pooled, pool_t, units, scaling, vectors, active):
    tokens, width = units.shape
    hidden = active.shape[1]
    shape = jax.ShapeDtypeStruct
    full = lambda a: pl.BlockSpec(a.shape, lambda i: (0,) * a.ndim)
    flat = pl.BlockSpec((tokens, width), lambda i: (0, 0))
    return pl.pallas_call(
        down_kernel,
        grid=(hidden // width,),
        in_specs=[full(grad_pooled), full(pool_t), full(units), full(scaling), full(vectors),
                  pl.BlockSpec((tokens, width), lambda i: (0, i))],
        out_specs=[pl.BlockSpec((width, width), lambda i: (i, 0)), flat, flat,
                   pl.BlockSpec((2, width), lambda i: (0, 0))],
        out_shape=[shape((hidden, width), BF16), shape((tokens, width), F32),
                   shape((tokens, width), BF16), shape((2, width), F32)],
        compiler_params=params(40),
        cost_estimate=pl.CostEstimate(
            flops=2 * tokens * width * hidden, bytes_accessed=12 * MIB, transcendentals=0
        ),
    )(grad_pooled, pool_t, units, scaling, vectors, active)


def gates_kernel(branch_ref, mid_ref, act1_ref, act2_ref, low_ref, unit_ref, scale_ref, vec_ref,
                 wgate_ref, wup_ref, wdown_ref,
                 dgate_ref, dup_ref, hid_ref, attn_ref, sums_ref, acc_ref):
    step = pl.program_id(0)
    tokens, width = low_ref.shape
    low = low_ref[...]
    grad_active = joined(branch_ref[...], wdown_ref[...].reshape(width, width), 1, 1)
    grad_gate = (grad_active * act1_ref[...].astype(F32)).astype(BF16)
    grad_up = (grad_active * act2_ref[...].astype(F32)).astype(BF16)
    dgate_ref[...] = joined(low, grad_gate, 0, 0).astype(BF16)
    dup_ref[...] = joined(low, grad_up, 0, 0).astype(BF16)
    back = joined(grad_gate, wgate_ref[:, 0].reshape(width, width), 1, 1) + joined(
        grad_up, wup_ref[:, 0].reshape(width, width), 1, 1
    )

    @pl.when(step == 0)
    def _():
        acc_ref[...] = mid_ref[...] + back

    @pl.when(step > 0)
    def _():
        acc_ref[...] += back

    @pl.when(step == pl.num_programs(0) - 1)
    def _():
        grad_hidden, gain, bias = norm_back(
            acc_ref[...], unit_ref[...], scale_ref[...], vec_ref[0:1, :]
        )
        hid_ref[...] = grad_hidden
        attn_ref[...] = grad_hidden.astype(BF16)
        sums_ref[0:1, :] = gain
        sums_ref[1:2, :] = bias


def gates_back(branch, mid, to_gate, to_up, low, units, scaling, vectors, pack):
    tokens, width = low.shape
    lead, _, per, _ = pack.shape
    blocks = 4
    shape = jax.ShapeDtypeStruct
    full = lambda *dims: pl.BlockSpec(dims, lambda i: (0,) * len(dims))
    flat = full(tokens, width)
    column = pl.BlockSpec((tokens, width), lambda i: (0, i))
    grads = pl.BlockSpec((width, width), lambda i: (0, i))
    return pl.pallas_call(
        gates_kernel,
        grid=(blocks,),
        in_specs=[flat, flat, column, column, flat, flat, full(tokens, 1), full(4, width),
                  pl.BlockSpec((lead, 1, per, width), lambda i: (0, i, 0, 0)),
                  pl.BlockSpec((lead, 1, per, width), lambda i: (0, blocks + i, 0, 0)),
                  down_spec(pack)],
        out_specs=[grads, grads, flat, flat, full(2, width)],
        out_shape=[shape((width, blocks * width), BF16)] * 2
        + [shape((tokens, width), F32), shape((tokens, width), BF16), shape((2, width), F32)],
        scratch_shapes=[pltpu.VMEM((tokens, width), F32)],
        compiler_params=params(48),
        cost_estimate=pl.CostEstimate(
            flops=10 * tokens * width * width * blocks, bytes_accessed=30 * MIB, transcendentals=0
        ),
    )(branch, mid, to_gate, to_up, low, units, scaling, vectors, pack, pack, pack)


def attend_back_kernel(
    rows_ref, wqkv_ref, wout_ref, cos_ref, sin_ref, mark_ref, markt_ref,
    q_ref, k_ref, v_ref, att_ref, grad_ref, hid_ref,
    dout_ref, dqkv_ref, tok_ref, bias_ref, gatt_ref, mixed_ref,
):
    rows = rows_ref[...]
    tokens, width = rows.shape
    pair = 2 * HD
    cosine, sine = cos_ref[...], sin_ref[...]
    bias_ref[...] = jnp.where(mark_ref[...] == markt_ref[...], 0.0, MASKED)
    grad = grad_ref[...]
    dout_ref[...] = joined(att_ref[...], grad, 0, 0).astype(BF16)
    gatt_ref[...] = joined(grad, wout_ref[:, 0].reshape(width, width), 1, 1).astype(BF16)
    first_half = lax.broadcasted_iota(jnp.int32, (tokens, pair), 1) < HD
    for at in range(0, width, pair):
        query = q_ref[:, at : at + pair]
        key = k_ref[:, at : at + pair]
        value = v_ref[:, at : at + pair]
        grad_out = gatt_ref[:, at : at + pair]
        found = []
        for half in range(2):
            inside = first_half if half == 0 else jnp.logical_not(first_half)
            scores = (
                joined(jnp.where(inside, key, jnp.zeros_like(key)), query, 1, 1) * HD**-0.5
                + bias_ref[...]
            )
            raised = jnp.exp(scores - jnp.max(scores, axis=0, keepdims=True))
            probs = raised * (1.0 / jnp.sum(raised, axis=0, keepdims=True))
            grad_probs = joined(
                jnp.where(inside, value, jnp.zeros_like(value)), grad_out, 1, 1
            )
            delta = jnp.sum(probs * grad_probs, axis=0, keepdims=True)
            grad_scores = (probs * (grad_probs - delta)).astype(BF16)
            found.append(
                (
                    joined(grad_scores, key, 0, 0),
                    joined(grad_scores, query, 1, 0),
                    joined(probs.astype(BF16), grad_out, 1, 0),
                )
            )
        grad_query = jnp.where(first_half, found[0][0], found[1][0]) * HD**-0.5
        grad_key = jnp.where(first_half, found[0][1], found[1][1]) * HD**-0.5
        grad_value = jnp.where(first_half, found[0][2], found[1][2])
        mixed_ref[0, :, at : at + pair] = (
            grad_query * cosine - partner(grad_query) * sine
        ).astype(BF16)
        mixed_ref[1, :, at : at + pair] = (
            grad_key * cosine - partner(grad_key) * sine
        ).astype(BF16)
        mixed_ref[2, :, at : at + pair] = grad_value.astype(BF16)
    back = hid_ref[...]
    for part in range(3):
        mixed = mixed_ref[part]
        dqkv_ref[:, part * width : (part + 1) * width] = joined(rows, mixed, 0, 0).astype(BF16)
        back += joined(mixed, wqkv_ref[:, part].reshape(width, width), 1, 1)
    tok_ref[...] = back


def attend_back(rows, pack, cosine, sine, labels, query, key, value, attended, grad, hidden):
    tokens, width = rows.shape
    lead, _, per, _ = pack.shape
    shape = jax.ShapeDtypeStruct
    full = lambda *dims: pl.BlockSpec(dims, lambda i: (0,) * len(dims))
    flat = full(tokens, width)
    mark = labels.astype(F32)
    return pl.pallas_call(
        attend_back_kernel,
        grid=(1,),
        in_specs=[flat,
                  pl.BlockSpec((lead, 3, per, width), lambda i: (0, 3, 0, 0)),
                  pl.BlockSpec((lead, 1, per, width), lambda i: (0, 8, 0, 0)),
                  full(tokens, 2 * HD), full(tokens, 2 * HD), full(tokens, 1), full(1, tokens)]
        + [flat] * 6,
        out_specs=[full(width, width), full(width, 3 * width), flat],
        out_shape=[shape((width, width), BF16), shape((width, 3 * width), BF16),
                   shape((tokens, width), F32)],
        scratch_shapes=[pltpu.VMEM((tokens, tokens), F32), pltpu.VMEM((tokens, width), BF16),
                        pltpu.VMEM((3, tokens, width), BF16)],
        compiler_params=params(56),
        cost_estimate=pl.CostEstimate(
            flops=24 * tokens * width * width, bytes_accessed=20 * MIB, transcendentals=0
        ),
    )(rows, pack, pack, cosine, sine, mark[:, None], mark[None, :],
      query, key, value, attended, grad, hidden)


def reduce_digit(parts, sizes, place, digit):
    size = sizes[place]
    total = pick(parts, 0, digit).astype(F32)
    for shift in range(1, size):
        sent = pick(parts, 0, (digit + shift) % size).astype(BF16)
        total += lax.ppermute(sent, "dp", digit_shift(sizes, place, shift)).astype(F32)
    return total


def shared_sum(grad, sizes, digits, tower_index):
    rows, columns = grad.shape
    count = math.prod(sizes)
    per = rows // count
    tiles = columns // 128
    side = max(1, round(tiles * 0.3)) * 128
    middle = columns - 2 * side
    last = len(sizes) - 1
    blocks = grad.astype(BF16).reshape(count // sizes[last], sizes[last], per, columns)
    chip = reduce_digit(jnp.moveaxis(blocks, 1, 0), sizes, last, digits[last]).astype(BF16)
    lead = chip.shape[0]
    mine = lax.dynamic_slice(chip, (0, 0, tower_index * (columns - side)), (lead, per, side))
    other = lax.dynamic_slice(
        chip, (0, 0, (1 - tower_index) * (columns - side)), (lead, per, side)
    )
    mine = mine.astype(F32) + lax.ppermute(other, "tower", SWAP).astype(F32)
    part = jnp.concatenate([mine.astype(BF16), chip[:, :, side : side + middle]], axis=2)
    for place in range(last - 1, -1, -1):
        size = sizes[place]
        part = jnp.moveaxis(part.reshape(part.shape[0] // size, size, per, side + middle), 1, 0)
        part = reduce_digit(part, sizes, place, digits[place]).astype(BF16)
    part = part[0]
    back = lax.ppermute(part, "tower", SWAP).astype(F32)
    part = part.astype(F32)
    centre = part[:, side:] + back[:, side:]
    first = tower_index == 0
    return jnp.concatenate(
        [
            jnp.where(first, part[:, :side], back[:, :side]),
            centre,
            jnp.where(first, back[:, :side], part[:, :side]),
        ],
        axis=1,
    )


def body(
    tokens,
    lengths,
    pos_doc,
    w_qkv,
    w_out,
    w_gate,
    w_up,
    w_down,
    ln1_gain,
    ln1_bias,
    ln2_gain,
    ln2_bias,
):
    dp_count = lax.axis_size("dp")
    device_count = 2 * dp_count
    sizes = split_dp(dp_count)
    dp_index = lax.axis_index("dp")
    tower_index = lax.axis_index("tower")
    digits = digits_of(dp_index, sizes)
    per, narrow = w_out.shape
    wide = w_gate.shape[1]
    spread = wide // narrow

    chunks = [w_gate[:, at : at + narrow] for at in range(0, wide, narrow)]
    chunks += [w_up[:, at : at + narrow] for at in range(0, wide, narrow)]
    chunks += [w_out] + [w_qkv[:, at : at + narrow] for at in range(0, 3 * narrow, narrow)]
    chunks += [w_down]
    own_pack = jnp.concatenate(chunks, axis=0)
    pack = lax.all_gather(own_pack, "dp", axis=0, tiled=True)
    pack = pack.reshape(dp_count, 4 * spread, per, narrow)
    if per % 16:
        front = pack[:, : 3 * spread].transpose(1, 0, 2, 3).reshape(3 * spread, narrow, narrow)
        back = pack[:, 3 * spread :].reshape(spread, narrow, narrow)
        pack = jnp.concatenate([front, back], axis=0)[None]
    vectors_own = jnp.stack([ln1_gain, ln1_bias, ln2_gain, ln2_bias])
    vectors = lax.all_to_all(
        jnp.broadcast_to(vectors_own[None], (dp_count, 4, per)), "dp", 0, 0, tiled=True
    )
    vectors = vectors.transpose(1, 0, 2).reshape(4, narrow).astype(F32)

    rows_in = tokens[0]
    row_count = rows_in.shape[0]
    pooling, labels, offsets = layout(lengths[0], row_count)
    pool_t = pooling.T
    cosine, sine = rotary_tables(offsets)

    query, key, value, attended, first_low, unit_one, scale_one = attend(
        rows_in, pack, cosine, sine, labels, vectors
    )
    active, to_gate, to_up, unit_two, scale_two, pooled, unit_vectors = feed(
        first_low, unit_one, pack, vectors, pool_t
    )
    seq_count = unit_vectors.shape[0]
    everyone = lax.all_to_all(
        jnp.broadcast_to(unit_vectors[None], (device_count,) + unit_vectors.shape),
        ("tower", "dp"),
        0,
        0,
        tiled=True,
    ).reshape(device_count * seq_count, narrow)
    loss_value, grad_pooled = loss_and_grad(
        everyone, pos_doc, tower_index, dp_index, unit_vectors, pooled
    )
    grad_down, grad_mid, grad_branch, sums_two = down_back(
        grad_pooled, pool_t, unit_two, scale_two, vectors, active
    )
    grad_gate, grad_up, grad_hidden, grad_attn, sums_one = gates_back(
        grad_branch, grad_mid, to_gate, to_up, first_low, unit_one, scale_one, vectors, pack
    )
    grad_out, grad_qkv, grad_rows = attend_back(
        rows_in, pack, cosine, sine, labels, query, key, value, attended, grad_attn, grad_hidden
    )

    sums = jnp.concatenate([sums_one, sums_two], axis=0).reshape(4, dp_count, per)
    sums = sums.transpose(1, 0, 2)
    sums = jnp.broadcast_to(sums[None], (2, dp_count, 4, per)).reshape(device_count, 4, per)
    sums = jnp.sum(lax.all_to_all(sums, ("tower", "dp"), 0, 0, tiled=True), axis=0)

    down_rows = (
        grad_down.reshape(dp_count, spread, per, narrow)
        .transpose(0, 2, 1, 3)
        .reshape(narrow, wide)
    )
    sum_down = shared_sum(down_rows, sizes, digits, tower_index)
    sum_gate = shared_sum(grad_gate, sizes, digits, tower_index)
    sum_up = shared_sum(grad_up, sizes, digits, tower_index)
    sum_rest = shared_sum(
        jnp.concatenate([grad_out, grad_qkv], axis=1), sizes, digits, tower_index
    )
    sum_down = sum_down.reshape(per, spread, narrow).transpose(1, 0, 2).reshape(per * spread, narrow)
    return (
        loss_value.reshape(()),
        unit_vectors[None],
        grad_rows[None],
        sum_rest[:, narrow:],
        sum_rest[:, :narrow],
        sum_gate,
        sum_up,
        sum_down,
        sums[0],
        sums[1],
        sums[2],
        sums[3],
    )


def solution(mesh):
    placed = (
        P("tower", "dp", None),
        P("tower", "dp"),
        P(),
        P("dp", None),
        P("dp", None),
        P("dp", None),
        P("dp", None),
        P("dp", None),
        P("dp"),
        P("dp"),
        P("dp"),
        P("dp"),
    )
    return jax.shard_map(
        body,
        mesh=mesh,
        in_specs=placed,
        out_specs=(
            P(),
            P("tower", "dp", None),
            P("tower", "dp", None),
            P("dp", None),
            P("dp", None),
            P("dp", None),
            P("dp", None),
            P("dp", None),
            P("dp"),
            P("dp"),
            P("dp"),
            P("dp"),
        ),
        check_vma=False,
    )
```

```python
import math

import jax
import jax.numpy as jnp
from jax import lax
from jax.experimental import pallas as pl
from jax.experimental.pallas import tpu as pltpu
from jax.sharding import PartitionSpec as P

HD = 64
PAD = 128
VECTORS = 4
TEMPER = 0.05
EPS_NORM = 1e-05
EPS_UNIT = 1e-06
MASKED = -1e30
F32 = jnp.float32
BF16 = jnp.bfloat16
MIB = 1 << 20
LONG = pl.CostEstimate(flops=30000000000, bytes_accessed=10000000, transcendentals=0)
SHORT = pl.CostEstimate(flops=100000000, bytes_accessed=1000000, transcendentals=0)


def joined(left_arr, right_arr, left_dim, right_dim):
    return lax.dot_general(
        left_arr,
        right_arr,
        (((left_dim,), (right_dim,)), ((), ())),
        preferred_element_type=F32,
    )


def joined_high(left_arr, right_arr, left_dim, right_dim):
    return lax.dot_general(
        left_arr,
        right_arr,
        (((left_dim,), (right_dim,)), ((), ())),
        precision=lax.Precision.HIGHEST,
        preferred_element_type=F32,
    )


def split_dp(count):
    sizes = [2] if count % 2 == 0 else []
    rest = count // 2 if sizes else count
    front = []
    while rest > 1:
        step = 4 if rest % 4 == 0 else (2 if rest % 2 == 0 else rest)
        front.append(step)
        rest //= step
    return front + sizes


def digit_shift(sizes, place, shift):
    stride = math.prod(sizes[place + 1 :])
    size = sizes[place]
    pairs = []
    for index in range(math.prod(sizes)):
        digit = index // stride % size
        pairs.append((index, index + ((digit + shift) % size - digit) * stride))
    return pairs


def digits_of(index, sizes):
    found = []
    for size in reversed(sizes):
        found.append(index % size)
        index = index // size
    return found[::-1]


SWAP = [(0, 1), (1, 0)]


def pick(array, axis, place):
    return lax.dynamic_index_in_dim(array, place, axis, keepdims=False)


def layout(seq_spans, row_count):
    seq_total = seq_spans.shape[0]
    starts = jnp.cumsum(seq_spans) - seq_spans
    places = jnp.arange(row_count, dtype=jnp.int32)
    member = (
        (places[None, :] >= starts[:, None]) & (places[None, :] < (starts + seq_spans)[:, None])
    ).astype(jnp.int32)
    labels = jnp.sum(member * jnp.arange(seq_total, dtype=jnp.int32)[:, None], axis=0)
    offsets = places - jnp.sum(member * starts[:, None], axis=0)
    pooling = member.astype(F32) / seq_spans.astype(F32)[:, None]
    return (pooling, labels, offsets)


def rotary_tables(offsets):
    half_size = HD // 2
    frequency = 1000.0 ** (-jnp.arange(half_size, dtype=F32) / half_size)
    angles = offsets.astype(F32)[:, None] * frequency[None, :]
    cosine, sine = jnp.cos(angles), jnp.sin(angles)
    return (
        jnp.concatenate([cosine] * 4, axis=1),
        jnp.concatenate([-sine, sine, -sine, sine], axis=1),
    )


def partner(values):
    lane = lax.broadcasted_iota(jnp.int32, values.shape, 1)
    return jnp.where(
        lane % HD < HD // 2, pltpu.roll(values, 96, 1), pltpu.roll(values, 32, 1)
    )


def unit_rows(values):
    centered = values - jnp.mean(values, axis=-1, keepdims=True)
    scaling = lax.rsqrt(jnp.mean(centered * centered, axis=-1, keepdims=True) + EPS_NORM)
    return centered * scaling, scaling


def norm_back(grad_rows, units, scaling, gain_row):
    along = grad_rows * gain_row
    back_rows = scaling * (
        along
        - jnp.mean(along, axis=-1, keepdims=True)
        - units * jnp.mean(along * units, axis=-1, keepdims=True)
    )
    return (
        back_rows,
        jnp.sum(grad_rows * units, axis=0, keepdims=True),
        jnp.sum(grad_rows, axis=0, keepdims=True),
    )


def whole_spec():
    return pl.BlockSpec(memory_space=pltpu.VMEM)


def params():
    return pltpu.CompilerParams(vmem_limit_bytes=60 * MIB)


def attend_kernel(
    rows_ref, wqkv_ref, wout_ref, cos_ref, sin_ref, mark_ref, markt_ref, vec_ref,
    q_ref, k_ref, v_ref, att_ref, low_ref, unit_ref, scale_ref, bias_ref,
):
    rows = rows_ref[...]
    tokens, width = rows.shape
    pair = 2 * HD
    cosine, sine = cos_ref[...], sin_ref[...]
    bias_ref[...] = jnp.where(mark_ref[...] == markt_ref[...], 0.0, MASKED)
    for part, out_ref in enumerate((q_ref, k_ref, v_ref)):
        mixed = joined(rows, wqkv_ref[:, part].reshape(width, width), 1, 0)
        if part == 2:
            out_ref[...] = mixed.astype(BF16)
        else:
            for at in range(0, width, pair):
                piece = mixed[:, at : at + pair]
                turned = piece * cosine + partner(piece) * sine
                out_ref[:, at : at + pair] = turned.astype(BF16)
    first_half = lax.broadcasted_iota(jnp.int32, (tokens, pair), 1) < HD
    for at in range(0, width, pair):
        query = q_ref[:, at : at + pair]
        key = k_ref[:, at : at + pair]
        value = v_ref[:, at : at + pair]
        outs = []
        for half in range(2):
            inside = first_half if half == 0 else jnp.logical_not(first_half)
            only = jnp.where(inside, query, jnp.zeros_like(query))
            scores = joined(only, key, 1, 1) * HD**-0.5 + bias_ref[...]
            raised = jnp.exp(scores - jnp.max(scores, axis=-1, keepdims=True))
            total = jnp.sum(raised, axis=-1, keepdims=True)
            weights = (raised * (1.0 / total)).astype(BF16)
            outs.append(joined(weights, value, 1, 0))
        att_ref[:, at : at + pair] = jnp.where(first_half, outs[0], outs[1]).astype(BF16)
    hidden = rows.astype(F32) + joined(att_ref[...], wout_ref[:, 0].reshape(width, width), 1, 0)
    units, scaling = unit_rows(hidden)
    unit_ref[...] = units
    scale_ref[...] = scaling
    low_ref[...] = (units * vec_ref[0:1, :] + vec_ref[1:2, :]).astype(BF16)


def attend(rows, pack, cosine, sine, labels, vectors):
    tokens, width = rows.shape
    lead, _, per, _ = pack.shape
    shape = jax.ShapeDtypeStruct
    full = lambda *dims: pl.BlockSpec(dims, lambda i: (0,) * len(dims))
    mark = labels.astype(F32)
    return pl.pallas_call(
        attend_kernel,
        grid=(1,),
        in_specs=[
            full(tokens, width),
            pl.BlockSpec((lead, 3, per, width), lambda i: (0, 3, 0, 0)),
            pl.BlockSpec((lead, 1, per, width), lambda i: (0, 8, 0, 0)),
            full(tokens, 2 * HD),
            full(tokens, 2 * HD),
            full(tokens, 1),
            full(1, tokens),
            full(4, width),
        ],
        out_specs=[full(tokens, width)] * 6 + [full(tokens, 1)],
        out_shape=[shape((tokens, width), BF16)] * 5
        + [shape((tokens, width), F32), shape((tokens, 1), F32)],
        scratch_shapes=[pltpu.VMEM((tokens, tokens), F32)],
        compiler_params=params(),
        cost_estimate=LONG,
    )(rows, pack, pack, cosine, sine, mark[:, None], mark[None, :], vectors)


def feed_kernel(
    low_ref, unit1_ref, wgate_ref, wup_ref, wdown_ref, vec_ref, pool_ref,
    act_ref, togate_ref, toup_ref, unit_ref, scale_ref, pooled_ref, emb_ref, acc_ref,
):
    step = pl.program_id(0)
    tokens, width = low_ref.shape
    low = low_ref[...]
    gate = joined(low, wgate_ref[:, 0].reshape(width, width), 1, 0)
    up = joined(low, wup_ref[:, 0].reshape(width, width), 1, 0)
    sig = 1.0 / (1.0 + jnp.exp(-gate))
    silu = gate * sig
    active = (silu * up).astype(BF16)
    act_ref[...] = active
    toup_ref[...] = silu.astype(BF16)
    togate_ref[...] = (up * sig * (1.0 + gate * (1.0 - sig))).astype(BF16)
    product = joined(active, wdown_ref[...].reshape(width, width), 1, 0)

    @pl.when(step == 0)
    def _():
        acc_ref[...] = unit1_ref[...] * vec_ref[0:1, :] + vec_ref[1:2, :] + product

    @pl.when(step > 0)
    def _():
        acc_ref[...] += product

    @pl.when(step == pl.num_programs(0) - 1)
    def _():
        units, scaling = unit_rows(acc_ref[...])
        unit_ref[...] = units
        scale_ref[...] = scaling
        second = units * vec_ref[2:3, :] + vec_ref[3:4, :]
        rows = [
            jnp.sum(second * pool_ref[:, s : s + 1], axis=0, keepdims=True)
            for s in range(pool_ref.shape[1])
        ]
        pooled = jnp.concatenate(rows, axis=0)
        pooled_ref[...] = pooled
        emb_ref[...] = pooled * lax.rsqrt(
            jnp.sum(pooled * pooled, axis=-1, keepdims=True) + EPS_UNIT
        )


def feed(low, units, pack, vectors, pool_t):
    tokens, width = low.shape
    lead, _, per, _ = pack.shape
    blocks = 4
    seqs = pool_t.shape[1]
    shape = jax.ShapeDtypeStruct
    full = lambda *dims: pl.BlockSpec(dims, lambda i: (0,) * len(dims))
    column = pl.BlockSpec((tokens, width), lambda i: (0, i))
    return pl.pallas_call(
        feed_kernel,
        grid=(blocks,),
        in_specs=[
            full(tokens, width),
            full(tokens, width),
            pl.BlockSpec((lead, 1, per, width), lambda i: (0, i, 0, 0)),
            pl.BlockSpec((lead, 1, per, width), lambda i: (0, blocks + i, 0, 0)),
            down_spec(pack),
            full(4, width),
            full(tokens, seqs),
        ],
        out_specs=[column] * 3
        + [full(tokens, width), full(tokens, 1), full(seqs, width), full(seqs, width)],
        out_shape=[shape((tokens, blocks * width), BF16)] * 3
        + [
            shape((tokens, width), F32),
            shape((tokens, 1), F32),
            shape((seqs, width), F32),
            shape((seqs, width), F32),
        ],
        scratch_shapes=[pltpu.VMEM((tokens, width), F32)],
        compiler_params=params(),
        cost_estimate=LONG,
    )(low, units, pack, pack, pack, vectors, pool_t)


def down_spec(pack, first=0):
    lead, chunks, per, width = pack.shape
    if lead == 1:
        return pl.BlockSpec((1, 1, per, width), lambda i, *p: (0, chunks - 4 + first + i, 0, 0))
    return pl.BlockSpec((lead // 4, 4, per, width), lambda i, *p: (first + i, 3, 0, 0))


def lse(values, axis):
    top = jnp.max(values, axis=axis, keepdims=True)
    return top + jnp.log(jnp.sum(jnp.exp(values - top), axis=axis, keepdims=True))


def loss_kernel(
    every_ref, match_ref, own_match_ref, tower_ref, emb_ref, pooled_ref, loss_ref, grad_ref
):
    total = every_ref.shape[0] // 2
    queries = every_ref[0:total, :]
    documents = every_ref[total : 2 * total, :]
    similar = joined_high(queries, documents, 1, 1) / TEMPER
    flipped = joined_high(documents, queries, 1, 1) / TEMPER
    row_log = lse(similar, 1)
    loss = (
        0.5 * (jnp.sum(row_log, keepdims=True) + jnp.sum(lse(similar, 0), keepdims=True))
        - jnp.sum(similar * match_ref[...], keepdims=True)
    ) / total
    loss_ref[...] = loss
    first = tower_ref[...] == 0
    others = jnp.where(first, documents, queries)
    other_log = jnp.where(first, lse(similar, 0), lse(flipped, 0))
    own = joined_high(emb_ref[...], others, 1, 1) / TEMPER
    grad_similar = (
        0.5 * (jnp.exp(own - lse(own, 1)) + jnp.exp(own - other_log)) - own_match_ref[...]
    ) / total
    grad_unit = joined_high(grad_similar, others, 1, 0) / TEMPER
    pooled = pooled_ref[...]
    inverse = lax.rsqrt(jnp.sum(pooled * pooled, axis=-1, keepdims=True) + EPS_UNIT)
    along = jnp.sum(pooled * grad_unit, axis=-1, keepdims=True)
    grad_ref[...] = inverse * grad_unit - inverse * inverse * inverse * pooled * along


def loss_and_grad(everyone, pos_doc, tower_index, dp_index, emb, pooled):
    total = everyone.shape[0] // 2
    seqs, width = emb.shape
    match = (pos_doc[:, None] == jnp.arange(total, dtype=jnp.int32)[None, :]).astype(F32)
    oriented = jnp.where(tower_index == 0, match, match.T)
    own_match = lax.dynamic_slice_in_dim(oriented, dp_index * seqs, seqs, 0)
    shape = jax.ShapeDtypeStruct
    return pl.pallas_call(
        loss_kernel,
        in_specs=[whole_spec()] * 6,
        out_specs=[whole_spec()] * 2,
        out_shape=[shape((1, 1), F32), shape((seqs, width), F32)],
        compiler_params=params(),
    )(everyone, match, own_match, tower_index.reshape(1, 1), emb, pooled)


def place_table(digits, tower_index):
    z, y, c = digits
    table = [
        ((z + dz) % 4) * 4 + ((y + dy) % 2) * 2 + (c + dc) % 2
        for dc in range(2)
        for dy in range(2)
        for dz in range(4)
    ]
    return jnp.stack(table + [tower_index]).astype(jnp.int32)


def spill(place_ref, blocks_ref, keep_ref, send_ref, *at):
    for k in range(8):
        keep_ref[(k, *at)] = blocks_ref[place_ref[k]]
        send_ref[(k, *at)] = blocks_ref[place_ref[8 + k]]


def down_first(gp_ref, pool_ref, unit_ref, scale_ref, vec_ref, mid_ref, low_ref, sums_ref):
    grad_second = sum(
        pool_ref[:, s : s + 1] * gp_ref[s : s + 1, :] for s in range(gp_ref.shape[0])
    )
    mid, gain, bias = norm_back(grad_second, unit_ref[...], scale_ref[...], vec_ref[2:3, :])
    mid_ref[...] = mid
    low_ref[...] = mid.astype(BF16)
    sums_ref[0:1, :] = gain
    sums_ref[1:2, :] = bias


def down_kernel(gp_ref, pool_ref, unit_ref, scale_ref, vec_ref, act_ref,
               dw_ref, mid_ref, low_ref, sums_ref):
    @pl.when(pl.program_id(0) == 0)
    def _():
        down_first(gp_ref, pool_ref, unit_ref, scale_ref, vec_ref, mid_ref, low_ref, sums_ref)

    dw_ref[...] = joined(act_ref[...], low_ref[...], 0, 0).astype(BF16).reshape(dw_ref.shape)


def down_back(blocks, grad_pooled, pool_t, units, scaling, vectors, active):
    tokens, width = units.shape
    hidden = active.shape[1]
    shape = jax.ShapeDtypeStruct
    full = lambda a: pl.BlockSpec(a.shape, lambda i: (0,) * a.ndim)
    flat = pl.BlockSpec((tokens, width), lambda i: (0, 0))
    if blocks is None:
        grad_shape, grads = (hidden, width), pl.BlockSpec((width, width), lambda i: (i, 0))
    else:
        lead, per = blocks
        grad_shape = (lead, 8, per, width)
        grads = pl.BlockSpec((lead // 4, 4, per, width), lambda i: (i, 0, 0, 0))
    return pl.pallas_call(
        down_kernel,
        grid=(hidden // width,),
        in_specs=[full(grad_pooled), full(pool_t), full(units), full(scaling), full(vectors),
                  pl.BlockSpec((tokens, width), lambda i: (0, i))],
        out_specs=[grads, flat, flat, pl.BlockSpec((2, width), lambda i: (0, 0))],
        out_shape=[shape(grad_shape, BF16), shape((tokens, width), F32),
                   shape((tokens, width), BF16), shape((2, width), F32)],
        compiler_params=params(),
        cost_estimate=LONG,
    )(grad_pooled, pool_t, units, scaling, vectors, active)


def gates_kernel(fast, last, waits, *refs):
    refs = list(refs)
    place_ref = refs.pop(0) if fast and last else None
    (branch_ref, sum_ref, act1_ref, act2_ref, low_ref, unit_ref, scale_ref, vec_ref,
     wgate_ref, wup_ref, wdown_ref) = refs[:11]
    count = 2 if last or not fast else 1
    grad_refs, refs = refs[11 + waits : 11 + waits + count], refs[11 + waits + count :]
    step = pl.program_id(0)
    tokens, width = low_ref.shape
    lead = wgate_ref.shape[0]
    low = low_ref[...]
    acc_ref = refs[3] if last else refs[0]
    grad_active = joined(branch_ref[...], wdown_ref[...].reshape(width, width), 1, 1)
    grad_gate = (grad_active * act1_ref[...].astype(F32)).astype(BF16)
    grad_up = (grad_active * act2_ref[...].astype(F32)).astype(BF16)
    for k, grad in enumerate((grad_gate, grad_up)):
        product = joined(low, grad, 0, 0).astype(BF16)
        if fast and last:
            blocks_ref = refs[-1]
            blocks_ref[k] = product.reshape(blocks_ref.shape[1:])
            spill(place_ref, blocks_ref.at[k], *grad_refs, (k + place_ref[16]) % 2, 0)
        elif fast:
            grad_refs[0][:, k] = product.reshape(lead, -1, width)
        else:
            grad_refs[k][...] = product
    back = joined(grad_gate, wgate_ref[:, 0].reshape(width, width), 1, 1) + joined(
        grad_up, wup_ref[:, 0].reshape(width, width), 1, 1
    )

    @pl.when(step == 0)
    def _():
        acc_ref[...] = sum_ref[...] + back

    @pl.when(step > 0)
    def _():
        acc_ref[...] += back

    if last:
        hid_ref, attn_ref, sums_ref = refs[:3]

        @pl.when(step == pl.num_programs(0) - 1)
        def _():
            grad_hidden, gain, bias = norm_back(
                acc_ref[...], unit_ref[...], scale_ref[...], vec_ref[0:1, :]
            )
            hid_ref[...] = grad_hidden
            attn_ref[...] = grad_hidden.astype(BF16)
            sums_ref[0:1, :] = gain
            sums_ref[1:2, :] = bias


def gates_back(part, after, place, branch, so_far, to_gate, to_up, low, units, scaling, vectors, pack):
    tokens, width = low.shape
    lead, _, per, _ = pack.shape
    steps = 2
    first = part * steps
    last = part == 1
    shape = jax.ShapeDtypeStruct
    full = lambda *dims: pl.BlockSpec(dims, lambda i, *p: (0,) * len(dims))
    flat = full(tokens, width)
    column = pl.BlockSpec((tokens, width), lambda i, *p: (0, first + i))
    ins = [flat, flat, column, column, flat, flat, full(tokens, 1), full(4, width),
           pl.BlockSpec((lead, 1, per, width), lambda i, *p: (0, first + i, 0, 0)),
           pl.BlockSpec((lead, 1, per, width), lambda i, *p: (0, 4 + first + i, 0, 0)),
           down_spec(pack, first)]
    ins += [pl.BlockSpec(memory_space=pl.ANY)] * len(after)
    outs, shapes, scratch = [flat], [shape((tokens, width), F32)], []
    if last:
        outs += [flat, full(2, width)]
        shapes += [shape((tokens, width), BF16), shape((2, width), F32)]
        scratch = [pltpu.VMEM((tokens, width), F32)]
    args = (branch, so_far, to_gate, to_up, low, units, scaling, vectors, pack, pack, pack, *after)
    more = dict(
        compiler_params=params(),
        cost_estimate=LONG,
    )
    fast = place is not None
    kernel = lambda *refs: gates_kernel(fast, last, len(after), *refs)
    if not fast:
        return pl.pallas_call(
            kernel,
            grid=(steps,),
            in_specs=ins,
            out_specs=[pl.BlockSpec((width, width), lambda i: (0, i))] * 2 + outs,
            out_shape=[shape((width, steps * width), BF16)] * 2 + shapes,
            scratch_shapes=scratch,
            **more,
        )(*args)
    if not last:
        return pl.pallas_call(
            kernel,
            grid=(steps,),
            in_specs=ins,
            out_specs=[pl.BlockSpec((lead, 2, per, width), lambda i: (0, 2 + i, 0, 0))] + outs,
            out_shape=[shape(after[0].shape, BF16)] + shapes,
            input_output_aliases={11: 0},
            **more,
        )(*args)
    keep, send, *others = pl.pallas_call(
        kernel,
        grid_spec=pltpu.PrefetchScalarGridSpec(
            num_scalar_prefetch=1,
            grid=(steps,),
            in_specs=ins,
            out_specs=[pl.BlockSpec((8, 2, 1, per, width), lambda i, p: (0, 0, i, 0, 0))] * 2
            + outs,
            scratch_shapes=scratch + [pltpu.VMEM((2, lead, per, width), BF16)],
        ),
        out_shape=[shape((8, 2, steps, per, width), BF16)] * 2 + shapes,
        **more,
    )(place, *args)
    grads = tuple(a.reshape(2, 4, 2, steps, per, width) for a in (keep, send))
    return (grads, *others)


def attend_back_kernel(fast, first, pairs, vectors, waits, *refs):
    refs = list(refs)
    place_ref = refs.pop(0) if fast else None
    (rows_ref, wqkv_ref, wout_ref, cos_ref, sin_ref, mark_ref, markt_ref,
     q_ref, k_ref, v_ref, att_ref, grad_ref, back_ref) = refs[:13]
    sum_refs = refs[13 : 13 + vectors]
    refs = refs[13 + vectors + waits :]
    grad_refs = [refs.pop(0) for _ in range(2 if fast else 1)]
    tok_ref = refs.pop(0)
    if first:
        gatt_ref = refs.pop(0)
    else:
        gatt_ref = grad_ref
    bias_ref, mixed_ref = refs[:2]

    def emit(at, value):
        if fast:
            blocks_ref = refs[-1]
            lead, sides, per, side_columns = blocks_ref.shape
            done = 0
            while done < value.shape[1]:
                side, start = divmod(at + done, side_columns)
                count = min(side_columns - start, value.shape[1] - done)
                blocks_ref[:, side, :, start : start + count] = value[
                    :, done : done + count
                ].reshape(lead, per, count)
                done += count
        else:
            grad_refs[0][:, at : at + value.shape[1]] = value

    rows = rows_ref[...]
    tokens, width = rows.shape
    pair = 2 * HD
    cosine, sine = cos_ref[...], sin_ref[...]
    bias_ref[...] = jnp.where(mark_ref[...] == markt_ref[...], 0.0, MASKED)
    base = 0
    if first:
        grad = grad_ref[...]
        emit(0, joined(att_ref[...], grad, 0, 0).astype(BF16))
        base = width
        gatt_ref[...] = joined(grad, wout_ref[:, 0].reshape(width, width), 1, 1).astype(BF16)
    first_half = lax.broadcasted_iota(jnp.int32, (tokens, pair), 1) < HD
    for local, index in enumerate(pairs):
        at, to = index * pair, local * pair
        query = q_ref[:, at : at + pair]
        key = k_ref[:, at : at + pair]
        value = v_ref[:, at : at + pair]
        grad_out = gatt_ref[:, at : at + pair]
        found = []
        for half in range(2):
            inside = first_half if half == 0 else jnp.logical_not(first_half)
            scores = (
                joined(jnp.where(inside, key, jnp.zeros_like(key)), query, 1, 1) * HD**-0.5
                + bias_ref[...]
            )
            raised = jnp.exp(scores - jnp.max(scores, axis=0, keepdims=True))
            probs = raised * (1.0 / jnp.sum(raised, axis=0, keepdims=True))
            grad_probs = joined(
                jnp.where(inside, value, jnp.zeros_like(value)), grad_out, 1, 1
            )
            delta = jnp.sum(probs * grad_probs, axis=0, keepdims=True)
            grad_scores = (probs * (grad_probs - delta)).astype(BF16)
            found.append(
                (
                    joined(grad_scores, key, 0, 0),
                    joined(grad_scores, query, 1, 0),
                    joined(probs.astype(BF16), grad_out, 1, 0),
                )
            )
        grad_query = jnp.where(first_half, found[0][0], found[1][0]) * HD**-0.5
        grad_key = jnp.where(first_half, found[0][1], found[1][1]) * HD**-0.5
        grad_value = jnp.where(first_half, found[0][2], found[1][2])
        mixed_ref[0, :, to : to + pair] = (
            grad_query * cosine - partner(grad_query) * sine
        ).astype(BF16)
        mixed_ref[1, :, to : to + pair] = (
            grad_key * cosine - partner(grad_key) * sine
        ).astype(BF16)
        mixed_ref[2, :, to : to + pair] = grad_value.astype(BF16)
    span = pair * len(pairs)
    at = pairs[0] * pair
    for part in range(3):
        emit(base + part * span, joined(rows, mixed_ref[part], 0, 0).astype(BF16))
    if vectors:
        emit(base + 3 * span, two_parts([ref[...] for ref in sum_refs]))
    if fast:
        sides = refs[-1].shape[1]
        for side in range(sides):
            to = (side + place_ref[16]) % 2 if sides == 2 else 0
            spill(place_ref, refs[-1].at[:, side], *grad_refs, to)
    back = back_ref[...]
    for part in range(3):
        matrix = wqkv_ref[:, part].reshape(width, width)[:, at : at + span]
        back += joined(mixed_ref[part], matrix, 1, 1)
    tok_ref[...] = back


def two_parts(vectors):
    values = jnp.concatenate(vectors, axis=0)
    upper = values.astype(BF16).astype(F32)
    blank = jnp.zeros((PAD - 2 * values.shape[0], values.shape[1]), F32)
    return jnp.concatenate([upper, values - upper, blank], axis=0).T.astype(BF16)


def attend_back(
    pairs, vectors, after, place, rows, pack, cosine, sine, labels, query, key, value, attended, grad, so_far
):
    tokens, width = rows.shape
    lead, _, per, _ = pack.shape
    first = pairs[0] == 0
    span = 2 * HD * len(pairs)
    columns = 3 * span + (width if first else 0) + (PAD if vectors else 0)
    sides = 1 if first else 2
    shape = jax.ShapeDtypeStruct
    full = lambda *dims: pl.BlockSpec(dims, lambda i, *p: (0,) * len(dims))
    flat = full(tokens, width)
    mark = labels.astype(F32)
    ins = [flat,
           pl.BlockSpec((lead, 3, per, width), lambda i, *p: (0, 3, 0, 0)),
           pl.BlockSpec((lead, 1, per, width), lambda i, *p: (0, 8, 0, 0)),
           full(tokens, 2 * HD), full(tokens, 2 * HD), full(tokens, 1), full(1, tokens)]
    ins += [flat] * 6 + [full(2, width)] * len(vectors)
    ins += [pl.BlockSpec(memory_space=pl.ANY)] * len(after)
    outs, shapes = [flat], [shape((tokens, width), F32)]
    if first:
        outs, shapes = outs + [flat], shapes + [shape((tokens, width), BF16)]
    scratch = [pltpu.VMEM((tokens, tokens), F32), pltpu.VMEM((3, tokens, span), BF16)]
    args = (rows, pack, pack, cosine, sine, mark[:, None], mark[None, :],
            query, key, value, attended, grad, so_far, *vectors, *after)
    more = dict(
        compiler_params=params(),
        cost_estimate=LONG,
    )
    fast = place is not None
    kernel = lambda *refs: attend_back_kernel(
        fast, first, pairs, len(vectors), len(after), *refs
    )
    if not fast:
        return pl.pallas_call(
            kernel,
            grid=(1,),
            in_specs=ins,
            out_specs=[full(width, columns)] + outs,
            out_shape=[shape((width, columns), BF16)] + shapes,
            scratch_shapes=scratch,
            **more,
        )(*args)
    keep, send, *others = pl.pallas_call(
        kernel,
        grid_spec=pltpu.PrefetchScalarGridSpec(
            num_scalar_prefetch=1,
            grid=(1,),
            in_specs=ins,
            out_specs=[full(8, sides, per, columns // sides)] * 2 + outs,
            scratch_shapes=scratch + [pltpu.VMEM((lead, sides, per, columns // sides), BF16)],
        ),
        out_shape=[shape((8, sides, per, columns // sides), BF16)] * 2 + shapes,
        **more,
    )(place, *args)
    return (
        tuple(a.reshape(2, 4, sides, 1, per, columns // sides) for a in (keep, send)),
        *others,
    )


def reduce_digit(parts, sizes, place, digit):
    size = sizes[place]
    total = pick(parts, 0, digit).astype(F32)
    for shift in range(1, size):
        sent = pick(parts, 0, (digit + shift) % size).astype(BF16)
        total += lax.ppermute(sent, "dp", digit_shift(sizes, place, shift)).astype(F32)
    return total


def shared_sum(grad, sizes, digits, tower_index):
    rows, columns = grad.shape
    count = math.prod(sizes)
    per = rows // count
    tiles = columns // 128
    side = max(1, round(tiles * 0.3)) * 128
    middle = columns - 2 * side
    last = len(sizes) - 1
    blocks = grad.astype(BF16).reshape(count // sizes[last], sizes[last], per, columns)
    chip = reduce_digit(jnp.moveaxis(blocks, 1, 0), sizes, last, digits[last]).astype(BF16)
    lead = chip.shape[0]
    mine = lax.dynamic_slice(chip, (0, 0, tower_index * (columns - side)), (lead, per, side))
    other = lax.dynamic_slice(
        chip, (0, 0, (1 - tower_index) * (columns - side)), (lead, per, side)
    )
    mine = mine.astype(F32) + lax.ppermute(other, "tower", SWAP).astype(F32)
    part = jnp.concatenate([mine.astype(BF16), chip[:, :, side : side + middle]], axis=2)
    for place in range(last - 1, -1, -1):
        size = sizes[place]
        part = jnp.moveaxis(part.reshape(part.shape[0] // size, size, per, side + middle), 1, 0)
        part = reduce_digit(part, sizes, place, digits[place]).astype(BF16)
    part = part[0]
    back = lax.ppermute(part, "tower", SWAP).astype(F32)
    part = part.astype(F32)
    centre = part[:, side:] + back[:, side:]
    first = tower_index == 0
    return jnp.concatenate(
        [
            jnp.where(first, part[:, :side], back[:, :side]),
            centre,
            jnp.where(first, back[:, :side], part[:, :side]),
        ],
        axis=1,
    )


def plus_kernel(plan, vectors, count, *refs):
    for out_ref, terms in zip(refs[count:], plan, strict=True):
        total = None
        for place, index in terms:
            piece = refs[place][index].astype(F32)
            total = piece if total is None else total + piece
        total = total.reshape(out_ref.shape)
        if vectors:
            at = total.shape[-1] - PAD
            parts = total[..., at:].reshape(-1, PAD)
            lane = lax.broadcasted_iota(jnp.int32, parts.shape, 1)
            values = parts + pltpu.roll(parts, PAD - VECTORS, 1)
            upper = values.astype(BF16).astype(F32)
            lower = pltpu.roll(values - upper, VECTORS, 1)
            parts = jnp.where(lane < VECTORS, upper, jnp.where(lane < 2 * VECTORS, lower, 0.0))
            out_ref[..., :at] = total[..., :at].astype(BF16)
            out_ref[..., at:] = parts.astype(BF16).reshape(*out_ref.shape[:-1], PAD)
        else:
            out_ref[...] = total.astype(BF16)


def plus(inputs, axis, plan, shapes, out_axes, after=(), vectors=False):
    def spec(dims, along):
        if axis is None:
            return pl.BlockSpec(dims, lambda i: (0,) * len(dims))
        block = tuple(1 if d == along else n for d, n in enumerate(dims))
        return pl.BlockSpec(
            block, lambda i: tuple(i if d == along else 0 for d in range(len(dims)))
        )

    steps = 1 if axis is None else inputs[0].shape[axis]
    return pl.pallas_call(
        lambda *refs: plus_kernel(
            plan, vectors, len(inputs), *refs[: len(inputs)], *refs[len(inputs) + len(after) :]
        ),
        grid=(steps,),
        in_specs=[spec(a.shape, axis) for a in inputs]
        + [pl.BlockSpec(memory_space=pl.ANY)] * len(after),
        out_specs=[spec(d, out_axes) for d in shapes],
        out_shape=[jax.ShapeDtypeStruct(d, BF16) for d in shapes],
        compiler_params=params(),
        cost_estimate=SHORT,
    )(*inputs, *after)


class GradSum:
    def __init__(self, pair, sizes, vectors=False):
        self.sizes = sizes
        self.vectors = vectors
        self.keep, send = pair
        self.sides = self.keep.shape[2]
        self.tail = self.keep.shape[3:]
        self.got = self.shift(send, 2)

    def shift(self, value, place, count=1):
        return lax.ppermute(value, "dp", digit_shift(self.sizes, place, count))

    def over_core(self, *after):
        whole = slice(None)
        if self.sides == 2:
            plan = [
                [(0, (whole, whole, k)), (1, (whole, whole, k))] for k in (1, 0)
            ]
            shapes = [(2, 4, *self.tail)] * 2
            lent, self.held = plus((self.keep, self.got), 1, plan, shapes, 1, after, self.vectors)
            self.got = lax.ppermute(lent, "tower", SWAP)
            return lent
        return self.send_y(self.keep, self.got, after)

    def over_tower(self, *after):
        return self.send_y(self.held, self.got, after)

    def send_y(self, held, got, after):
        plan = [[(0, (k,)), (1, (k,))] for k in (1, 0)]
        shapes = [(4, *self.tail)] * 2
        moving, self.held = plus((held, got), 1, plan, shapes, 0, after, self.vectors)
        self.got = self.shift(moving, 1)
        return moving

    def over_y(self, *after):
        plan = [[(0, (k,)), (1, (k,))] for k in range(4)]
        *moving, self.held = plus(
            (self.held, self.got), None, plan[1:] + plan[:1], [self.tail] * 4, None, after,
            self.vectors,
        )
        self.got = [self.shift(part, 0, k + 1) for k, part in enumerate(moving)]
        return self.held

    def over_z(self, *after):
        plan = [[(k, (Ellipsis,)) for k in range(4)]]
        (self.held,) = plus(
            (self.held, *self.got), None, plan, [self.tail], None, after, self.vectors
        )
        self.got = lax.ppermute(self.held, "tower", SWAP)
        return self.held

    def result(self, tower_index):
        if self.sides == 1:
            return (self.held.astype(F32) + self.got.astype(F32))[None]
        first = tower_index == 0
        return jnp.stack(
            [jnp.where(first, self.held, self.got), jnp.where(first, self.got, self.held)]
        ).astype(F32)


def sum_norms(sums_one, sums_two, dp_count):
    sums = jnp.concatenate([sums_one, sums_two], axis=0)
    sums = sums.reshape(4, dp_count, -1).transpose(1, 0, 2)
    sums = jnp.concatenate([sums, sums], axis=0)
    return jnp.sum(lax.all_to_all(sums, ("tower", "dp"), 0, 0, tiled=True), axis=0)


def beside(chunks):
    return jnp.concatenate(list(chunks), axis=1)


def body(
    tokens,
    lengths,
    pos_doc,
    w_qkv,
    w_out,
    w_gate,
    w_up,
    w_down,
    ln1_gain,
    ln1_bias,
    ln2_gain,
    ln2_bias,
):
    dp_count = lax.axis_size("dp")
    device_count = 2 * dp_count
    sizes = split_dp(dp_count)
    dp_index = lax.axis_index("dp")
    tower_index = lax.axis_index("tower")
    digits = digits_of(dp_index, sizes)
    per, narrow = w_out.shape
    wide = w_gate.shape[1]
    spread = wide // narrow

    chunks = [w_gate[:, at : at + narrow] for at in range(0, wide, narrow)]
    chunks += [w_up[:, at : at + narrow] for at in range(0, wide, narrow)]
    chunks += [w_out] + [w_qkv[:, at : at + narrow] for at in range(0, 3 * narrow, narrow)]
    chunks += [w_down]
    own_pack = jnp.concatenate(chunks, axis=0)
    pack = lax.all_gather(own_pack, "dp", axis=0, tiled=True)
    pack = pack.reshape(dp_count, 4 * spread, per, narrow)
    if per % 16:
        front = pack[:, : 3 * spread].transpose(1, 0, 2, 3).reshape(3 * spread, narrow, narrow)
        back = pack[:, 3 * spread :].reshape(spread, narrow, narrow)
        pack = jnp.concatenate([front, back], axis=0)[None]
    vectors_own = jnp.stack([ln1_gain, ln1_bias, ln2_gain, ln2_bias])
    vectors = lax.all_to_all(
        jnp.broadcast_to(vectors_own[None], (dp_count, 4, per)), "dp", 0, 0, tiled=True
    )
    vectors = vectors.transpose(1, 0, 2).reshape(4, narrow).astype(F32)

    rows_in = tokens[0]
    row_count = rows_in.shape[0]
    pooling, labels, offsets = layout(lengths[0], row_count)
    pool_t = pooling.T
    cosine, sine = rotary_tables(offsets)

    query, key, value, attended, first_low, unit_one, scale_one = attend(
        rows_in, pack, cosine, sine, labels, vectors
    )
    active, to_gate, to_up, unit_two, scale_two, pooled, unit_vectors = feed(
        first_low, unit_one, pack, vectors, pool_t
    )
    seq_count = unit_vectors.shape[0]
    everyone = lax.all_to_all(
        jnp.broadcast_to(unit_vectors[None], (device_count,) + unit_vectors.shape),
        ("tower", "dp"),
        0,
        0,
        tiled=True,
    ).reshape(device_count * seq_count, narrow)
    loss_value, grad_pooled = loss_and_grad(
        everyone, pos_doc, tower_index, dp_index, unit_vectors, pooled
    )
    fast = per % 16 == 0 and sizes == [4, 2, 2] and spread == 4
    place = place_table(digits, tower_index) if fast else None
    grad_down, grad_mid, grad_branch, sums_two = down_back(
        (dp_count, per) if fast else None,
        grad_pooled, pool_t, unit_two, scale_two, vectors, active,
    )
    feed_args = (to_gate, to_up, first_low, unit_one, scale_one, vectors, pack)
    heads_args = (rows_in, pack, cosine, sine, labels, query, key, value, attended)
    pairs = tuple(range(narrow // (2 * HD)))
    cut = max(1, len(pairs) * 2 // 3)
    if fast:
        grad_one, so_far = gates_back(0, (grad_down,), place, grad_branch, grad_mid, *feed_args)
        one = lax.psum_scatter(
            grad_one.reshape(-1, narrow), "dp", scatter_dimension=0, tiled=True
        )
        grad_two, grad_hidden, grad_attn, sums_one = gates_back(
            1, (), place, grad_branch, so_far, *feed_args
        )
        two = GradSum(grad_two, sizes)
        grad_three, so_far, grad_attended = attend_back(
            pairs[:cut], (sums_one, sums_two), (), place, *heads_args, grad_attn, grad_hidden
        )
        three = GradSum(grad_three, sizes, vectors=True)
        order = two.over_core(so_far)
        grad_four, grad_rows = attend_back(
            pairs[cut:], (), (order,), place, *heads_args, grad_attended, so_far
        )
        four = GradSum(grad_four, sizes)
        order = three.over_core(grad_rows)
        order = four.over_core(order)
        order = two.over_tower(order)
        order = four.over_tower(order)
        order = three.over_y(order)
        order = two.over_y(order)
        order = four.over_y(order)
        order = three.over_z(order)
        order = two.over_z(order)
        order = four.over_z(order)
        one = one.astype(F32) + lax.ppermute(one, "tower", SWAP).astype(F32)
        ones = one.reshape(2 * spread, per, narrow)
        twos = two.result(tower_index)
        sum_down = ones[:spread].reshape(spread * per, narrow)
        sum_gate = beside([*ones[spread::2], *twos[0]])
        sum_up = beside([*ones[spread + 1 :: 2], *twos[1]])
        heads_one = three.result(tower_index)[0, 0]
        sums = heads_one[:, -PAD:].T
        sums = sums[:VECTORS] + sums[VECTORS : 2 * VECTORS]
        heads_two = beside(four.result(tower_index)[:, 0])
    else:
        grad_gate, grad_up, so_far = gates_back(0, (), None, grad_branch, grad_mid, *feed_args)
        more_gate, more_up, grad_hidden, grad_attn, sums_one = gates_back(
            1, (), None, grad_branch, so_far, *feed_args
        )
        grad_gate = jnp.concatenate([grad_gate, more_gate], axis=1)
        grad_up = jnp.concatenate([grad_up, more_up], axis=1)
        heads_one, so_far, grad_attended = attend_back(
            pairs[:cut], (), (), None, *heads_args, grad_attn, grad_hidden
        )
        heads_two, grad_rows = attend_back(
            pairs[cut:], (), (), None, *heads_args, grad_attended, so_far
        )
        down_rows = (
            grad_down.reshape(dp_count, spread, per, narrow)
            .transpose(0, 2, 1, 3)
            .reshape(narrow, wide)
        )
        sum_down = shared_sum(down_rows, sizes, digits, tower_index)
        sum_down = (
            sum_down.reshape(per, spread, narrow).transpose(1, 0, 2).reshape(wide // dp_count, narrow)
        )
        sum_gate = shared_sum(grad_gate, sizes, digits, tower_index)
        sum_up = shared_sum(grad_up, sizes, digits, tower_index)
        heads_one = shared_sum(heads_one, sizes, digits, tower_index)
        heads_two = shared_sum(heads_two, sizes, digits, tower_index)
    sum_out = heads_one[:, :narrow]
    one, two = cut * 2 * HD, (len(pairs) - cut) * 2 * HD
    sum_qkv = beside(
        piece
        for k in range(3)
        for piece in (
            heads_one[:, narrow + k * one : narrow + (k + 1) * one],
            heads_two[:, k * two : (k + 1) * two],
        )
    )

    if not fast:
        sums = sum_norms(sums_one, sums_two, dp_count)
    return (
        loss_value.reshape(()),
        unit_vectors[None],
        grad_rows[None],
        sum_qkv,
        sum_out,
        sum_gate,
        sum_up,
        sum_down,
        sums[0],
        sums[1],
        sums[2],
        sums[3],
    )


def solution(mesh):
    placed = (
        P("tower", "dp", None),
        P("tower", "dp"),
        P(),
        P("dp", None),
        P("dp", None),
        P("dp", None),
        P("dp", None),
        P("dp", None),
        P("dp"),
        P("dp"),
        P("dp"),
        P("dp"),
    )
    return jax.shard_map(
        body,
        mesh=mesh,
        in_specs=placed,
        out_specs=(
            P(),
            P("tower", "dp", None),
            P("tower", "dp", None),
            P("dp", None),
            P("dp", None),
            P("dp", None),
            P("dp", None),
            P("dp", None),
            P("dp"),
            P("dp"),
            P("dp"),
            P("dp"),
        ),
        check_vma=False,
    )
```

```python
import math

import jax
import jax.numpy as jnp
from jax import lax
from jax.experimental import pallas as pl
from jax.experimental.pallas import tpu as pltpu
from jax.sharding import PartitionSpec as P

HD = 64
PAD = 128
VECTORS = 4
TEMPER = 0.05
EPS_NORM = 1e-05
EPS_UNIT = 1e-06
MASKED = -1e30
F32 = jnp.float32
BF16 = jnp.bfloat16
MIB = 1 << 20
LONG = pl.CostEstimate(flops=100000000000, bytes_accessed=100000000, transcendentals=0)
SHORT = pl.CostEstimate(flops=100000000000, bytes_accessed=100000000, transcendentals=0)


def joined(left_arr, right_arr, left_dim, right_dim):
    return lax.dot_general(
        left_arr,
        right_arr,
        (((left_dim,), (right_dim,)), ((), ())),
        preferred_element_type=F32,
    )


def joined_high(left_arr, right_arr, left_dim, right_dim):
    return lax.dot_general(
        left_arr,
        right_arr,
        (((left_dim,), (right_dim,)), ((), ())),
        precision=lax.Precision.HIGHEST,
        preferred_element_type=F32,
    )


def split_dp(count):
    sizes = [2] if count % 2 == 0 else []
    rest = count // 2 if sizes else count
    front = []
    while rest > 1:
        step = 4 if rest % 4 == 0 else (2 if rest % 2 == 0 else rest)
        front.append(step)
        rest //= step
    return front + sizes


def digit_shift(sizes, place, shift):
    stride = math.prod(sizes[place + 1 :])
    size = sizes[place]
    pairs = []
    for index in range(math.prod(sizes)):
        digit = index // stride % size
        pairs.append((index, index + ((digit + shift) % size - digit) * stride))
    return pairs


def digits_of(index, sizes):
    found = []
    for size in reversed(sizes):
        found.append(index % size)
        index = index // size
    return found[::-1]


SWAP = [(0, 1), (1, 0)]


def pick(array, axis, place):
    return lax.dynamic_index_in_dim(array, place, axis, keepdims=False)


def layout(seq_spans, row_count):
    seq_total = seq_spans.shape[0]
    starts = jnp.cumsum(seq_spans) - seq_spans
    places = jnp.arange(row_count, dtype=jnp.int32)
    member = (
        (places[None, :] >= starts[:, None]) & (places[None, :] < (starts + seq_spans)[:, None])
    ).astype(jnp.int32)
    labels = jnp.sum(member * jnp.arange(seq_total, dtype=jnp.int32)[:, None], axis=0)
    offsets = places - jnp.sum(member * starts[:, None], axis=0)
    pooling = member.astype(F32) / seq_spans.astype(F32)[:, None]
    return (pooling, labels, offsets)


def rotary_tables(offsets):
    half_size = HD // 2
    frequency = 1000.0 ** (-jnp.arange(half_size, dtype=F32) / half_size)
    angles = offsets.astype(F32)[:, None] * frequency[None, :]
    cosine, sine = jnp.cos(angles), jnp.sin(angles)
    return (
        jnp.concatenate([cosine] * 4, axis=1),
        jnp.concatenate([-sine, sine, -sine, sine], axis=1),
    )


def partner(values):
    lane = lax.broadcasted_iota(jnp.int32, values.shape, 1)
    return jnp.where(
        lane % HD < HD // 2, pltpu.roll(values, 96, 1), pltpu.roll(values, 32, 1)
    )


def reorder(source):
    count = source.shape[1]
    rows = lax.broadcasted_iota(jnp.int32, (count, count), 0)
    return jnp.where(rows == source, 1.0, 0.0).astype(BF16)


def unit_rows(values):
    centered = values - jnp.mean(values, axis=-1, keepdims=True)
    scaling = lax.rsqrt(jnp.mean(centered * centered, axis=-1, keepdims=True) + EPS_NORM)
    return centered * scaling, scaling


def norm_back(grad_rows, units, scaling, gain_row):
    along = grad_rows * gain_row
    back_rows = scaling * (
        along
        - jnp.mean(along, axis=-1, keepdims=True)
        - units * jnp.mean(along * units, axis=-1, keepdims=True)
    )
    return (
        back_rows,
        jnp.sum(grad_rows * units, axis=0, keepdims=True),
        jnp.sum(grad_rows, axis=0, keepdims=True),
    )


def whole_spec():
    return pl.BlockSpec(memory_space=pltpu.VMEM)


def params(mib=60):
    return pltpu.CompilerParams(vmem_limit_bytes=mib * MIB)


def pack_kernel(*refs):
    *weight_refs, out_ref = refs
    rows, width = weight_refs[2].shape
    to = 0
    for ref in weight_refs:
        count = ref.shape[0]
        for at in range(0, ref.shape[1], width):
            out_ref[to : to + count, :] = ref[:, at : at + width]
            to += count


def pack_own(*weights):
    rows, width = weights[2].shape
    if rows % 16:
        parts = [
            w[:, at : at + width] for w in weights[:-1] for at in range(0, w.shape[1], width)
        ]
        return jnp.concatenate(parts + [weights[-1]], axis=0)
    total = sum(w.size for w in weights) // width
    full = lambda *dims: pl.BlockSpec(dims, lambda i: (0,) * len(dims))
    return pl.pallas_call(
        pack_kernel,
        grid=(1,),
        in_specs=[full(*w.shape) for w in weights],
        out_specs=full(total, width),
        out_shape=jax.ShapeDtypeStruct((total, width), BF16),
        compiler_params=params(),
    )(*weights)


def attend_kernel(
    fast, rows_ref, wqkv_ref, wout_ref, cos_ref, sin_ref, mark_ref, markt_ref, vec_ref, source_ref,
    q_ref, k_ref, v_ref, att_ref, low_ref, unit_ref, scale_ref, *refs,
):
    bias_ref = refs[-1]
    rows = rows_ref[...]
    tokens, width = rows.shape
    pair = 2 * HD
    cosine, sine = cos_ref[...], sin_ref[...]
    bias_ref[...] = jnp.where(mark_ref[...] == markt_ref[...], 0.0, MASKED)
    for part, out_ref in enumerate((q_ref, k_ref, v_ref)):
        mixed = joined(rows, wqkv_ref[:, part].reshape(width, width), 1, 0)
        if part == 2:
            out_ref[...] = mixed.astype(BF16)
        else:
            for at in range(0, width, pair):
                piece = mixed[:, at : at + pair]
                turned = piece * cosine + partner(piece) * sine
                out_ref[:, at : at + pair] = turned.astype(BF16)
    first_half = lax.broadcasted_iota(jnp.int32, (tokens, pair), 1) < HD
    for at in range(0, width, pair):
        query = q_ref[:, at : at + pair]
        key = k_ref[:, at : at + pair]
        value = v_ref[:, at : at + pair]
        outs = []
        for half in range(2):
            inside = first_half if half == 0 else jnp.logical_not(first_half)
            only = jnp.where(inside, query, jnp.zeros_like(query))
            scores = joined(only, key, 1, 1) * HD**-0.5 + bias_ref[...]
            raised = jnp.exp(scores - jnp.max(scores, axis=-1, keepdims=True))
            total = jnp.sum(raised, axis=-1, keepdims=True)
            weights = (raised * (1.0 / total)).astype(BF16)
            outs.append(joined(weights, value, 1, 0))
        att_ref[:, at : at + pair] = jnp.where(first_half, outs[0], outs[1]).astype(BF16)
    hidden = rows.astype(F32) + joined(att_ref[...], wout_ref[:, 0].reshape(width, width), 1, 0)
    units, scaling = unit_rows(hidden)
    unit_ref[...] = units
    scale_ref[...] = scaling
    low_ref[...] = (units * vec_ref[0:1, :] + vec_ref[1:2, :]).astype(BF16)
    if fast:
        keep_ref, send_ref = refs[:2]
        order = reorder(source_ref[...])
        for part, values in enumerate((rows, att_ref[...], low_ref[...])):
            moved = joined(values, order, 1, 0).astype(BF16)
            keep_ref[part] = moved[:, : width // 2]
            send_ref[part] = moved[:, width // 2 :]


def attend(fast, source, rows, pack, cosine, sine, labels, vectors):
    tokens, width = rows.shape
    lead, _, per, _ = pack.shape
    shape = jax.ShapeDtypeStruct
    full = lambda *dims: pl.BlockSpec(dims, lambda i: (0,) * len(dims))
    mark = labels.astype(F32)
    halves = (3, tokens, width // 2)
    more = 2 if fast else 0
    return pl.pallas_call(
        lambda *refs: attend_kernel(fast, *refs),
        grid=(1,),
        in_specs=[
            full(tokens, width),
            pl.BlockSpec((lead, 3, per, width), lambda i: (0, 3, 0, 0)),
            pl.BlockSpec((lead, 1, per, width), lambda i: (0, 8, 0, 0)),
            full(tokens, 2 * HD),
            full(tokens, 2 * HD),
            full(tokens, 1),
            full(1, tokens),
            full(4, width),
            full(1, width),
        ],
        out_specs=[full(tokens, width)] * 6 + [full(tokens, 1)] + [full(*halves)] * more,
        out_shape=[shape((tokens, width), BF16)] * 5
        + [shape((tokens, width), F32), shape((tokens, 1), F32)]
        + [shape(halves, BF16)] * more,
        scratch_shapes=[pltpu.VMEM((tokens, tokens), F32)],
        compiler_params=params(),
        cost_estimate=LONG,
    )(rows, pack, pack, cosine, sine, mark[:, None], mark[None, :], vectors, source)


def feed_kernel(
    fast, low_ref, unit1_ref, wgate_ref, wup_ref, wdown_ref, vec_ref, pool_ref, source_ref,
    togate_ref, toup_ref, unit_ref, scale_ref, pooled_ref, emb_ref, *refs,
):
    acc_ref = refs[-1]
    step = pl.program_id(0)
    tokens, width = low_ref.shape
    low = low_ref[...]
    gate = joined(low, wgate_ref[:, 0].reshape(width, width), 1, 0)
    up = joined(low, wup_ref[:, 0].reshape(width, width), 1, 0)
    sig = 1.0 / (1.0 + jnp.exp(-gate))
    silu = gate * sig
    active = (silu * up).astype(BF16)
    if fast:
        moved = joined(active, reorder(source_ref[...]), 1, 0).astype(BF16)
        refs[0][0] = moved[:, : width // 2]
        refs[1][0] = moved[:, width // 2 :]
    else:
        refs[0][...] = active
    toup_ref[...] = silu.astype(BF16)
    togate_ref[...] = (up * sig * (1.0 + gate * (1.0 - sig))).astype(BF16)
    product = joined(active, wdown_ref[...].reshape(width, width), 1, 0)

    @pl.when(step == 0)
    def _():
        acc_ref[...] = unit1_ref[...] * vec_ref[0:1, :] + vec_ref[1:2, :] + product

    @pl.when(step > 0)
    def _():
        acc_ref[...] += product

    @pl.when(step == pl.num_programs(0) - 1)
    def _():
        units, scaling = unit_rows(acc_ref[...])
        unit_ref[...] = units
        scale_ref[...] = scaling
        second = units * vec_ref[2:3, :] + vec_ref[3:4, :]
        rows = [
            jnp.sum(second * pool_ref[:, s : s + 1], axis=0, keepdims=True)
            for s in range(pool_ref.shape[1])
        ]
        pooled = jnp.concatenate(rows, axis=0)
        pooled_ref[...] = pooled
        emb_ref[...] = pooled * lax.rsqrt(
            jnp.sum(pooled * pooled, axis=-1, keepdims=True) + EPS_UNIT
        )


def feed(fast, source, low, units, pack, vectors, pool_t):
    tokens, width = low.shape
    lead, _, per, _ = pack.shape
    blocks = 4
    seqs = pool_t.shape[1]
    shape = jax.ShapeDtypeStruct
    full = lambda *dims: pl.BlockSpec(dims, lambda i: (0,) * len(dims))
    column = pl.BlockSpec((tokens, width), lambda i: (0, i))
    if fast:
        active = [shape((blocks, tokens, width // 2), BF16)] * 2
        active_specs = [pl.BlockSpec((1, tokens, width // 2), lambda i: (i, 0, 0))] * 2
    else:
        active, active_specs = [shape((tokens, blocks * width), BF16)], [column]
    return pl.pallas_call(
        lambda *refs: feed_kernel(fast, *refs),
        grid=(blocks,),
        in_specs=[
            full(tokens, width),
            full(tokens, width),
            pl.BlockSpec((lead, 1, per, width), lambda i: (0, i, 0, 0)),
            pl.BlockSpec((lead, 1, per, width), lambda i: (0, blocks + i, 0, 0)),
            down_spec(pack),
            full(4, width),
            full(tokens, seqs),
            full(1, width),
        ],
        out_specs=[column] * 2
        + [full(tokens, width), full(tokens, 1), full(seqs, width), full(seqs, width)]
        + active_specs,
        out_shape=[shape((tokens, blocks * width), BF16)] * 2
        + [
            shape((tokens, width), F32),
            shape((tokens, 1), F32),
            shape((seqs, width), F32),
            shape((seqs, width), F32),
        ]
        + active,
        scratch_shapes=[pltpu.VMEM((tokens, width), F32)],
        compiler_params=params(),
        cost_estimate=LONG,
    )(low, units, pack, pack, pack, vectors, pool_t, source)


def down_spec(pack, first=0):
    lead, chunks, per, width = pack.shape
    if lead == 1:
        return pl.BlockSpec((1, 1, per, width), lambda i, *p: (0, chunks - 4 + first + i, 0, 0))
    return pl.BlockSpec((lead // 4, 4, per, width), lambda i, *p: (first + i, 3, 0, 0))


def lse(values, axis):
    top = jnp.max(values, axis=axis, keepdims=True)
    return top + jnp.log(jnp.sum(jnp.exp(values - top), axis=axis, keepdims=True))


def loss_kernel(
    every_ref, match_ref, own_match_ref, tower_ref, emb_ref, pooled_ref, pool_ref, unit_ref,
    scale_ref, vec_ref, *refs,
):
    loss_ref, mid_ref, low_ref, sums_ref = refs[-4:]
    total = every_ref.shape[0] // 2
    queries = every_ref[0:total, :]
    documents = every_ref[total : 2 * total, :]
    similar = joined_high(queries, documents, 1, 1) / TEMPER
    flipped = joined_high(documents, queries, 1, 1) / TEMPER
    row_log = lse(similar, 1)
    loss = (
        0.5 * (jnp.sum(row_log, keepdims=True) + jnp.sum(lse(similar, 0), keepdims=True))
        - jnp.sum(similar * match_ref[...], keepdims=True)
    ) / total
    loss_ref[...] = loss
    first = tower_ref[...] == 0
    others = jnp.where(first, documents, queries)
    other_log = jnp.where(first, lse(similar, 0), lse(flipped, 0))
    own = joined_high(emb_ref[...], others, 1, 1) / TEMPER
    grad_similar = (
        0.5 * (jnp.exp(own - lse(own, 1)) + jnp.exp(own - other_log)) - own_match_ref[...]
    ) / total
    grad_unit = joined_high(grad_similar, others, 1, 0) / TEMPER
    pooled = pooled_ref[...]
    inverse = lax.rsqrt(jnp.sum(pooled * pooled, axis=-1, keepdims=True) + EPS_UNIT)
    along = jnp.sum(pooled * grad_unit, axis=-1, keepdims=True)
    grad_pooled = inverse * grad_unit - inverse * inverse * inverse * pooled * along
    grad_second = sum(
        pool_ref[:, s : s + 1] * grad_pooled[s : s + 1, :] for s in range(grad_pooled.shape[0])
    )
    mid, gain, bias = norm_back(grad_second, unit_ref[...], scale_ref[...], vec_ref[2:3, :])
    mid_ref[...] = mid
    low_ref[...] = mid.astype(BF16)
    sums_ref[0:1, :] = gain
    sums_ref[1:2, :] = bias


def loss_and_grad(
    everyone, pos_doc, tower_index, dp_index, emb, pooled, pool_t, units, scaling, vectors, after
):
    tokens = units.shape[0]
    total = everyone.shape[0] // 2
    seqs, width = emb.shape
    match = (pos_doc[:, None] == jnp.arange(total, dtype=jnp.int32)[None, :]).astype(F32)
    oriented = jnp.where(tower_index == 0, match, match.T)
    own_match = lax.dynamic_slice_in_dim(oriented, dp_index * seqs, seqs, 0)
    shape = jax.ShapeDtypeStruct
    return pl.pallas_call(
        loss_kernel,
        in_specs=[whole_spec()] * 10 + [pl.BlockSpec(memory_space=pl.ANY)] * len(after),
        out_specs=[whole_spec()] * 4,
        out_shape=[shape((1, 1), F32), shape((tokens, width), F32), shape((tokens, width), BF16),
                   shape((2, width), F32)],
        compiler_params=params(),
        cost_estimate=LONG,
    )(everyone, match, own_match, tower_index.reshape(1, 1), emb, pooled, pool_t, units, scaling,
      vectors, *after)


def gates_kernel(fast, branch_ref, mid_ref, act1_ref, act2_ref, unit_ref, scale_ref, vec_ref,
                 two_ref, source_ref, wgate_ref, wup_ref, wdown_ref,
                 grads_ref, hid_ref, attn_ref, sums_ref, *refs):
    acc_ref = refs[-1]
    step = pl.program_id(0)
    tokens, width = mid_ref.shape
    grad_active = joined(branch_ref[...], wdown_ref[...].reshape(width, width), 1, 1)
    grad_gate = (grad_active * act1_ref[...].astype(F32)).astype(BF16)
    grad_up = (grad_active * act2_ref[...].astype(F32)).astype(BF16)
    grads_ref[0, 0] = grad_gate
    grads_ref[1, 0] = grad_up
    back = joined(grad_gate, wgate_ref[:, 0].reshape(width, width), 1, 1) + joined(
        grad_up, wup_ref[:, 0].reshape(width, width), 1, 1
    )

    @pl.when(step == 0)
    def _():
        acc_ref[...] = mid_ref[...] + back

    @pl.when(step > 0)
    def _():
        acc_ref[...] += back

    @pl.when(step == pl.num_programs(0) - 1)
    def _():
        grad_hidden, gain, bias = norm_back(
            acc_ref[...], unit_ref[...], scale_ref[...], vec_ref[0:1, :]
        )
        hid_ref[...] = grad_hidden
        attn_ref[0:tokens, :] = grad_hidden.astype(BF16)
        if fast:
            values = jnp.concatenate([gain, bias, two_ref[...]], axis=0)
            upper = values.astype(BF16).astype(F32)
            blank = jnp.zeros((8, width), F32)
            parts = jnp.concatenate([upper, values - upper, blank], axis=0).astype(BF16)
            moved = joined(parts, reorder(source_ref[...]), 1, 0).astype(BF16)
            attn_ref[tokens:, :] = moved
        else:
            sums_ref[0:1, :] = gain
            sums_ref[1:2, :] = bias


def gates_back(fast, source, branch, mid, to_gate, to_up, units, scaling, vectors, sums_two, pack):
    tokens, width = mid.shape
    lead, _, per, _ = pack.shape
    blocks = 4
    shape = jax.ShapeDtypeStruct
    full = lambda *dims: pl.BlockSpec(dims, lambda i: (0,) * len(dims))
    flat = full(tokens, width)
    column = pl.BlockSpec((tokens, width), lambda i: (0, i))
    rows = tokens + (16 if fast else 0)
    return pl.pallas_call(
        lambda *refs: gates_kernel(fast, *refs),
        grid=(blocks,),
        in_specs=[flat, flat, column, column, flat, full(tokens, 1), full(4, width),
                  full(2, width), full(1, width),
                  pl.BlockSpec((lead, 1, per, width), lambda i: (0, i, 0, 0)),
                  pl.BlockSpec((lead, 1, per, width), lambda i: (0, 4 + i, 0, 0)),
                  down_spec(pack)],
        out_specs=[pl.BlockSpec((2, 1, tokens, width), lambda i: (0, i, 0, 0)), flat,
                   full(rows, width), full(2, width)],
        out_shape=[shape((2, blocks, tokens, width), BF16), shape((tokens, width), F32),
                   shape((rows, width), BF16), shape((2, width), F32)],
        scratch_shapes=[pltpu.VMEM((tokens, width), F32)],
        compiler_params=params(),
        cost_estimate=LONG,
    )(branch, mid, to_gate, to_up, units, scaling, vectors, sums_two, source, pack, pack, pack)


def attend_back_kernel(
    wout_ref, cos_ref, sin_ref, mark_ref, markt_ref, q_ref, k_ref, v_ref, grad_ref, *refs
):
    mixed_ref, bias_ref, gatt_ref = refs[-3:]
    tokens, width = q_ref.shape
    pair = 2 * HD
    cosine, sine = cos_ref[...], sin_ref[...]
    bias_ref[...] = jnp.where(mark_ref[...] == markt_ref[...], 0.0, MASKED)
    gatt_ref[...] = joined(grad_ref[...], wout_ref[:, 0].reshape(width, width), 1, 1).astype(BF16)
    first_half = lax.broadcasted_iota(jnp.int32, (tokens, pair), 1) < HD
    for at in range(0, width, pair):
        query = q_ref[:, at : at + pair]
        key = k_ref[:, at : at + pair]
        value = v_ref[:, at : at + pair]
        grad_out = gatt_ref[:, at : at + pair]
        found = []
        for half in range(2):
            inside = first_half if half == 0 else jnp.logical_not(first_half)
            scores = (
                joined(jnp.where(inside, key, jnp.zeros_like(key)), query, 1, 1) * HD**-0.5
                + bias_ref[...]
            )
            raised = jnp.exp(scores - jnp.max(scores, axis=0, keepdims=True))
            probs = raised * (1.0 / jnp.sum(raised, axis=0, keepdims=True))
            grad_probs = joined(
                jnp.where(inside, value, jnp.zeros_like(value)), grad_out, 1, 1
            )
            delta = jnp.sum(probs * grad_probs, axis=0, keepdims=True)
            grad_scores = (probs * (grad_probs - delta)).astype(BF16)
            found.append(
                (
                    joined(grad_scores, key, 0, 0),
                    joined(grad_scores, query, 1, 0),
                    joined(probs.astype(BF16), grad_out, 1, 0),
                )
            )
        grad_query = jnp.where(first_half, found[0][0], found[1][0]) * HD**-0.5
        grad_key = jnp.where(first_half, found[0][1], found[1][1]) * HD**-0.5
        grad_value = jnp.where(first_half, found[0][2], found[1][2])
        mixed_ref[0, :, at : at + pair] = (
            grad_query * cosine - partner(grad_query) * sine
        ).astype(BF16)
        mixed_ref[1, :, at : at + pair] = (
            grad_key * cosine - partner(grad_key) * sine
        ).astype(BF16)
        mixed_ref[2, :, at : at + pair] = grad_value.astype(BF16)


def attend_back(pack, cosine, sine, labels, query, key, value, grad, after=()):
    tokens, width = query.shape
    lead, _, per, _ = pack.shape
    full = lambda *dims: pl.BlockSpec(dims, lambda i: (0,) * len(dims))
    flat = full(tokens, width)
    mark = labels.astype(F32)
    return pl.pallas_call(
        attend_back_kernel,
        grid=(1,),
        in_specs=[pl.BlockSpec((lead, 1, per, width), lambda i: (0, 8, 0, 0)),
                  full(tokens, 2 * HD), full(tokens, 2 * HD), full(tokens, 1), full(1, tokens)]
        + [flat] * 4 + [pl.BlockSpec(memory_space=pl.ANY)] * len(after),
        out_specs=full(3, tokens, width),
        out_shape=jax.ShapeDtypeStruct((3, tokens, width), BF16),
        scratch_shapes=[pltpu.VMEM((tokens, tokens), F32), pltpu.VMEM((tokens, width), BF16)],
        compiler_params=params(),
        cost_estimate=LONG,
    )(pack, cosine, sine, mark[:, None], mark[None, :], query, key, value, grad, *after)


def tokens_kernel(mixed_ref, hid_ref, wqkv_ref, *refs):
    tokens, width = hid_ref.shape
    back = hid_ref[...]
    for part in range(3):
        back += joined(mixed_ref[part], wqkv_ref[:, part].reshape(width, width), 1, 1)
    refs[-1][...] = back


def tokens_back(mixed, hidden, pack, after=()):
    tokens, width = hidden.shape
    lead, _, per, _ = pack.shape
    full = lambda *dims: pl.BlockSpec(dims, lambda i: (0,) * len(dims))
    return pl.pallas_call(
        tokens_kernel,
        grid=(1,),
        in_specs=[full(3, tokens, width), full(tokens, width),
                  pl.BlockSpec((lead, 3, per, width), lambda i: (0, 3, 0, 0))]
        + [pl.BlockSpec(memory_space=pl.ANY)] * len(after),
        out_specs=full(tokens, width),
        out_shape=jax.ShapeDtypeStruct((tokens, width), F32),
        compiler_params=params(),
        cost_estimate=LONG,
    )(mixed, hidden, pack, *after)


def both(own_left, got_left, own_right, got_right):
    return (joined(own_left, own_right, 0, 0) + joined(got_left, got_right, 0, 0)).astype(BF16)


def steps_call(kernel, grid, ins, args, outs, shapes, scalars=None, after=()):
    ins = ins + [pl.BlockSpec(memory_space=pl.ANY)] * len(after)
    shapes = [jax.ShapeDtypeStruct(dims, BF16) for dims in shapes]
    more = dict(out_shape=shapes, compiler_params=params(), cost_estimate=LONG)
    if scalars is None:
        return pl.pallas_call(
            kernel, grid=grid, in_specs=ins, out_specs=outs, **more
        )(*args, *after)
    return pl.pallas_call(
        kernel,
        grid_spec=pltpu.PrefetchScalarGridSpec(
            num_scalar_prefetch=1, grid=grid, in_specs=ins, out_specs=outs
        ),
        **more,
    )(scalars, *args, *after)


def down_kernel(own_ref, got_ref, grad_ref, got_grad_ref, *refs):
    held_ref, moving_ref = refs[-2:]
    value = both(own_ref[0], got_ref[0], grad_ref[...], got_grad_ref[...])
    half = value.shape[0] // 2
    held_ref[0] = value[:half]
    moving_ref[0] = value[half:]


def down_grads(own, got, grad, got_grad, after=()):
    blocks, tokens, rows = own.shape
    width = grad.shape[1]
    left = pl.BlockSpec((1, tokens, rows), lambda i: (i, 0, 0))
    right = pl.BlockSpec((tokens, width), lambda i: (0, 0))
    out = pl.BlockSpec((1, rows // 2, width), lambda i: (i, 0, 0))
    dims = (blocks, rows // 2, width)
    return steps_call(
        down_kernel, (blocks,), [left, left, right, right], (own, got, grad, got_grad),
        [out, out], [dims, dims], after=after,
    )


def first_kernel(own_ref, got_ref, grad_ref, got_grad_ref, *refs):
    held_ref, moving_ref = refs[-2:]
    value = both(own_ref[0], got_ref[0], grad_ref[0, 0], got_grad_ref[0, 0])
    half = value.shape[0] // 2
    held_ref[...] = value[:half].reshape(held_ref.shape)
    moving_ref[...] = value[half:].reshape(held_ref.shape)


def first_grads(own, got, grads, got_grads, which, part, after=()):
    _, tokens, rows = own.shape
    _, chunks, _, width = grads.shape
    left = pl.BlockSpec((1, tokens, rows), lambda i: (part, 0, 0))
    right = pl.BlockSpec((1, 1, tokens, width), lambda i: (which, i, 0, 0))
    out = pl.BlockSpec((4, 1, rows // 8, width), lambda i: (0, i, 0, 0))
    dims = (4, chunks, rows // 8, width)
    return steps_call(
        first_kernel, (chunks,), [left, left, right, right], (own, got, grads, got_grads),
        [out, out], [dims, dims], after=after,
    )


def tower_kernel(tower_ref, own_ref, got_ref, grad_ref, got_grad_ref, *refs):
    held_ref, lent_ref = refs[-2:]
    value = both(own_ref[0], got_ref[0], grad_ref[0, 0], got_grad_ref[0, 0])
    value = value.reshape(held_ref.shape)
    here = pl.program_id(0) < pl.num_programs(0) // 2

    @pl.when(here)
    def _():
        held_ref[...] = value

    @pl.when(jnp.logical_not(here))
    def _():
        lent_ref[...] = value


def tower_grads(tower, own, got, grads, got_grads, which, chunks, first, part, after=()):
    _, tokens, rows = own.shape
    width = grads.shape[-1]
    half = chunks // 2
    left = pl.BlockSpec((1, tokens, rows), lambda i, t: (part, 0, 0))
    right = pl.BlockSpec(
        (1, 1, tokens, width), lambda i, t: (which, first + (i + half * t[0]) % chunks, 0, 0)
    )
    block = (2, 4, 1, rows // 8, width)
    dims = (2, 4, half, rows // 8, width)
    outs = [
        pl.BlockSpec(block, lambda i, t: (0, 0, jnp.minimum(i, half - 1), 0, 0)),
        pl.BlockSpec(block, lambda i, t: (0, 0, jnp.maximum(i - half, 0), 0, 0)),
    ]
    return steps_call(
        tower_kernel, (chunks,), [left, left, right, right], (own, got, grads, got_grads),
        outs, [dims, dims], scalars=tower, after=after,
    )


def rest_kernel(own_ref, got_ref, attn_ref, got_attn_ref, mixed_ref, got_mixed_ref, *refs):
    held_ref, moving_ref = refs[-2:]
    tokens, width = mixed_ref.shape[1:]
    half = width // 4
    pieces = [
        both(own_ref[1], got_ref[1], attn_ref[0:tokens, :], got_attn_ref[0:tokens, :]),
        both(own_ref[0], got_ref[0], mixed_ref[0], got_mixed_ref[0]),
    ]
    parts = attn_ref[tokens:, : width // 2].astype(F32)
    got = got_attn_ref[tokens:, width // 2 :].astype(F32)
    values = parts[0:4] + parts[4:8] + got[0:4] + got[4:8]
    upper = values.astype(BF16).astype(F32)
    blank = jnp.zeros((PAD - 2 * VECTORS, width // 2), F32)
    pieces.append(jnp.concatenate([upper, values - upper, blank], axis=0).T.astype(BF16))
    at = 0
    for piece in pieces:
        columns = piece.shape[1]
        for k, out_ref in enumerate((held_ref, moving_ref)):
            out_ref[:, :, at : at + columns] = piece[k * 2 * half // 2 : (k + 1) * half].reshape(
                4, -1, columns
            )
        at += columns


def rest_grads(own, got, attn, got_attn, mixed, got_mixed, after=()):
    _, tokens, rows = own.shape
    width = mixed.shape[2]
    full = lambda *dims: pl.BlockSpec(dims, lambda i: (0,) * len(dims))
    one = pl.BlockSpec((1, tokens, width), lambda i: (0, 0, 0))
    dims = (4, rows // 8, 2 * width + PAD)
    return steps_call(
        rest_kernel, (1,),
        [full(*own.shape), full(*own.shape), full(*attn.shape), full(*attn.shape), one, one],
        (own, got, attn, got_attn, mixed, got_mixed),
        [full(*dims)] * 2, [dims, dims], after=after,
    )


def reduce_digit(parts, sizes, place, digit):
    size = sizes[place]
    total = pick(parts, 0, digit).astype(F32)
    for shift in range(1, size):
        sent = pick(parts, 0, (digit + shift) % size).astype(BF16)
        total += lax.ppermute(sent, "dp", digit_shift(sizes, place, shift)).astype(F32)
    return total


def shared_sum(grad, sizes, digits, tower_index):
    rows, columns = grad.shape
    count = math.prod(sizes)
    per = rows // count
    tiles = columns // 128
    side = max(1, round(tiles * 0.3)) * 128
    middle = columns - 2 * side
    last = len(sizes) - 1
    blocks = grad.astype(BF16).reshape(count // sizes[last], sizes[last], per, columns)
    chip = reduce_digit(jnp.moveaxis(blocks, 1, 0), sizes, last, digits[last]).astype(BF16)
    lead = chip.shape[0]
    mine = lax.dynamic_slice(chip, (0, 0, tower_index * (columns - side)), (lead, per, side))
    other = lax.dynamic_slice(
        chip, (0, 0, (1 - tower_index) * (columns - side)), (lead, per, side)
    )
    mine = mine.astype(F32) + lax.ppermute(other, "tower", SWAP).astype(F32)
    part = jnp.concatenate([mine.astype(BF16), chip[:, :, side : side + middle]], axis=2)
    for place in range(last - 1, -1, -1):
        size = sizes[place]
        part = jnp.moveaxis(part.reshape(part.shape[0] // size, size, per, side + middle), 1, 0)
        part = reduce_digit(part, sizes, place, digits[place]).astype(BF16)
    part = part[0]
    back = lax.ppermute(part, "tower", SWAP).astype(F32)
    part = part.astype(F32)
    centre = part[:, side:] + back[:, side:]
    first = tower_index == 0
    return jnp.concatenate(
        [
            jnp.where(first, part[:, :side], back[:, :side]),
            centre,
            jnp.where(first, back[:, :side], part[:, :side]),
        ],
        axis=1,
    )


def plus_kernel(jobs, count, z_ref, *refs):
    for out_ref, (terms, vectors) in zip(refs[count:], jobs, strict=True):
        total = None
        for place, index in terms:
            piece = refs[place][index(z_ref[0]) if callable(index) else index].astype(F32)
            total = piece if total is None else total + piece
        total = total.reshape(out_ref.shape)
        if vectors:
            at = total.shape[-1] - PAD
            parts = total[..., at:].reshape(-1, PAD)
            lane = lax.broadcasted_iota(jnp.int32, parts.shape, 1)
            values = parts + pltpu.roll(parts, PAD - VECTORS, 1)
            upper = values.astype(BF16).astype(F32)
            lower = pltpu.roll(values - upper, VECTORS, 1)
            parts = jnp.where(lane < VECTORS, upper, jnp.where(lane < 2 * VECTORS, lower, 0.0))
            out_ref[..., :at] = total[..., :at].astype(BF16)
            out_ref[..., at:] = parts.astype(BF16).reshape(*out_ref.shape[:-1], PAD)
        else:
            out_ref[...] = total.astype(BF16)


def plus(jobs, z, after=()):
    inputs, outs, shapes = [], [], []
    for arrays, plan, dims, vectors in jobs:
        base = len(inputs)
        inputs += arrays
        outs += [([(base + place, index) for place, index in terms], vectors) for terms in plan]
        shapes += dims
    count = len(inputs)
    spec = lambda dims: pl.BlockSpec(dims, lambda i: (0,) * len(dims))
    return pl.pallas_call(
        lambda *refs: plus_kernel(
            outs, count, *refs[: 1 + count], *refs[1 + count + len(after) :]
        ),
        grid=(1,),
        in_specs=[pl.BlockSpec(memory_space=pltpu.SMEM)]
        + [spec(a.shape) for a in inputs]
        + [pl.BlockSpec(memory_space=pl.ANY)] * len(after),
        out_specs=[spec(dims) for dims in shapes],
        out_shape=[jax.ShapeDtypeStruct(dims, BF16) for dims in shapes],
        compiler_params=params(24),
        cost_estimate=SHORT,
    )(z, *inputs, *after)


class GradSum:
    def __init__(self, pair, sizes, z, by_tower, direct, vectors=False):
        self.sizes = sizes
        self.z = z
        self.direct = direct
        self.vectors = vectors
        self.by_tower = by_tower
        self.held, sent = pair
        self.got = lax.ppermute(sent, "tower", SWAP) if by_tower else self.shift_y(sent)
        self.steps = ["tower", "y", "z"] if by_tower else ["y", "z"]

    def shift_y(self, sent):
        return lax.ppermute(sent, "dp", digit_shift(self.sizes, 1, 1))

    def job(self):
        step = self.steps[0]
        if step == "tower":
            plan = [[(0, (k,)), (1, (k,))] for k in (1, 0)]
            return [self.held, self.got], plan, [self.held.shape[1:]] * 2, self.vectors
        depth = self.sizes[0]
        if step == "y" and self.direct:
            views = [lambda z, k=k: ((z + k) % depth,) for k in (1, 2, 3, 0)]
            plan = [[(0, view), (1, view)] for view in views]
            return [self.held, self.got], plan, [self.held.shape[1:]] * depth, self.vectors
        if step == "y":
            plan = [[(0, (Ellipsis,)), (1, (Ellipsis,))]]
            return [self.held, self.got], plan, [self.held.shape], self.vectors
        if self.direct:
            plan = [[(k, (Ellipsis,)) for k in range(depth)]]
            return [self.held, *self.got], plan, [self.held.shape], self.vectors
        plan = [[(0, (k,)) for k in range(depth)]]
        return [self.got], plan, [self.got.shape[1:]], self.vectors

    def take(self, outs):
        step = self.steps.pop(0)
        if step == "tower":
            moving, self.held = outs
            self.got = self.shift_y(moving)
        elif step == "y" and self.direct:
            *parts, self.held = outs
            self.got = [
                lax.ppermute(part, "dp", digit_shift(self.sizes, 0, k + 1))
                for k, part in enumerate(parts)
            ]
        elif step == "y":
            depth, rest = self.sizes[0], math.prod(self.sizes[1:])
            groups = [[z * rest + other for z in range(depth)] for other in range(rest)]
            self.got = lax.all_to_all(outs[0], "dp", 0, 0, axis_index_groups=groups, tiled=True)
        else:
            (self.held,) = outs
            self.got = lax.ppermute(self.held, "tower", SWAP)

    def result(self, tower_index):
        if not self.by_tower:
            return self.held.astype(F32) + self.got.astype(F32)
        first = tower_index == 0
        return jnp.stack(
            [jnp.where(first, self.held, self.got), jnp.where(first, self.got, self.held)]
        ).astype(F32)


def advance(order, *sums):
    jobs = [one.job() for one in sums]
    outs = plus(jobs, sums[0].z, (order,))
    last = outs[-1]
    for one, (_, plan, _, _) in zip(sums, jobs, strict=True):
        one.take(outs[: len(plan)])
        outs = outs[len(plan) :]
    return last


def sum_norms(sums_one, sums_two, dp_count):
    sums = jnp.concatenate([sums_one, sums_two], axis=0)
    sums = sums.reshape(4, dp_count, -1).transpose(1, 0, 2)
    sums = jnp.concatenate([sums, sums], axis=0)
    return jnp.sum(lax.all_to_all(sums, ("tower", "dp"), 0, 0, tiled=True), axis=0)


def beside(chunks):
    return jnp.concatenate(list(chunks), axis=1)


def column_orders(digits, per, spread, width):
    _, y, c = digits
    place = jnp.arange(width, dtype=jnp.int32)
    block, row = place // per, place % per
    core, dy, z = block // 8, block // 4 % 2, block % 4
    source = ((z * 4 + (dy + y) % 2 * 2 + (core + c) % 2)) * per + row
    device = (dy + y) % 2 * 2 + (core + c) % 2
    return source[None], ((device * spread + block % 4) * per + row)[None]


def body(
    tokens,
    lengths,
    pos_doc,
    w_qkv,
    w_out,
    w_gate,
    w_up,
    w_down,
    ln1_gain,
    ln1_bias,
    ln2_gain,
    ln2_bias,
):
    dp_count = lax.axis_size("dp")
    device_count = 2 * dp_count
    sizes = split_dp(dp_count)
    dp_index = lax.axis_index("dp")
    tower_index = lax.axis_index("tower")
    digits = digits_of(dp_index, sizes)
    per, narrow = w_out.shape
    wide = w_gate.shape[1]
    spread = wide // narrow

    own_pack = pack_own(w_gate, w_up, w_out, w_qkv, w_down)
    pack = lax.all_gather(own_pack, "dp", axis=0, tiled=True)
    pack = pack.reshape(dp_count, 4 * spread, per, narrow)
    if per % 16:
        front = pack[:, : 3 * spread].transpose(1, 0, 2, 3).reshape(3 * spread, narrow, narrow)
        back = pack[:, 3 * spread :].reshape(spread, narrow, narrow)
        pack = jnp.concatenate([front, back], axis=0)[None]
    vectors_own = jnp.stack([ln1_gain, ln1_bias, ln2_gain, ln2_bias])
    vectors = lax.all_to_all(
        jnp.broadcast_to(vectors_own[None], (dp_count, 4, per)), "dp", 0, 0, tiled=True
    )
    vectors = vectors.transpose(1, 0, 2).reshape(4, narrow).astype(F32)

    rows_in = tokens[0]
    row_count = rows_in.shape[0]
    pooling, labels, offsets = layout(lengths[0], row_count)
    pool_t = pooling.T
    cosine, sine = rotary_tables(offsets)

    fast = sizes == [4, 2, 2] and spread == 4 and per % 16 == 0
    source, source_down = column_orders(digits, per, spread, narrow) if fast else (
        jnp.zeros((1, narrow), jnp.int32),
    ) * 2
    core_swap = digit_shift(sizes, len(sizes) - 1, 1)
    swap_cores = lambda values: lax.ppermute(values, "dp", core_swap)
    query, key, value, attended, first_low, unit_one, scale_one, *left = attend(
        fast, source, rows_in, pack, cosine, sine, labels, vectors
    )
    to_gate, to_up, unit_two, scale_two, pooled, unit_vectors, *active = feed(
        fast, source_down, first_low, unit_one, pack, vectors, pool_t
    )
    seq_count = unit_vectors.shape[0]
    everyone = lax.all_to_all(
        jnp.broadcast_to(unit_vectors[None], (device_count,) + unit_vectors.shape),
        ("tower", "dp"),
        0,
        0,
        tiled=True,
    ).reshape(device_count * seq_count, narrow)
    moved = [swap_cores(left[1]), swap_cores(active[1])] if fast else []
    loss_value, grad_mid, grad_branch, sums_two = loss_and_grad(
        everyone, pos_doc, tower_index, dp_index, unit_vectors, pooled, pool_t, unit_two, scale_two,
        vectors, moved,
    )
    grad_feed, grad_hidden, grad_attn, sums_one = gates_back(
        fast, source, grad_branch, grad_mid, to_gate, to_up, unit_one, scale_one, vectors, sums_two,
        pack,
    )
    heads_args = (pack, cosine, sine, labels, query, key, value, grad_attn)
    if fast:
        own, (got, got_active) = left[0], moved
        got_branch = swap_cores(grad_branch)
        got_feed = swap_cores(grad_feed)
        got_attn = swap_cores(grad_attn)
        tower = tower_index.reshape(1).astype(jnp.int32)
        summed = lambda pair, **how: GradSum(pair, sizes, digits[0].reshape(1), **how)
        down = summed(
            down_grads(active[0], got_active, grad_branch, got_branch),
            by_tower=False, direct=False,
        )
        grad_mixed = attend_back(*heads_args, (down.held, got_attn))
        got_mixed = swap_cores(grad_mixed)
        gate = summed(
            tower_grads(
                tower, own, got, grad_feed, got_feed, 0, 4, 0, 2, (grad_mixed,)
            ),
            by_tower=True, direct=True,
        )
        up = summed(
            first_grads(own, got, grad_feed, got_feed, 1, 2, (gate.held,)),
            by_tower=False, direct=True,
        )
        order = advance(up.held, down)
        rest = summed(
            rest_grads(own, got, grad_attn, got_attn, grad_mixed, got_mixed, (order,)),
            by_tower=False, direct=False, vectors=True,
        )
        last = summed(
            tower_grads(
                tower, own, got, grad_mixed[None], got_mixed[None], 0, 2, 1, 0, (rest.held,)
            ),
            by_tower=True, direct=True,
        )
        order = advance(last.held, gate)
        grad_rows = tokens_back(grad_mixed, grad_hidden, pack, (order,))
        order = advance(grad_rows, up)
        order = advance(order, last)
        order = advance(order, down)
        order = advance(order, rest)
        order = advance(order, gate)
        order = advance(order, up)
        order = advance(order, last)
        order = advance(order, rest)
        order = advance(order, gate)
        order = advance(order, last)
        sum_down = down.result(tower_index).reshape(spread * per, narrow)
        sum_gate = beside(gate.result(tower_index).reshape(spread, per, narrow))
        sum_up = beside(up.result(tower_index))
        heads = rest.result(tower_index)
        sum_out = heads[:, :narrow]
        sum_qkv = beside([heads[:, narrow : 2 * narrow], *last.result(tower_index)[:, 0]])
        sums = heads[:, 2 * narrow :].T
        sums = sums[:VECTORS] + sums[VECTORS : 2 * VECTORS]
    else:
        grad_mixed = attend_back(*heads_args)
        grad_rows = tokens_back(grad_mixed, grad_hidden, pack)
        grad_down = joined(active[0], grad_branch, 0, 0)
        down_rows = (
            grad_down.reshape(dp_count, spread, per, narrow)
            .transpose(0, 2, 1, 3)
            .reshape(narrow, wide)
        )
        share = lambda grad: shared_sum(grad, sizes, digits, tower_index)
        sum_down = share(down_rows).reshape(per, spread, narrow).transpose(1, 0, 2)
        sum_down = sum_down.reshape(wide // dp_count, narrow)
        sum_gate, sum_up = (
            share(joined(first_low, beside(grad_feed[k]), 0, 0)) for k in range(2)
        )
        sum_out = share(joined(attended, grad_attn, 0, 0))
        sum_qkv = share(joined(rows_in, beside(grad_mixed), 0, 0))
        sums = sum_norms(sums_one, sums_two, dp_count)
    return (
        loss_value.reshape(()),
        unit_vectors[None],
        grad_rows[None],
        sum_qkv,
        sum_out,
        sum_gate,
        sum_up,
        sum_down,
        sums[0],
        sums[1],
        sums[2],
        sums[3],
    )


def solution(mesh):
    placed = (
        P("tower", "dp", None),
        P("tower", "dp"),
        P(),
        P("dp", None),
        P("dp", None),
        P("dp", None),
        P("dp", None),
        P("dp", None),
        P("dp"),
        P("dp"),
        P("dp"),
        P("dp"),
    )
    return jax.shard_map(
        body,
        mesh=mesh,
        in_specs=placed,
        out_specs=(
            P(),
            P("tower", "dp", None),
            P("tower", "dp", None),
            P("dp", None),
            P("dp", None),
            P("dp", None),
            P("dp", None),
            P("dp", None),
            P("dp"),
            P("dp"),
            P("dp"),
            P("dp"),
        ),
        check_vma=False,
    )
```

```python
import math

import jax
import jax.numpy as jnp
from jax import lax
from jax.experimental import pallas as pl
from jax.experimental.pallas import tpu as pltpu
from jax.sharding import PartitionSpec as P

HD = 64
PAD = 128
VECTORS = 4
TEMPER = 0.05
EPS_NORM = 1e-05
EPS_UNIT = 1e-06
MASKED = -1e30
F32 = jnp.float32
BF16 = jnp.bfloat16
MIB = 1 << 20
LONG = pl.CostEstimate(flops=100000000000, bytes_accessed=100000000, transcendentals=0)
SHORT = pl.CostEstimate(flops=100000000000, bytes_accessed=100000000, transcendentals=0)


def joined(left_arr, right_arr, left_dim, right_dim):
    return lax.dot_general(
        left_arr,
        right_arr,
        (((left_dim,), (right_dim,)), ((), ())),
        preferred_element_type=F32,
    )


def joined_high(left_arr, right_arr, left_dim, right_dim):
    return lax.dot_general(
        left_arr,
        right_arr,
        (((left_dim,), (right_dim,)), ((), ())),
        precision=lax.Precision.HIGHEST,
        preferred_element_type=F32,
    )


def split_dp(count):
    sizes = [2] if count % 2 == 0 else []
    rest = count // 2 if sizes else count
    front = []
    while rest > 1:
        step = 4 if rest % 4 == 0 else (2 if rest % 2 == 0 else rest)
        front.append(step)
        rest //= step
    return front + sizes


def digit_shift(sizes, place, shift):
    stride = math.prod(sizes[place + 1 :])
    size = sizes[place]
    pairs = []
    for index in range(math.prod(sizes)):
        digit = index // stride % size
        pairs.append((index, index + ((digit + shift) % size - digit) * stride))
    return pairs


def digits_of(index, sizes):
    found = []
    for size in reversed(sizes):
        found.append(index % size)
        index = index // size
    return found[::-1]


SWAP = [(0, 1), (1, 0)]


def pick(array, axis, place):
    return lax.dynamic_index_in_dim(array, place, axis, keepdims=False)


def layout(seq_spans, row_count):
    seq_total = seq_spans.shape[0]
    starts = jnp.cumsum(seq_spans) - seq_spans
    places = jnp.arange(row_count, dtype=jnp.int32)
    member = (
        (places[None, :] >= starts[:, None]) & (places[None, :] < (starts + seq_spans)[:, None])
    ).astype(jnp.int32)
    labels = jnp.sum(member * jnp.arange(seq_total, dtype=jnp.int32)[:, None], axis=0)
    offsets = places - jnp.sum(member * starts[:, None], axis=0)
    pooling = member.astype(F32) / seq_spans.astype(F32)[:, None]
    return (pooling, labels, offsets)


def rotary_tables(offsets):
    half_size = HD // 2
    frequency = 1000.0 ** (-jnp.arange(half_size, dtype=F32) / half_size)
    angles = offsets.astype(F32)[:, None] * frequency[None, :]
    cosine, sine = jnp.cos(angles), jnp.sin(angles)
    return (
        jnp.concatenate([cosine] * 4, axis=1),
        jnp.concatenate([-sine, sine, -sine, sine], axis=1),
    )


def partner(values):
    lane = lax.broadcasted_iota(jnp.int32, values.shape, 1)
    return jnp.where(
        lane % HD < HD // 2, pltpu.roll(values, 96, 1), pltpu.roll(values, 32, 1)
    )


def reorder(source):
    count = source.shape[1]
    rows = lax.broadcasted_iota(jnp.int32, (count, count), 0)
    return jnp.where(rows == source, 1.0, 0.0).astype(BF16)


def unit_rows(values):
    centered = values - jnp.mean(values, axis=-1, keepdims=True)
    scaling = lax.rsqrt(jnp.mean(centered * centered, axis=-1, keepdims=True) + EPS_NORM)
    return centered * scaling, scaling


def norm_back(grad_rows, units, scaling, gain_row):
    along = grad_rows * gain_row
    back_rows = scaling * (
        along
        - jnp.mean(along, axis=-1, keepdims=True)
        - units * jnp.mean(along * units, axis=-1, keepdims=True)
    )
    return (
        back_rows,
        jnp.sum(grad_rows * units, axis=0, keepdims=True),
        jnp.sum(grad_rows, axis=0, keepdims=True),
    )


def whole_spec():
    return pl.BlockSpec(memory_space=pltpu.VMEM)


def params(mib=60):
    return pltpu.CompilerParams(vmem_limit_bytes=mib * MIB)


def pack_kernel(*refs):
    *weight_refs, out_ref = refs
    rows, width = weight_refs[2].shape
    to = 0
    for ref in weight_refs:
        count = ref.shape[0]
        for at in range(0, ref.shape[1], width):
            out_ref[to : to + count, :] = ref[:, at : at + width]
            to += count


def pack_own(*weights):
    rows, width = weights[2].shape
    if rows % 16:
        parts = [
            w[:, at : at + width] for w in weights[:-1] for at in range(0, w.shape[1], width)
        ]
        return jnp.concatenate(parts + [weights[-1]], axis=0)
    total = sum(w.size for w in weights) // width
    full = lambda *dims: pl.BlockSpec(dims, lambda i: (0,) * len(dims))
    return pl.pallas_call(
        pack_kernel,
        grid=(1,),
        in_specs=[full(*w.shape) for w in weights],
        out_specs=full(total, width),
        out_shape=jax.ShapeDtypeStruct((total, width), BF16),
        compiler_params=params(),
    )(*weights)


def attend_kernel(
    rows_ref, wqkv_ref, wout_ref, cos_ref, sin_ref, mark_ref, markt_ref, vec_ref,
    q_ref, k_ref, v_ref, att_ref, low_ref, unit_ref, scale_ref, bias_ref,
):
    rows = rows_ref[...]
    tokens, width = rows.shape
    pair = 2 * HD
    cosine, sine = cos_ref[...], sin_ref[...]
    bias_ref[...] = jnp.where(mark_ref[...] == markt_ref[...], 0.0, MASKED)
    for part, out_ref in enumerate((q_ref, k_ref, v_ref)):
        mixed = joined(rows, wqkv_ref[:, part].reshape(width, width), 1, 0)
        if part == 2:
            out_ref[...] = mixed.astype(BF16)
        else:
            for at in range(0, width, pair):
                piece = mixed[:, at : at + pair]
                turned = piece * cosine + partner(piece) * sine
                out_ref[:, at : at + pair] = turned.astype(BF16)
    first_half = lax.broadcasted_iota(jnp.int32, (tokens, pair), 1) < HD
    for at in range(0, width, pair):
        query = q_ref[:, at : at + pair]
        key = k_ref[:, at : at + pair]
        value = v_ref[:, at : at + pair]
        outs = []
        for half in range(2):
            inside = first_half if half == 0 else jnp.logical_not(first_half)
            only = jnp.where(inside, query, jnp.zeros_like(query))
            scores = joined(only, key, 1, 1) * HD**-0.5 + bias_ref[...]
            raised = jnp.exp(scores - jnp.max(scores, axis=-1, keepdims=True))
            total = jnp.sum(raised, axis=-1, keepdims=True)
            weights = (raised * (1.0 / total)).astype(BF16)
            outs.append(joined(weights, value, 1, 0))
        att_ref[:, at : at + pair] = jnp.where(first_half, outs[0], outs[1]).astype(BF16)
    hidden = rows.astype(F32) + joined(att_ref[...], wout_ref[:, 0].reshape(width, width), 1, 0)
    units, scaling = unit_rows(hidden)
    unit_ref[...] = units
    scale_ref[...] = scaling
    low_ref[...] = (units * vec_ref[0:1, :] + vec_ref[1:2, :]).astype(BF16)


def attend(rows, pack, cosine, sine, labels, vectors):
    tokens, width = rows.shape
    lead, _, per, _ = pack.shape
    shape = jax.ShapeDtypeStruct
    full = lambda *dims: pl.BlockSpec(dims, lambda i: (0,) * len(dims))
    mark = labels.astype(F32)
    return pl.pallas_call(
        attend_kernel,
        grid=(1,),
        in_specs=[
            full(tokens, width),
            pl.BlockSpec((lead, 3, per, width), lambda i: (0, 3, 0, 0)),
            pl.BlockSpec((lead, 1, per, width), lambda i: (0, 8, 0, 0)),
            full(tokens, 2 * HD),
            full(tokens, 2 * HD),
            full(tokens, 1),
            full(1, tokens),
            full(4, width),
        ],
        out_specs=[full(tokens, width)] * 6 + [full(tokens, 1)],
        out_shape=[shape((tokens, width), BF16)] * 5
        + [shape((tokens, width), F32), shape((tokens, 1), F32)],
        scratch_shapes=[pltpu.VMEM((tokens, tokens), F32)],
        compiler_params=params(),
        cost_estimate=LONG,
    )(rows, pack, pack, cosine, sine, mark[:, None], mark[None, :], vectors)


def feed_kernel(
    low_ref, unit1_ref, wgate_ref, wup_ref, wdown_ref, vec_ref, pool_ref,
    act_ref, togate_ref, toup_ref, unit_ref, scale_ref, pooled_ref, emb_ref, acc_ref,
):
    step = pl.program_id(0)
    tokens, width = low_ref.shape
    low = low_ref[...]
    gate = joined(low, wgate_ref[:, 0].reshape(width, width), 1, 0)
    up = joined(low, wup_ref[:, 0].reshape(width, width), 1, 0)
    sig = 1.0 / (1.0 + jnp.exp(-gate))
    silu = gate * sig
    active = (silu * up).astype(BF16)
    act_ref[...] = active
    toup_ref[...] = silu.astype(BF16)
    togate_ref[...] = (up * sig * (1.0 + gate * (1.0 - sig))).astype(BF16)
    product = joined(active, wdown_ref[...].reshape(width, width), 1, 0)

    @pl.when(step == 0)
    def _():
        acc_ref[...] = unit1_ref[...] * vec_ref[0:1, :] + vec_ref[1:2, :] + product

    @pl.when(step > 0)
    def _():
        acc_ref[...] += product

    @pl.when(step == pl.num_programs(0) - 1)
    def _():
        units, scaling = unit_rows(acc_ref[...])
        unit_ref[...] = units
        scale_ref[...] = scaling
        second = units * vec_ref[2:3, :] + vec_ref[3:4, :]
        rows = [
            jnp.sum(second * pool_ref[:, s : s + 1], axis=0, keepdims=True)
            for s in range(pool_ref.shape[1])
        ]
        pooled = jnp.concatenate(rows, axis=0)
        pooled_ref[...] = pooled
        emb_ref[...] = pooled * lax.rsqrt(
            jnp.sum(pooled * pooled, axis=-1, keepdims=True) + EPS_UNIT
        )


def feed(low, units, pack, vectors, pool_t):
    tokens, width = low.shape
    lead, _, per, _ = pack.shape
    blocks = 4
    seqs = pool_t.shape[1]
    shape = jax.ShapeDtypeStruct
    full = lambda *dims: pl.BlockSpec(dims, lambda i: (0,) * len(dims))
    column = pl.BlockSpec((tokens, width), lambda i: (0, i))
    return pl.pallas_call(
        feed_kernel,
        grid=(blocks,),
        in_specs=[
            full(tokens, width),
            full(tokens, width),
            pl.BlockSpec((lead, 1, per, width), lambda i: (0, i, 0, 0)),
            pl.BlockSpec((lead, 1, per, width), lambda i: (0, blocks + i, 0, 0)),
            down_spec(pack),
            full(4, width),
            full(tokens, seqs),
        ],
        out_specs=[column] * 3
        + [full(tokens, width), full(tokens, 1), full(seqs, width), full(seqs, width)],
        out_shape=[shape((tokens, blocks * width), BF16)] * 3
        + [
            shape((tokens, width), F32),
            shape((tokens, 1), F32),
            shape((seqs, width), F32),
            shape((seqs, width), F32),
        ],
        scratch_shapes=[pltpu.VMEM((tokens, width), F32)],
        compiler_params=params(),
        cost_estimate=LONG,
    )(low, units, pack, pack, pack, vectors, pool_t)


def down_spec(pack, first=0):
    lead, chunks, per, width = pack.shape
    if lead == 1:
        return pl.BlockSpec((1, 1, per, width), lambda i, *p: (0, chunks - 4 + first + i, 0, 0))
    return pl.BlockSpec((lead // 4, 4, per, width), lambda i, *p: (first + i, 3, 0, 0))


def halves_kernel(rows_ref, att_ref, low_ref, act_ref, source_ref, source_down_ref,
                  keep_ref, send_ref, act_keep_ref, act_send_ref):
    step = pl.program_id(0)
    half = rows_ref.shape[1] // 2
    moved = joined(act_ref[...], reorder(source_down_ref[...]), 1, 0).astype(BF16)
    act_keep_ref[0] = moved[:, :half]
    act_send_ref[0] = moved[:, half:]
    for part, ref in enumerate((rows_ref, att_ref, low_ref)):

        @pl.when(step == part)
        def _(ref=ref):
            moved = joined(ref[...], reorder(source_ref[...]), 1, 0).astype(BF16)
            keep_ref[0] = moved[:, :half]
            send_ref[0] = moved[:, half:]


def halves(rows, attended, low, active, source, source_down):
    tokens, width = rows.shape
    blocks = active.shape[1] // width
    full = lambda *dims: pl.BlockSpec(dims, lambda i: (0,) * len(dims))
    three = pl.BlockSpec((1, tokens, width // 2), lambda i: (jnp.minimum(i, 2), 0, 0))
    four = pl.BlockSpec((1, tokens, width // 2), lambda i: (i, 0, 0))
    shape = jax.ShapeDtypeStruct
    return pl.pallas_call(
        halves_kernel,
        grid=(blocks,),
        in_specs=[full(tokens, width)] * 3
        + [pl.BlockSpec((tokens, width), lambda i: (0, i)), full(1, width), full(1, width)],
        out_specs=[three, three, four, four],
        out_shape=[shape((3, tokens, width // 2), BF16)] * 2
        + [shape((blocks, tokens, width // 2), BF16)] * 2,
        compiler_params=params(),
        cost_estimate=LONG,
    )(rows, attended, low, active, source, source_down)


def lse(values, axis):
    top = jnp.max(values, axis=axis, keepdims=True)
    return top + jnp.log(jnp.sum(jnp.exp(values - top), axis=axis, keepdims=True))


def loss_kernel(
    every_ref, match_ref, own_match_ref, tower_ref, emb_ref, pooled_ref, pool_ref, unit_ref,
    scale_ref, vec_ref, *refs,
):
    loss_ref, mid_ref, low_ref, sums_ref = refs[-4:]
    total = every_ref.shape[0] // 2
    queries = every_ref[0:total, :]
    documents = every_ref[total : 2 * total, :]
    similar = joined_high(queries, documents, 1, 1) / TEMPER
    flipped = joined_high(documents, queries, 1, 1) / TEMPER
    row_log = lse(similar, 1)
    loss = (
        0.5 * (jnp.sum(row_log, keepdims=True) + jnp.sum(lse(similar, 0), keepdims=True))
        - jnp.sum(similar * match_ref[...], keepdims=True)
    ) / total
    loss_ref[...] = loss
    first = tower_ref[...] == 0
    others = jnp.where(first, documents, queries)
    other_log = jnp.where(first, lse(similar, 0), lse(flipped, 0))
    own = joined_high(emb_ref[...], others, 1, 1) / TEMPER
    grad_similar = (
        0.5 * (jnp.exp(own - lse(own, 1)) + jnp.exp(own - other_log)) - own_match_ref[...]
    ) / total
    grad_unit = joined_high(grad_similar, others, 1, 0) / TEMPER
    pooled = pooled_ref[...]
    inverse = lax.rsqrt(jnp.sum(pooled * pooled, axis=-1, keepdims=True) + EPS_UNIT)
    along = jnp.sum(pooled * grad_unit, axis=-1, keepdims=True)
    grad_pooled = inverse * grad_unit - inverse * inverse * inverse * pooled * along
    grad_second = sum(
        pool_ref[:, s : s + 1] * grad_pooled[s : s + 1, :] for s in range(grad_pooled.shape[0])
    )
    mid, gain, bias = norm_back(grad_second, unit_ref[...], scale_ref[...], vec_ref[2:3, :])
    mid_ref[...] = mid
    low_ref[...] = mid.astype(BF16)
    sums_ref[0:1, :] = gain
    sums_ref[1:2, :] = bias


def loss_and_grad(
    everyone, pos_doc, tower_index, dp_index, emb, pooled, pool_t, units, scaling, vectors, after
):
    tokens = units.shape[0]
    total = everyone.shape[0] // 2
    seqs, width = emb.shape
    match = (pos_doc[:, None] == jnp.arange(total, dtype=jnp.int32)[None, :]).astype(F32)
    oriented = jnp.where(tower_index == 0, match, match.T)
    own_match = lax.dynamic_slice_in_dim(oriented, dp_index * seqs, seqs, 0)
    shape = jax.ShapeDtypeStruct
    return pl.pallas_call(
        loss_kernel,
        in_specs=[whole_spec()] * 10 + [pl.BlockSpec(memory_space=pl.ANY)] * len(after),
        out_specs=[whole_spec()] * 4,
        out_shape=[shape((1, 1), F32), shape((tokens, width), F32), shape((tokens, width), BF16),
                   shape((2, width), F32)],
        compiler_params=params(30),
        cost_estimate=LONG,
    )(everyone, match, own_match, tower_index.reshape(1, 1), emb, pooled, pool_t, units, scaling,
      vectors, *after)


def gates_kernel(fast, branch_ref, mid_ref, act1_ref, act2_ref, unit_ref, scale_ref, vec_ref,
                 two_ref, source_ref, wgate_ref, wup_ref, wdown_ref,
                 grads_ref, hid_ref, attn_ref, sums_ref, *refs):
    acc_ref = refs[-1]
    step = pl.program_id(0)
    tokens, width = mid_ref.shape
    grad_active = joined(branch_ref[...], wdown_ref[...].reshape(width, width), 1, 1)
    grad_gate = (grad_active * act1_ref[...].astype(F32)).astype(BF16)
    grad_up = (grad_active * act2_ref[...].astype(F32)).astype(BF16)
    grads_ref[0, 0] = grad_gate
    grads_ref[1, 0] = grad_up
    back = joined(grad_gate, wgate_ref[:, 0].reshape(width, width), 1, 1) + joined(
        grad_up, wup_ref[:, 0].reshape(width, width), 1, 1
    )

    @pl.when(step == 0)
    def _():
        acc_ref[...] = mid_ref[...] + back

    @pl.when(step > 0)
    def _():
        acc_ref[...] += back

    @pl.when(step == pl.num_programs(0) - 1)
    def _():
        grad_hidden, gain, bias = norm_back(
            acc_ref[...], unit_ref[...], scale_ref[...], vec_ref[0:1, :]
        )
        hid_ref[...] = grad_hidden
        attn_ref[0:tokens, :] = grad_hidden.astype(BF16)
        if fast:
            values = jnp.concatenate([gain, bias, two_ref[...]], axis=0)
            upper = values.astype(BF16).astype(F32)
            blank = jnp.zeros((8, width), F32)
            parts = jnp.concatenate([upper, values - upper, blank], axis=0).astype(BF16)
            moved = joined(parts, reorder(source_ref[...]), 1, 0).astype(BF16)
            attn_ref[tokens:, :] = moved
        else:
            sums_ref[0:1, :] = gain
            sums_ref[1:2, :] = bias


def gates_back(fast, source, branch, mid, to_gate, to_up, units, scaling, vectors, sums_two, pack):
    tokens, width = mid.shape
    lead, _, per, _ = pack.shape
    blocks = 4
    shape = jax.ShapeDtypeStruct
    full = lambda *dims: pl.BlockSpec(dims, lambda i: (0,) * len(dims))
    flat = full(tokens, width)
    column = pl.BlockSpec((tokens, width), lambda i: (0, i))
    rows = tokens + (16 if fast else 0)
    return pl.pallas_call(
        lambda *refs: gates_kernel(fast, *refs),
        grid=(blocks,),
        in_specs=[flat, flat, column, column, flat, full(tokens, 1), full(4, width),
                  full(2, width), full(1, width),
                  pl.BlockSpec((lead, 1, per, width), lambda i: (0, i, 0, 0)),
                  pl.BlockSpec((lead, 1, per, width), lambda i: (0, 4 + i, 0, 0)),
                  down_spec(pack)],
        out_specs=[pl.BlockSpec((2, 1, tokens, width), lambda i: (0, i, 0, 0)), flat,
                   full(rows, width), full(2, width)],
        out_shape=[shape((2, blocks, tokens, width), BF16), shape((tokens, width), F32),
                   shape((rows, width), BF16), shape((2, width), F32)],
        scratch_shapes=[pltpu.VMEM((tokens, width), F32)],
        compiler_params=params(30),
        cost_estimate=LONG,
    )(branch, mid, to_gate, to_up, units, scaling, vectors, sums_two, source, pack, pack, pack)


def attend_back_kernel(
    wout_ref, cos_ref, sin_ref, mark_ref, markt_ref, q_ref, k_ref, v_ref, grad_ref, *refs
):
    mixed_ref, bias_ref, gatt_ref = refs[-3:]
    tokens, width = q_ref.shape
    pair = 2 * HD
    cosine, sine = cos_ref[...], sin_ref[...]
    bias_ref[...] = jnp.where(mark_ref[...] == markt_ref[...], 0.0, MASKED)
    gatt_ref[...] = joined(grad_ref[...], wout_ref[:, 0].reshape(width, width), 1, 1).astype(BF16)
    first_half = lax.broadcasted_iota(jnp.int32, (tokens, pair), 1) < HD
    for at in range(0, width, pair):
        query = q_ref[:, at : at + pair]
        key = k_ref[:, at : at + pair]
        value = v_ref[:, at : at + pair]
        grad_out = gatt_ref[:, at : at + pair]
        found = []
        for half in range(2):
            inside = first_half if half == 0 else jnp.logical_not(first_half)
            scores = (
                joined(jnp.where(inside, key, jnp.zeros_like(key)), query, 1, 1) * HD**-0.5
                + bias_ref[...]
            )
            raised = jnp.exp(scores - jnp.max(scores, axis=0, keepdims=True))
            probs = raised * (1.0 / jnp.sum(raised, axis=0, keepdims=True))
            grad_probs = joined(
                jnp.where(inside, value, jnp.zeros_like(value)), grad_out, 1, 1
            )
            delta = jnp.sum(probs * grad_probs, axis=0, keepdims=True)
            grad_scores = (probs * (grad_probs - delta)).astype(BF16)
            found.append(
                (
                    joined(grad_scores, key, 0, 0),
                    joined(grad_scores, query, 1, 0),
                    joined(probs.astype(BF16), grad_out, 1, 0),
                )
            )
        grad_query = jnp.where(first_half, found[0][0], found[1][0]) * HD**-0.5
        grad_key = jnp.where(first_half, found[0][1], found[1][1]) * HD**-0.5
        grad_value = jnp.where(first_half, found[0][2], found[1][2])
        mixed_ref[0, :, at : at + pair] = (
            grad_query * cosine - partner(grad_query) * sine
        ).astype(BF16)
        mixed_ref[1, :, at : at + pair] = (
            grad_key * cosine - partner(grad_key) * sine
        ).astype(BF16)
        mixed_ref[2, :, at : at + pair] = grad_value.astype(BF16)


def attend_back(pack, cosine, sine, labels, query, key, value, grad, after=()):
    tokens, width = query.shape
    lead, _, per, _ = pack.shape
    full = lambda *dims: pl.BlockSpec(dims, lambda i: (0,) * len(dims))
    flat = full(tokens, width)
    mark = labels.astype(F32)
    return pl.pallas_call(
        attend_back_kernel,
        grid=(1,),
        in_specs=[pl.BlockSpec((lead, 1, per, width), lambda i: (0, 8, 0, 0)),
                  full(tokens, 2 * HD), full(tokens, 2 * HD), full(tokens, 1), full(1, tokens)]
        + [flat] * 4 + [pl.BlockSpec(memory_space=pl.ANY)] * len(after),
        out_specs=full(3, tokens, width),
        out_shape=jax.ShapeDtypeStruct((3, tokens, width), BF16),
        scratch_shapes=[pltpu.VMEM((tokens, tokens), F32), pltpu.VMEM((tokens, width), BF16)],
        compiler_params=params(30),
        cost_estimate=LONG,
    )(pack, cosine, sine, mark[:, None], mark[None, :], query, key, value, grad, *after)


def tokens_kernel(mixed_ref, hid_ref, wqkv_ref, *refs):
    tokens, width = hid_ref.shape
    back = hid_ref[...]
    for part in range(3):
        back += joined(mixed_ref[part], wqkv_ref[:, part].reshape(width, width), 1, 1)
    refs[-1][...] = back


def tokens_back(mixed, hidden, pack, after=()):
    tokens, width = hidden.shape
    lead, _, per, _ = pack.shape
    full = lambda *dims: pl.BlockSpec(dims, lambda i: (0,) * len(dims))
    return pl.pallas_call(
        tokens_kernel,
        grid=(1,),
        in_specs=[full(3, tokens, width), full(tokens, width),
                  pl.BlockSpec((lead, 3, per, width), lambda i: (0, 3, 0, 0))]
        + [pl.BlockSpec(memory_space=pl.ANY)] * len(after),
        out_specs=full(tokens, width),
        out_shape=jax.ShapeDtypeStruct((tokens, width), F32),
        compiler_params=params(),
        cost_estimate=LONG,
    )(mixed, hidden, pack, *after)


def both(own_left, got_left, own_right, got_right):
    return (joined(own_left, own_right, 0, 0) + joined(got_left, got_right, 0, 0)).astype(BF16)


def steps_call(kernel, grid, ins, args, outs, shapes, scalars=None, after=()):
    ins = ins + [pl.BlockSpec(memory_space=pl.ANY)] * len(after)
    shapes = [jax.ShapeDtypeStruct(dims, BF16) for dims in shapes]
    more = dict(out_shape=shapes, compiler_params=params(30), cost_estimate=LONG)
    if scalars is None:
        return pl.pallas_call(
            kernel, grid=grid, in_specs=ins, out_specs=outs, **more
        )(*args, *after)
    return pl.pallas_call(
        kernel,
        grid_spec=pltpu.PrefetchScalarGridSpec(
            num_scalar_prefetch=1, grid=grid, in_specs=ins, out_specs=outs
        ),
        **more,
    )(scalars, *args, *after)


def down_kernel(own_ref, got_ref, grad_ref, got_grad_ref, *refs):
    held_ref, moving_ref = refs[-2:]
    value = both(own_ref[0], got_ref[0], grad_ref[...], got_grad_ref[...])
    half = value.shape[0] // 2
    held_ref[0] = value[:half]
    moving_ref[0] = value[half:]


def down_grads(own, got, grad, got_grad, after=()):
    blocks, tokens, rows = own.shape
    width = grad.shape[1]
    left = pl.BlockSpec((1, tokens, rows), lambda i: (i, 0, 0))
    right = pl.BlockSpec((tokens, width), lambda i: (0, 0))
    out = pl.BlockSpec((1, rows // 2, width), lambda i: (i, 0, 0))
    dims = (blocks, rows // 2, width)
    return steps_call(
        down_kernel, (blocks,), [left, left, right, right], (own, got, grad, got_grad),
        [out, out], [dims, dims], after=after,
    )


def first_kernel(own_ref, got_ref, grad_ref, got_grad_ref, *refs):
    held_ref, moving_ref = refs[-2:]
    value = both(own_ref[0], got_ref[0], grad_ref[0, 0], got_grad_ref[0, 0])
    half = value.shape[0] // 2
    held_ref[...] = value[:half].reshape(held_ref.shape)
    moving_ref[...] = value[half:].reshape(held_ref.shape)


def first_grads(own, got, grads, got_grads, which, part, after=()):
    _, tokens, rows = own.shape
    _, chunks, _, width = grads.shape
    left = pl.BlockSpec((1, tokens, rows), lambda i: (part, 0, 0))
    right = pl.BlockSpec((1, 1, tokens, width), lambda i: (which, i, 0, 0))
    out = pl.BlockSpec((4, 1, rows // 8, width), lambda i: (0, i, 0, 0))
    dims = (4, chunks, rows // 8, width)
    return steps_call(
        first_kernel, (chunks,), [left, left, right, right], (own, got, grads, got_grads),
        [out, out], [dims, dims], after=after,
    )


def tower_kernel(tower_ref, own_ref, got_ref, grad_ref, got_grad_ref, *refs):
    held_ref, lent_ref = refs[-2:]
    value = both(own_ref[0], got_ref[0], grad_ref[0, 0], got_grad_ref[0, 0])
    value = value.reshape(held_ref.shape)
    here = pl.program_id(0) < pl.num_programs(0) // 2

    @pl.when(here)
    def _():
        held_ref[...] = value

    @pl.when(jnp.logical_not(here))
    def _():
        lent_ref[...] = value


def tower_grads(tower, own, got, grads, got_grads, which, chunks, first, part, after=()):
    _, tokens, rows = own.shape
    width = grads.shape[-1]
    half = chunks // 2
    left = pl.BlockSpec((1, tokens, rows), lambda i, t: (part, 0, 0))
    right = pl.BlockSpec(
        (1, 1, tokens, width), lambda i, t: (which, first + (i + half * t[0]) % chunks, 0, 0)
    )
    block = (2, 4, 1, rows // 8, width)
    dims = (2, 4, half, rows // 8, width)
    outs = [
        pl.BlockSpec(block, lambda i, t: (0, 0, jnp.minimum(i, half - 1), 0, 0)),
        pl.BlockSpec(block, lambda i, t: (0, 0, jnp.maximum(i - half, 0), 0, 0)),
    ]
    return steps_call(
        tower_kernel, (chunks,), [left, left, right, right], (own, got, grads, got_grads),
        outs, [dims, dims], scalars=tower, after=after,
    )


def rest_kernel(own_ref, got_ref, attn_ref, got_attn_ref, mixed_ref, got_mixed_ref, *refs):
    held_ref, moving_ref = refs[-2:]
    tokens, width = mixed_ref.shape[1:]
    half = width // 4
    pieces = [
        both(own_ref[1], got_ref[1], attn_ref[0:tokens, :], got_attn_ref[0:tokens, :]),
        both(own_ref[0], got_ref[0], mixed_ref[0], got_mixed_ref[0]),
    ]
    parts = attn_ref[tokens:, : width // 2].astype(F32)
    got = got_attn_ref[tokens:, width // 2 :].astype(F32)
    values = parts[0:4] + parts[4:8] + got[0:4] + got[4:8]
    upper = values.astype(BF16).astype(F32)
    blank = jnp.zeros((PAD - 2 * VECTORS, width // 2), F32)
    pieces.append(jnp.concatenate([upper, values - upper, blank], axis=0).T.astype(BF16))
    at = 0
    for piece in pieces:
        columns = piece.shape[1]
        for k, out_ref in enumerate((held_ref, moving_ref)):
            out_ref[:, :, at : at + columns] = piece[k * 2 * half // 2 : (k + 1) * half].reshape(
                4, -1, columns
            )
        at += columns


def rest_grads(own, got, attn, got_attn, mixed, got_mixed, after=()):
    _, tokens, rows = own.shape
    width = mixed.shape[2]
    full = lambda *dims: pl.BlockSpec(dims, lambda i: (0,) * len(dims))
    one = pl.BlockSpec((1, tokens, width), lambda i: (0, 0, 0))
    dims = (4, rows // 8, 2 * width + PAD)
    return steps_call(
        rest_kernel, (1,),
        [full(*own.shape), full(*own.shape), full(*attn.shape), full(*attn.shape), one, one],
        (own, got, attn, got_attn, mixed, got_mixed),
        [full(*dims)] * 2, [dims, dims], after=after,
    )


def reduce_digit(parts, sizes, place, digit):
    size = sizes[place]
    total = pick(parts, 0, digit).astype(F32)
    for shift in range(1, size):
        sent = pick(parts, 0, (digit + shift) % size).astype(BF16)
        total += lax.ppermute(sent, "dp", digit_shift(sizes, place, shift)).astype(F32)
    return total


def shared_sum(grad, sizes, digits, tower_index):
    rows, columns = grad.shape
    count = math.prod(sizes)
    per = rows // count
    tiles = columns // 128
    side = max(1, round(tiles * 0.3)) * 128
    middle = columns - 2 * side
    last = len(sizes) - 1
    blocks = grad.astype(BF16).reshape(count // sizes[last], sizes[last], per, columns)
    chip = reduce_digit(jnp.moveaxis(blocks, 1, 0), sizes, last, digits[last]).astype(BF16)
    lead = chip.shape[0]
    mine = lax.dynamic_slice(chip, (0, 0, tower_index * (columns - side)), (lead, per, side))
    other = lax.dynamic_slice(
        chip, (0, 0, (1 - tower_index) * (columns - side)), (lead, per, side)
    )
    mine = mine.astype(F32) + lax.ppermute(other, "tower", SWAP).astype(F32)
    part = jnp.concatenate([mine.astype(BF16), chip[:, :, side : side + middle]], axis=2)
    for place in range(last - 1, -1, -1):
        size = sizes[place]
        part = jnp.moveaxis(part.reshape(part.shape[0] // size, size, per, side + middle), 1, 0)
        part = reduce_digit(part, sizes, place, digits[place]).astype(BF16)
    part = part[0]
    back = lax.ppermute(part, "tower", SWAP).astype(F32)
    part = part.astype(F32)
    centre = part[:, side:] + back[:, side:]
    first = tower_index == 0
    return jnp.concatenate(
        [
            jnp.where(first, part[:, :side], back[:, :side]),
            centre,
            jnp.where(first, back[:, :side], part[:, :side]),
        ],
        axis=1,
    )


def plus_kernel(jobs, count, z_ref, *refs):
    for out_ref, (terms, vectors) in zip(refs[count:], jobs, strict=True):
        total = None
        for place, index in terms:
            piece = refs[place][index(z_ref[0]) if callable(index) else index].astype(F32)
            total = piece if total is None else total + piece
        total = total.reshape(out_ref.shape)
        if vectors:
            at = total.shape[-1] - PAD
            parts = total[..., at:].reshape(-1, PAD)
            lane = lax.broadcasted_iota(jnp.int32, parts.shape, 1)
            values = parts + pltpu.roll(parts, PAD - VECTORS, 1)
            upper = values.astype(BF16).astype(F32)
            lower = pltpu.roll(values - upper, VECTORS, 1)
            parts = jnp.where(lane < VECTORS, upper, jnp.where(lane < 2 * VECTORS, lower, 0.0))
            out_ref[..., :at] = total[..., :at].astype(BF16)
            out_ref[..., at:] = parts.astype(BF16).reshape(*out_ref.shape[:-1], PAD)
        else:
            out_ref[...] = total.astype(BF16)


def plus(jobs, z, after=()):
    inputs, outs, shapes = [], [], []
    for arrays, plan, dims, vectors in jobs:
        base = len(inputs)
        inputs += arrays
        outs += [([(base + place, index) for place, index in terms], vectors) for terms in plan]
        shapes += dims
    count = len(inputs)
    spec = lambda dims: pl.BlockSpec(dims, lambda i: (0,) * len(dims))
    return pl.pallas_call(
        lambda *refs: plus_kernel(
            outs, count, *refs[: 1 + count], *refs[1 + count + len(after) :]
        ),
        grid=(1,),
        in_specs=[pl.BlockSpec(memory_space=pltpu.SMEM)]
        + [spec(a.shape) for a in inputs]
        + [pl.BlockSpec(memory_space=pl.ANY)] * len(after),
        out_specs=[spec(dims) for dims in shapes],
        out_shape=[jax.ShapeDtypeStruct(dims, BF16) for dims in shapes],
        compiler_params=params(24),
        cost_estimate=SHORT,
    )(z, *inputs, *after)


class GradSum:
    def __init__(self, pair, sizes, z, by_tower, direct, vectors=False):
        self.sizes = sizes
        self.z = z
        self.direct = direct
        self.vectors = vectors
        self.by_tower = by_tower
        self.held, sent = pair
        self.got = lax.ppermute(sent, "tower", SWAP) if by_tower else self.shift_y(sent)
        self.steps = ["tower", "y", "z"] if by_tower else ["y", "z"]

    def shift_y(self, sent):
        return lax.ppermute(sent, "dp", digit_shift(self.sizes, 1, 1))

    def job(self):
        step = self.steps[0]
        if step == "tower":
            plan = [[(0, (k,)), (1, (k,))] for k in (1, 0)]
            return [self.held, self.got], plan, [self.held.shape[1:]] * 2, self.vectors
        depth = self.sizes[0]
        if step == "y" and self.direct:
            views = [lambda z, k=k: ((z + k) % depth,) for k in (1, 2, 3, 0)]
            plan = [[(0, view), (1, view)] for view in views]
            return [self.held, self.got], plan, [self.held.shape[1:]] * depth, self.vectors
        if step == "y":
            plan = [[(0, (Ellipsis,)), (1, (Ellipsis,))]]
            return [self.held, self.got], plan, [self.held.shape], self.vectors
        if self.direct:
            plan = [[(k, (Ellipsis,)) for k in range(depth)]]
            return [self.held, *self.got], plan, [self.held.shape], self.vectors
        plan = [[(0, (k,)) for k in range(depth)]]
        return [self.got], plan, [self.got.shape[1:]], self.vectors

    def take(self, outs):
        step = self.steps.pop(0)
        if step == "tower":
            moving, self.held = outs
            self.got = self.shift_y(moving)
        elif step == "y" and self.direct:
            *parts, self.held = outs
            self.got = [
                lax.ppermute(part, "dp", digit_shift(self.sizes, 0, k + 1))
                for k, part in enumerate(parts)
            ]
        elif step == "y":
            depth, rest = self.sizes[0], math.prod(self.sizes[1:])
            groups = [[z * rest + other for z in range(depth)] for other in range(rest)]
            self.got = lax.all_to_all(outs[0], "dp", 0, 0, axis_index_groups=groups, tiled=True)
        else:
            (self.held,) = outs
            self.got = lax.ppermute(self.held, "tower", SWAP)

    def result(self, tower_index):
        first = tower_index == 0
        return jnp.where(first, self.held, self.got), jnp.where(first, self.got, self.held)


def advance(order, *sums, done=()):
    jobs = [one.job() for one in sums]
    outs = plus(jobs, sums[0].z, (order, *(one.got for one in done)))
    last = outs[-1]
    for one, (_, plan, _, _) in zip(sums, jobs, strict=True):
        one.take(outs[: len(plan)])
        outs = outs[len(plan) :]
    return last


def sum_norms(sums_one, sums_two, dp_count):
    sums = jnp.concatenate([sums_one, sums_two], axis=0)
    sums = sums.reshape(4, dp_count, -1).transpose(1, 0, 2)
    sums = jnp.concatenate([sums, sums], axis=0)
    return jnp.sum(lax.all_to_all(sums, ("tower", "dp"), 0, 0, tiled=True), axis=0)


def finish_kernel(plan, count, *refs):
    for out_ref, terms in zip(refs[count:], plan, strict=True):
        for to, places, index in terms:
            total = refs[places[0]][index].astype(F32)
            for place in places[1:]:
                total += refs[place][index].astype(F32)
            out_ref[to] = total


def finish(inputs, plan, shapes, after=()):
    count = len(inputs)
    spec = lambda dims: pl.BlockSpec(dims, lambda i: (0,) * len(dims))
    return pl.pallas_call(
        lambda *refs: finish_kernel(plan, count, *refs[:count], *refs[count + len(after) :]),
        grid=(1,),
        in_specs=[spec(a.shape) for a in inputs]
        + [pl.BlockSpec(memory_space=pl.ANY)] * len(after),
        out_specs=[spec(dims) for dims in shapes],
        out_shape=[jax.ShapeDtypeStruct(dims, F32) for dims in shapes],
        compiler_params=params(24),
        cost_estimate=SHORT,
    )(*inputs, *after)


def beside(chunks):
    return jnp.concatenate(list(chunks), axis=1)


def column_orders(digits, per, spread, width):
    _, y, c = digits
    place = jnp.arange(width, dtype=jnp.int32)
    block, row = place // per, place % per
    core, dy, z = block // 8, block // 4 % 2, block % 4
    source = ((z * 4 + (dy + y) % 2 * 2 + (core + c) % 2)) * per + row
    device = (dy + y) % 2 * 2 + (core + c) % 2
    return source[None], ((device * spread + block % 4) * per + row)[None]


def body(
    tokens,
    lengths,
    pos_doc,
    w_qkv,
    w_out,
    w_gate,
    w_up,
    w_down,
    ln1_gain,
    ln1_bias,
    ln2_gain,
    ln2_bias,
):
    dp_count = lax.axis_size("dp")
    device_count = 2 * dp_count
    sizes = split_dp(dp_count)
    dp_index = lax.axis_index("dp")
    tower_index = lax.axis_index("tower")
    digits = digits_of(dp_index, sizes)
    per, narrow = w_out.shape
    wide = w_gate.shape[1]
    spread = wide // narrow

    own_pack = pack_own(w_gate, w_up, w_out, w_qkv, w_down)
    pack = lax.all_gather(own_pack, "dp", axis=0, tiled=True)
    pack = pack.reshape(dp_count, 4 * spread, per, narrow)
    if per % 16:
        front = pack[:, : 3 * spread].transpose(1, 0, 2, 3).reshape(3 * spread, narrow, narrow)
        back = pack[:, 3 * spread :].reshape(spread, narrow, narrow)
        pack = jnp.concatenate([front, back], axis=0)[None]
    vectors_own = jnp.stack([ln1_gain, ln1_bias, ln2_gain, ln2_bias])
    vectors = lax.all_to_all(
        jnp.broadcast_to(vectors_own[None], (dp_count, 4, per)), "dp", 0, 0, tiled=True
    )
    vectors = vectors.transpose(1, 0, 2).reshape(4, narrow).astype(F32)

    rows_in = tokens[0]
    row_count = rows_in.shape[0]
    pooling, labels, offsets = layout(lengths[0], row_count)
    pool_t = pooling.T
    cosine, sine = rotary_tables(offsets)

    fast = sizes == [4, 2, 2] and spread == 4 and per % 16 == 0
    source, source_down = column_orders(digits, per, spread, narrow) if fast else (
        jnp.zeros((1, narrow), jnp.int32),
    ) * 2
    core_swap = digit_shift(sizes, len(sizes) - 1, 1)
    swap_cores = lambda values: lax.ppermute(values, "dp", core_swap)
    query, key, value, attended, first_low, unit_one, scale_one = attend(
        rows_in, pack, cosine, sine, labels, vectors
    )
    active, to_gate, to_up, unit_two, scale_two, pooled, unit_vectors = feed(
        first_low, unit_one, pack, vectors, pool_t
    )
    seq_count = unit_vectors.shape[0]
    everyone = lax.all_to_all(
        jnp.broadcast_to(unit_vectors[None], (device_count,) + unit_vectors.shape),
        ("tower", "dp"),
        0,
        0,
        tiled=True,
    ).reshape(device_count * seq_count, narrow)
    if fast:
        own, lent, own_active, lent_active = halves(
            rows_in, attended, first_low, active, source, source_down
        )
    loss_value, grad_mid, grad_branch, sums_two = loss_and_grad(
        everyone, pos_doc, tower_index, dp_index, unit_vectors, pooled, pool_t, unit_two, scale_two,
        vectors, (own,) if fast else (),
    )
    grad_feed, grad_hidden, grad_attn, sums_one = gates_back(
        fast, source, grad_branch, grad_mid, to_gate, to_up, unit_one, scale_one, vectors, sums_two,
        pack,
    )
    heads_args = (pack, cosine, sine, labels, query, key, value, grad_attn)
    if fast:
        got, got_active = swap_cores(lent), swap_cores(lent_active)
        got_branch = swap_cores(grad_branch)
        got_feed = swap_cores(grad_feed)
        got_attn = swap_cores(grad_attn)
        tower = tower_index.reshape(1).astype(jnp.int32)
        summed = lambda pair, **how: GradSum(pair, sizes, digits[0].reshape(1), **how)
        down = summed(
            down_grads(own_active, got_active, grad_branch, got_branch),
            by_tower=False, direct=False,
        )
        grad_mixed = attend_back(*heads_args, (down.held, got_attn))
        got_mixed = swap_cores(grad_mixed)
        gate = summed(
            tower_grads(
                tower, own, got, grad_feed, got_feed, 0, 4, 0, 2, (grad_mixed,)
            ),
            by_tower=True, direct=True,
        )
        up = summed(
            first_grads(own, got, grad_feed, got_feed, 1, 2, (gate.held,)),
            by_tower=False, direct=True,
        )
        order = advance(up.held, down)
        rest = summed(
            rest_grads(own, got, grad_attn, got_attn, grad_mixed, got_mixed, (order,)),
            by_tower=False, direct=False, vectors=True,
        )
        last = summed(
            tower_grads(
                tower, own, got, grad_mixed[None], got_mixed[None], 0, 2, 1, 0, (rest.held,)
            ),
            by_tower=True, direct=True,
        )
        order = advance(last.held, gate)
        grad_rows = tokens_back(grad_mixed, grad_hidden, pack, (order,))
        order = advance(grad_rows, up)
        order = advance(order, last)
        order = advance(order, down)
        order = advance(order, rest)
        order = advance(order, gate, done=(down,))
        order = advance(order, up)
        order = advance(order, last)
        order = advance(order, rest, done=(up,))
        columns = lambda k: (slice(None), slice(k * narrow, (k + 1) * narrow))
        sum_down, sum_up = finish(
            [down.held, down.got, up.held, up.got],
            [
                [((Ellipsis,), (0, 1), (Ellipsis,))],
                [(columns(k), (2, 3), (k,)) for k in range(spread)],
            ],
            [down.held.shape, (per, wide)],
            (order,),
        )
        order = advance(sum_up, gate, done=(rest,))
        order = advance(order, last, done=(gate,))
        lower, upper = gate.result(tower_index)
        (sum_gate,) = finish(
            [lower, upper],
            [[(columns(k), (k // 2,), (k % 2,)) for k in range(spread)]],
            [(per, wide)],
            (order,),
        )
        key_value = last.result(tower_index)
        sum_out, sum_qkv, sums = finish(
            [rest.held, rest.got, *key_value],
            [
                [((Ellipsis,), (0, 1), columns(0))],
                [(columns(0), (0, 1), columns(1)), (columns(1), (2,), (0,)), (columns(2), (3,), (0,))],
                [((Ellipsis,), (0, 1), (slice(None), slice(2 * narrow, 2 * narrow + PAD)))],
            ],
            [(per, narrow), (per, 3 * narrow), (per, PAD)],
        )
        sums = sums.T
        sums = sums[:VECTORS] + sums[VECTORS : 2 * VECTORS]
    else:
        grad_mixed = attend_back(*heads_args)
        grad_rows = tokens_back(grad_mixed, grad_hidden, pack)
        grad_down = joined(active, grad_branch, 0, 0)
        down_rows = (
            grad_down.reshape(dp_count, spread, per, narrow)
            .transpose(0, 2, 1, 3)
            .reshape(narrow, wide)
        )
        share = lambda grad: shared_sum(grad, sizes, digits, tower_index)
        sum_down = share(down_rows).reshape(per, spread, narrow).transpose(1, 0, 2)
        sum_down = sum_down.reshape(wide // dp_count, narrow)
        sum_gate, sum_up = (
            share(joined(first_low, beside(grad_feed[k]), 0, 0)) for k in range(2)
        )
        sum_out = share(joined(attended, grad_attn, 0, 0))
        sum_qkv = share(joined(rows_in, beside(grad_mixed), 0, 0))
        sums = sum_norms(sums_one, sums_two, dp_count)
    return (
        loss_value.reshape(()),
        unit_vectors[None],
        grad_rows[None],
        sum_qkv,
        sum_out,
        sum_gate,
        sum_up,
        sum_down,
        sums[0],
        sums[1],
        sums[2],
        sums[3],
    )


def solution(mesh):
    placed = (
        P("tower", "dp", None),
        P("tower", "dp"),
        P(),
        P("dp", None),
        P("dp", None),
        P("dp", None),
        P("dp", None),
        P("dp", None),
        P("dp"),
        P("dp"),
        P("dp"),
        P("dp"),
    )
    return jax.shard_map(
        body,
        mesh=mesh,
        in_specs=placed,
        out_specs=(
            P(),
            P("tower", "dp", None),
            P("tower", "dp", None),
            P("dp", None),
            P("dp", None),
            P("dp", None),
            P("dp", None),
            P("dp", None),
            P("dp"),
            P("dp"),
            P("dp"),
            P("dp"),
        ),
        check_vma=False,
    )
```

```python
import math

import jax
import jax.numpy as jnp
from jax import lax
from jax.experimental import pallas as pl
from jax.experimental.pallas import tpu as pltpu
from jax.sharding import PartitionSpec as P

HD = 64
PAD = 128
VECTORS = 4
TEMPER = 0.05
EPS_NORM = 1e-05
EPS_UNIT = 1e-06
MASKED = -1e30
F32 = jnp.float32
BF16 = jnp.bfloat16
MIB = 1 << 20
ORDER = (
    "down", "heads", "gate", "up", "d", "rest", "last", "g",
    "tokens", "u", "l", "d", "r", "g", "u", "l",
    "r", "l", "g",
)
DIRECT = "gulr"
LONG = pl.CostEstimate(flops=100000000000, bytes_accessed=100000000, transcendentals=0)
SHORT = pl.CostEstimate(flops=100000000000, bytes_accessed=100000000, transcendentals=0)


def joined(left_arr, right_arr, left_dim, right_dim):
    return lax.dot_general(
        left_arr,
        right_arr,
        (((left_dim,), (right_dim,)), ((), ())),
        preferred_element_type=F32,
    )


def joined_high(left_arr, right_arr, left_dim, right_dim):
    return lax.dot_general(
        left_arr,
        right_arr,
        (((left_dim,), (right_dim,)), ((), ())),
        precision=lax.Precision.HIGHEST,
        preferred_element_type=F32,
    )


def split_dp(count):
    sizes = [2] if count % 2 == 0 else []
    rest = count // 2 if sizes else count
    front = []
    while rest > 1:
        step = 4 if rest % 4 == 0 else (2 if rest % 2 == 0 else rest)
        front.append(step)
        rest //= step
    return front + sizes


def digit_shift(sizes, place, shift):
    stride = math.prod(sizes[place + 1 :])
    size = sizes[place]
    pairs = []
    for index in range(math.prod(sizes)):
        digit = index // stride % size
        pairs.append((index, index + ((digit + shift) % size - digit) * stride))
    return pairs


def digits_of(index, sizes):
    found = []
    for size in reversed(sizes):
        found.append(index % size)
        index = index // size
    return found[::-1]


SWAP = [(0, 1), (1, 0)]


def pick(array, axis, place):
    return lax.dynamic_index_in_dim(array, place, axis, keepdims=False)


def layout(seq_spans, row_count):
    seq_total = seq_spans.shape[0]
    starts = jnp.cumsum(seq_spans) - seq_spans
    places = jnp.arange(row_count, dtype=jnp.int32)
    member = (
        (places[None, :] >= starts[:, None]) & (places[None, :] < (starts + seq_spans)[:, None])
    ).astype(jnp.int32)
    labels = jnp.sum(member * jnp.arange(seq_total, dtype=jnp.int32)[:, None], axis=0)
    offsets = places - jnp.sum(member * starts[:, None], axis=0)
    pooling = member.astype(F32) / seq_spans.astype(F32)[:, None]
    return (pooling, labels, offsets)


def rotary_tables(offsets):
    half_size = HD // 2
    frequency = 1000.0 ** (-jnp.arange(half_size, dtype=F32) / half_size)
    angles = offsets.astype(F32)[:, None] * frequency[None, :]
    cosine, sine = jnp.cos(angles), jnp.sin(angles)
    return (
        jnp.concatenate([cosine] * 4, axis=1),
        jnp.concatenate([-sine, sine, -sine, sine], axis=1),
    )


def partner(values):
    lane = lax.broadcasted_iota(jnp.int32, values.shape, 1)
    return jnp.where(
        lane % HD < HD // 2, pltpu.roll(values, 96, 1), pltpu.roll(values, 32, 1)
    )


def reorder(source):
    count = source.shape[1]
    rows = lax.broadcasted_iota(jnp.int32, (count, count), 0)
    return jnp.where(rows == source, 1.0, 0.0).astype(BF16)


def unit_rows(values):
    centered = values - jnp.mean(values, axis=-1, keepdims=True)
    scaling = lax.rsqrt(jnp.mean(centered * centered, axis=-1, keepdims=True) + EPS_NORM)
    return centered * scaling, scaling


def norm_back(grad_rows, units, scaling, gain_row):
    along = grad_rows * gain_row
    back_rows = scaling * (
        along
        - jnp.mean(along, axis=-1, keepdims=True)
        - units * jnp.mean(along * units, axis=-1, keepdims=True)
    )
    return (
        back_rows,
        jnp.sum(grad_rows * units, axis=0, keepdims=True),
        jnp.sum(grad_rows, axis=0, keepdims=True),
    )


def whole_spec():
    return pl.BlockSpec(memory_space=pltpu.VMEM)


def params(mib=60):
    return pltpu.CompilerParams(vmem_limit_bytes=mib * MIB)


def pack_kernel(*refs):
    *weight_refs, out_ref = refs
    rows, width = weight_refs[2].shape
    to = 0
    for ref in weight_refs:
        count = ref.shape[0]
        for at in range(0, ref.shape[1], width):
            out_ref[to : to + count, :] = ref[:, at : at + width]
            to += count


def pack_own(*weights):
    rows, width = weights[2].shape
    if rows % 16:
        parts = [
            w[:, at : at + width] for w in weights[:-1] for at in range(0, w.shape[1], width)
        ]
        return jnp.concatenate(parts + [weights[-1]], axis=0)
    total = sum(w.size for w in weights) // width
    full = lambda *dims: pl.BlockSpec(dims, lambda i: (0,) * len(dims))
    return pl.pallas_call(
        pack_kernel,
        grid=(1,),
        in_specs=[full(*w.shape) for w in weights],
        out_specs=full(total, width),
        out_shape=jax.ShapeDtypeStruct((total, width), BF16),
        compiler_params=params(),
    )(*weights)


def attend_kernel(
    rows_ref, wqkv_ref, wout_ref, cos_ref, sin_ref, mark_ref, markt_ref, vec_ref,
    q_ref, k_ref, v_ref, att_ref, low_ref, unit_ref, scale_ref, bias_ref,
):
    rows = rows_ref[...]
    tokens, width = rows.shape
    pair = 2 * HD
    cosine, sine = cos_ref[...], sin_ref[...]
    bias_ref[...] = jnp.where(mark_ref[...] == markt_ref[...], 0.0, MASKED)
    for part, out_ref in enumerate((q_ref, k_ref, v_ref)):
        mixed = joined(rows, wqkv_ref[:, part].reshape(width, width), 1, 0)
        if part == 2:
            out_ref[...] = mixed.astype(BF16)
        else:
            for at in range(0, width, pair):
                piece = mixed[:, at : at + pair]
                turned = piece * cosine + partner(piece) * sine
                out_ref[:, at : at + pair] = turned.astype(BF16)
    first_half = lax.broadcasted_iota(jnp.int32, (tokens, pair), 1) < HD
    for at in range(0, width, pair):
        query = q_ref[:, at : at + pair]
        key = k_ref[:, at : at + pair]
        value = v_ref[:, at : at + pair]
        outs = []
        for half in range(2):
            inside = first_half if half == 0 else jnp.logical_not(first_half)
            only = jnp.where(inside, query, jnp.zeros_like(query))
            scores = joined(only, key, 1, 1) * HD**-0.5 + bias_ref[...]
            raised = jnp.exp(scores - jnp.max(scores, axis=-1, keepdims=True))
            total = jnp.sum(raised, axis=-1, keepdims=True)
            weights = (raised * (1.0 / total)).astype(BF16)
            outs.append(joined(weights, value, 1, 0))
        att_ref[:, at : at + pair] = jnp.where(first_half, outs[0], outs[1]).astype(BF16)
    hidden = rows.astype(F32) + joined(att_ref[...], wout_ref[:, 0].reshape(width, width), 1, 0)
    units, scaling = unit_rows(hidden)
    unit_ref[...] = units
    scale_ref[...] = scaling
    low_ref[...] = (units * vec_ref[0:1, :] + vec_ref[1:2, :]).astype(BF16)


def forward_kernel(
    rows_ref, wqkv_ref, wout_ref, cos_ref, sin_ref, mark_ref, markt_ref, vec_ref, pool_ref, pack_ref,
    q_ref, k_ref, v_ref, att_ref, low_ref, unit1_ref, scale1_ref, unit_ref, scale_ref, pooled_ref,
    emb_ref, act_ref, togate_ref, toup_ref,
    bias_ref, wide_ref, deep_ref, made_ref, in_sem, out_sem,
):
    tokens, width = rows_ref.shape
    blocks, deep = deep_ref.shape[0], deep_ref.shape[1:3]
    chunks = pack_ref.shape[1]
    arriving = []
    for j in range(blocks):
        if deep[0] * blocks == pack_ref.shape[0]:
            below = pack_ref.at[pl.ds(j * deep[0], deep[0]), pl.ds(chunks - deep[1], deep[1])]
        else:
            below = pack_ref.at[:, pl.ds(chunks - blocks + j, 1)]
        pairs = (
            (pack_ref.at[:, j], wide_ref.at[j]),
            (pack_ref.at[:, blocks + j], wide_ref.at[blocks + j]),
            (below, deep_ref.at[j]),
        )
        arriving.append(
            [pltpu.make_async_copy(*pair, in_sem.at[3 * j + k]) for k, pair in enumerate(pairs)]
        )
    for copies in arriving:
        for copy in copies:
            copy.start()
    attend_kernel(
        rows_ref, wqkv_ref, wout_ref, cos_ref, sin_ref, mark_ref, markt_ref, vec_ref,
        q_ref, k_ref, v_ref, att_ref, low_ref, unit1_ref, scale1_ref, bias_ref,
    )
    low = low_ref[...]
    total = unit1_ref[...] * vec_ref[0:1, :] + vec_ref[1:2, :]
    leaving = []
    for j in range(blocks):
        for copy in arriving[j]:
            copy.wait()
        gate = joined(low, wide_ref[j].reshape(width, width), 1, 0)
        up = joined(low, wide_ref[blocks + j].reshape(width, width), 1, 0)
        sig = 1.0 / (1.0 + jnp.exp(-gate))
        silu = gate * sig
        active = (silu * up).astype(BF16)
        made_ref[j, 0] = active
        made_ref[j, 1] = silu.astype(BF16)
        made_ref[j, 2] = (up * sig * (1.0 + gate * (1.0 - sig))).astype(BF16)
        for k, out_ref in enumerate((act_ref, toup_ref, togate_ref)):
            copy = pltpu.make_async_copy(
                made_ref.at[j, k], out_ref.at[:, pl.ds(j * width, width)], out_sem.at[3 * j + k]
            )
            copy.start()
            leaving.append(copy)
        total += joined(active, deep_ref[j].reshape(width, width), 1, 0)
    units, scaling = unit_rows(total)
    unit_ref[...] = units
    scale_ref[...] = scaling
    second = units * vec_ref[2:3, :] + vec_ref[3:4, :]
    rows = [
        jnp.sum(second * pool_ref[:, s : s + 1], axis=0, keepdims=True)
        for s in range(pool_ref.shape[1])
    ]
    pooled = jnp.concatenate(rows, axis=0)
    pooled_ref[...] = pooled
    emb_ref[...] = pooled * lax.rsqrt(jnp.sum(pooled * pooled, axis=-1, keepdims=True) + EPS_UNIT)
    for copy in leaving:
        copy.wait()


def forward(rows, pack, cosine, sine, labels, vectors, pool_t):
    tokens, width = rows.shape
    lead, _, per, _ = pack.shape
    blocks = 4
    seqs = pool_t.shape[1]
    shape = jax.ShapeDtypeStruct
    full = lambda *dims: pl.BlockSpec(dims, lambda i: (0,) * len(dims))
    anywhere = pl.BlockSpec(memory_space=pl.ANY)
    mark = labels.astype(F32)
    deep = (lead // 4, 4) if lead > 1 else (1, 1)
    return pl.pallas_call(
        forward_kernel,
        grid=(1,),
        in_specs=[
            full(tokens, width),
            pl.BlockSpec((lead, 3, per, width), lambda i: (0, 3, 0, 0)),
            pl.BlockSpec((lead, 1, per, width), lambda i: (0, 8, 0, 0)),
            full(tokens, 2 * HD),
            full(tokens, 2 * HD),
            full(tokens, 1),
            full(1, tokens),
            full(4, width),
            full(tokens, seqs),
            anywhere,
        ],
        out_specs=[full(tokens, width)] * 6
        + [full(tokens, 1), full(tokens, width), full(tokens, 1)]
        + [full(seqs, width)] * 2
        + [anywhere] * 3,
        out_shape=[shape((tokens, width), BF16)] * 5
        + [shape((tokens, width), F32), shape((tokens, 1), F32)] * 2
        + [shape((seqs, width), F32)] * 2
        + [shape((tokens, blocks * width), BF16)] * 3,
        scratch_shapes=[
            pltpu.VMEM((tokens, tokens), F32),
            pltpu.VMEM((2 * blocks, lead, per, width), BF16),
            pltpu.VMEM((blocks, *deep, per, width), BF16),
            pltpu.VMEM((blocks, 3, tokens, width), BF16),
            pltpu.SemaphoreType.DMA((3 * blocks,)),
            pltpu.SemaphoreType.DMA((3 * blocks,)),
        ],
        compiler_params=params(),
        cost_estimate=LONG,
    )(rows, pack, pack, cosine, sine, mark[:, None], mark[None, :], vectors, pool_t, pack)


def down_spec(pack, first=0):
    lead, chunks, per, width = pack.shape
    if lead == 1:
        return pl.BlockSpec((1, 1, per, width), lambda i, *p: (0, chunks - 4 + first + i, 0, 0))
    return pl.BlockSpec((lead // 4, 4, per, width), lambda i, *p: (first + i, 3, 0, 0))


def halves_kernel(rows_ref, att_ref, low_ref, act_ref, source_ref, source_down_ref,
                  keep_ref, send_ref, act_keep_ref, act_send_ref):
    step = pl.program_id(0)
    half = rows_ref.shape[1] // 2
    moved = joined(act_ref[...], reorder(source_down_ref[...]), 1, 0).astype(BF16)
    act_keep_ref[0] = moved[:, :half]
    act_send_ref[0] = moved[:, half:]
    for part, ref in enumerate((rows_ref, att_ref, low_ref)):

        @pl.when(step == part)
        def _(ref=ref):
            moved = joined(ref[...], reorder(source_ref[...]), 1, 0).astype(BF16)
            keep_ref[0] = moved[:, :half]
            send_ref[0] = moved[:, half:]


def halves(rows, attended, low, active, source, source_down):
    tokens, width = rows.shape
    blocks = active.shape[1] // width
    full = lambda *dims: pl.BlockSpec(dims, lambda i: (0,) * len(dims))
    three = pl.BlockSpec((1, tokens, width // 2), lambda i: (jnp.minimum(i, 2), 0, 0))
    four = pl.BlockSpec((1, tokens, width // 2), lambda i: (i, 0, 0))
    shape = jax.ShapeDtypeStruct
    return pl.pallas_call(
        halves_kernel,
        grid=(blocks,),
        in_specs=[full(tokens, width)] * 3
        + [pl.BlockSpec((tokens, width), lambda i: (0, i)), full(1, width), full(1, width)],
        out_specs=[three, three, four, four],
        out_shape=[shape((3, tokens, width // 2), BF16)] * 2
        + [shape((blocks, tokens, width // 2), BF16)] * 2,
        compiler_params=params(),
        cost_estimate=LONG,
    )(rows, attended, low, active, source, source_down)


def lse(values, axis):
    top = jnp.max(values, axis=axis, keepdims=True)
    return top + jnp.log(jnp.sum(jnp.exp(values - top), axis=axis, keepdims=True))


def loss_kernel(
    every_ref, match_ref, own_match_ref, tower_ref, emb_ref, pooled_ref, pool_ref, unit_ref,
    scale_ref, vec_ref, *refs,
):
    loss_ref, mid_ref, low_ref, sums_ref = refs[-4:]
    total = every_ref.shape[0] // 2
    queries = every_ref[0:total, :]
    documents = every_ref[total : 2 * total, :]
    similar = joined_high(queries, documents, 1, 1) / TEMPER
    flipped = joined_high(documents, queries, 1, 1) / TEMPER
    row_log = lse(similar, 1)
    loss = (
        0.5 * (jnp.sum(row_log, keepdims=True) + jnp.sum(lse(similar, 0), keepdims=True))
        - jnp.sum(similar * match_ref[...], keepdims=True)
    ) / total
    loss_ref[...] = loss
    first = tower_ref[...] == 0
    others = jnp.where(first, documents, queries)
    other_log = jnp.where(first, lse(similar, 0), lse(flipped, 0))
    own = joined_high(emb_ref[...], others, 1, 1) / TEMPER
    grad_similar = (
        0.5 * (jnp.exp(own - lse(own, 1)) + jnp.exp(own - other_log)) - own_match_ref[...]
    ) / total
    grad_unit = joined_high(grad_similar, others, 1, 0) / TEMPER
    pooled = pooled_ref[...]
    inverse = lax.rsqrt(jnp.sum(pooled * pooled, axis=-1, keepdims=True) + EPS_UNIT)
    along = jnp.sum(pooled * grad_unit, axis=-1, keepdims=True)
    grad_pooled = inverse * grad_unit - inverse * inverse * inverse * pooled * along
    grad_second = sum(
        pool_ref[:, s : s + 1] * grad_pooled[s : s + 1, :] for s in range(grad_pooled.shape[0])
    )
    mid, gain, bias = norm_back(grad_second, unit_ref[...], scale_ref[...], vec_ref[2:3, :])
    mid_ref[...] = mid
    low_ref[...] = mid.astype(BF16)
    sums_ref[0:1, :] = gain
    sums_ref[1:2, :] = bias


def loss_and_grad(
    everyone, pos_doc, tower_index, dp_index, emb, pooled, pool_t, units, scaling, vectors, after
):
    tokens = units.shape[0]
    total = everyone.shape[0] // 2
    seqs, width = emb.shape
    match = (pos_doc[:, None] == jnp.arange(total, dtype=jnp.int32)[None, :]).astype(F32)
    oriented = jnp.where(tower_index == 0, match, match.T)
    own_match = lax.dynamic_slice_in_dim(oriented, dp_index * seqs, seqs, 0)
    shape = jax.ShapeDtypeStruct
    return pl.pallas_call(
        loss_kernel,
        in_specs=[whole_spec()] * 10 + [pl.BlockSpec(memory_space=pl.ANY)] * len(after),
        out_specs=[whole_spec()] * 4,
        out_shape=[shape((1, 1), F32), shape((tokens, width), F32), shape((tokens, width), BF16),
                   shape((2, width), F32)],
        compiler_params=params(30),
        cost_estimate=LONG,
    )(everyone, match, own_match, tower_index.reshape(1, 1), emb, pooled, pool_t, units, scaling,
      vectors, *after)


def gates_kernel(fast, branch_ref, mid_ref, act1_ref, act2_ref, unit_ref, scale_ref, vec_ref,
                 two_ref, source_ref, wgate_ref, wup_ref, wdown_ref,
                 grads_ref, hid_ref, attn_ref, sums_ref, *refs):
    acc_ref = refs[-1]
    step = pl.program_id(0)
    tokens, width = mid_ref.shape
    grad_active = joined(branch_ref[...], wdown_ref[...].reshape(width, width), 1, 1)
    grad_gate = (grad_active * act1_ref[...].astype(F32)).astype(BF16)
    grad_up = (grad_active * act2_ref[...].astype(F32)).astype(BF16)
    grads_ref[0, 0] = grad_gate
    grads_ref[1, 0] = grad_up
    back = joined(grad_gate, wgate_ref[:, 0].reshape(width, width), 1, 1) + joined(
        grad_up, wup_ref[:, 0].reshape(width, width), 1, 1
    )

    @pl.when(step == 0)
    def _():
        acc_ref[...] = mid_ref[...] + back

    @pl.when(step > 0)
    def _():
        acc_ref[...] += back

    @pl.when(step == pl.num_programs(0) - 1)
    def _():
        grad_hidden, gain, bias = norm_back(
            acc_ref[...], unit_ref[...], scale_ref[...], vec_ref[0:1, :]
        )
        hid_ref[...] = grad_hidden
        attn_ref[0:tokens, :] = grad_hidden.astype(BF16)
        if fast:
            values = jnp.concatenate([gain, bias, two_ref[...]], axis=0)
            upper = values.astype(BF16).astype(F32)
            blank = jnp.zeros((8, width), F32)
            parts = jnp.concatenate([upper, values - upper, blank], axis=0).astype(BF16)
            moved = joined(parts, reorder(source_ref[...]), 1, 0).astype(BF16)
            attn_ref[tokens:, :] = moved
        else:
            sums_ref[0:1, :] = gain
            sums_ref[1:2, :] = bias


def gates_back(fast, source, branch, mid, to_gate, to_up, units, scaling, vectors, sums_two, pack):
    tokens, width = mid.shape
    lead, _, per, _ = pack.shape
    blocks = 4
    shape = jax.ShapeDtypeStruct
    full = lambda *dims: pl.BlockSpec(dims, lambda i: (0,) * len(dims))
    flat = full(tokens, width)
    column = pl.BlockSpec((tokens, width), lambda i: (0, i))
    rows = tokens + (16 if fast else 0)
    return pl.pallas_call(
        lambda *refs: gates_kernel(fast, *refs),
        grid=(blocks,),
        in_specs=[flat, flat, column, column, flat, full(tokens, 1), full(4, width),
                  full(2, width), full(1, width),
                  pl.BlockSpec((lead, 1, per, width), lambda i: (0, i, 0, 0)),
                  pl.BlockSpec((lead, 1, per, width), lambda i: (0, 4 + i, 0, 0)),
                  down_spec(pack)],
        out_specs=[pl.BlockSpec((2, 1, tokens, width), lambda i: (0, i, 0, 0)), flat,
                   full(rows, width), full(2, width)],
        out_shape=[shape((2, blocks, tokens, width), BF16), shape((tokens, width), F32),
                   shape((rows, width), BF16), shape((2, width), F32)],
        scratch_shapes=[pltpu.VMEM((tokens, width), F32)],
        compiler_params=params(30),
        cost_estimate=LONG,
    )(branch, mid, to_gate, to_up, units, scaling, vectors, sums_two, source, pack, pack, pack)


def attend_back_kernel(
    wout_ref, cos_ref, sin_ref, mark_ref, markt_ref, q_ref, k_ref, v_ref, grad_ref, *refs
):
    mixed_ref, bias_ref, gatt_ref = refs[-3:]
    tokens, width = q_ref.shape
    pair = 2 * HD
    cosine, sine = cos_ref[...], sin_ref[...]
    bias_ref[...] = jnp.where(mark_ref[...] == markt_ref[...], 0.0, MASKED)
    gatt_ref[...] = joined(grad_ref[...], wout_ref[:, 0].reshape(width, width), 1, 1).astype(BF16)
    first_half = lax.broadcasted_iota(jnp.int32, (tokens, pair), 1) < HD
    for at in range(0, width, pair):
        query = q_ref[:, at : at + pair]
        key = k_ref[:, at : at + pair]
        value = v_ref[:, at : at + pair]
        grad_out = gatt_ref[:, at : at + pair]
        found = []
        for half in range(2):
            inside = first_half if half == 0 else jnp.logical_not(first_half)
            scores = (
                joined(jnp.where(inside, key, jnp.zeros_like(key)), query, 1, 1) * HD**-0.5
                + bias_ref[...]
            )
            raised = jnp.exp(scores - jnp.max(scores, axis=0, keepdims=True))
            probs = raised * (1.0 / jnp.sum(raised, axis=0, keepdims=True))
            grad_probs = joined(
                jnp.where(inside, value, jnp.zeros_like(value)), grad_out, 1, 1
            )
            delta = jnp.sum(probs * grad_probs, axis=0, keepdims=True)
            grad_scores = (probs * (grad_probs - delta)).astype(BF16)
            found.append(
                (
                    joined(grad_scores, key, 0, 0),
                    joined(grad_scores, query, 1, 0),
                    joined(probs.astype(BF16), grad_out, 1, 0),
                )
            )
        grad_query = jnp.where(first_half, found[0][0], found[1][0]) * HD**-0.5
        grad_key = jnp.where(first_half, found[0][1], found[1][1]) * HD**-0.5
        grad_value = jnp.where(first_half, found[0][2], found[1][2])
        mixed_ref[0, :, at : at + pair] = (
            grad_query * cosine - partner(grad_query) * sine
        ).astype(BF16)
        mixed_ref[1, :, at : at + pair] = (
            grad_key * cosine - partner(grad_key) * sine
        ).astype(BF16)
        mixed_ref[2, :, at : at + pair] = grad_value.astype(BF16)


def attend_back(pack, cosine, sine, labels, query, key, value, grad, after=()):
    tokens, width = query.shape
    lead, _, per, _ = pack.shape
    full = lambda *dims: pl.BlockSpec(dims, lambda i: (0,) * len(dims))
    flat = full(tokens, width)
    mark = labels.astype(F32)
    return pl.pallas_call(
        attend_back_kernel,
        grid=(1,),
        in_specs=[pl.BlockSpec((lead, 1, per, width), lambda i: (0, 8, 0, 0)),
                  full(tokens, 2 * HD), full(tokens, 2 * HD), full(tokens, 1), full(1, tokens)]
        + [flat] * 4 + [pl.BlockSpec(memory_space=pl.ANY)] * len(after),
        out_specs=full(3, tokens, width),
        out_shape=jax.ShapeDtypeStruct((3, tokens, width), BF16),
        scratch_shapes=[pltpu.VMEM((tokens, tokens), F32), pltpu.VMEM((tokens, width), BF16)],
        compiler_params=params(30),
        cost_estimate=LONG,
    )(pack, cosine, sine, mark[:, None], mark[None, :], query, key, value, grad, *after)


def tokens_kernel(mixed_ref, hid_ref, wqkv_ref, *refs):
    tokens, width = hid_ref.shape
    back = hid_ref[...]
    for part in range(3):
        back += joined(mixed_ref[part], wqkv_ref[:, part].reshape(width, width), 1, 1)
    refs[-1][...] = back


def tokens_back(mixed, hidden, pack, after=()):
    tokens, width = hidden.shape
    lead, _, per, _ = pack.shape
    full = lambda *dims: pl.BlockSpec(dims, lambda i: (0,) * len(dims))
    return pl.pallas_call(
        tokens_kernel,
        grid=(1,),
        in_specs=[full(3, tokens, width), full(tokens, width),
                  pl.BlockSpec((lead, 3, per, width), lambda i: (0, 3, 0, 0))]
        + [pl.BlockSpec(memory_space=pl.ANY)] * len(after),
        out_specs=full(tokens, width),
        out_shape=jax.ShapeDtypeStruct((tokens, width), F32),
        compiler_params=params(),
        cost_estimate=LONG,
    )(mixed, hidden, pack, *after)


def both(own_left, got_left, own_right, got_right):
    return (joined(own_left, own_right, 0, 0) + joined(got_left, got_right, 0, 0)).astype(BF16)


def steps_call(kernel, grid, ins, args, outs, shapes, scalars=None, after=()):
    ins = ins + [pl.BlockSpec(memory_space=pl.ANY)] * len(after)
    shapes = [jax.ShapeDtypeStruct(dims, BF16) for dims in shapes]
    more = dict(out_shape=shapes, compiler_params=params(30), cost_estimate=LONG)
    if scalars is None:
        return pl.pallas_call(
            kernel, grid=grid, in_specs=ins, out_specs=outs, **more
        )(*args, *after)
    return pl.pallas_call(
        kernel,
        grid_spec=pltpu.PrefetchScalarGridSpec(
            num_scalar_prefetch=1, grid=grid, in_specs=ins, out_specs=outs
        ),
        **more,
    )(scalars, *args, *after)


def down_kernel(own_ref, got_ref, grad_ref, got_grad_ref, *refs):
    held_ref, moving_ref = refs[-2:]
    value = both(own_ref[0], got_ref[0], grad_ref[...], got_grad_ref[...])
    half = value.shape[0] // 2
    held_ref[0] = value[:half]
    moving_ref[0] = value[half:]


def down_grads(own, got, grad, got_grad, after=()):
    blocks, tokens, rows = own.shape
    width = grad.shape[1]
    left = pl.BlockSpec((1, tokens, rows), lambda i: (i, 0, 0))
    right = pl.BlockSpec((tokens, width), lambda i: (0, 0))
    out = pl.BlockSpec((1, rows // 2, width), lambda i: (i, 0, 0))
    dims = (blocks, rows // 2, width)
    return steps_call(
        down_kernel, (blocks,), [left, left, right, right], (own, got, grad, got_grad),
        [out, out], [dims, dims], after=after,
    )


def first_kernel(own_ref, got_ref, grad_ref, got_grad_ref, *refs):
    held_ref, moving_ref = refs[-2:]
    value = both(own_ref[0], got_ref[0], grad_ref[0, 0], got_grad_ref[0, 0])
    half = value.shape[0] // 2
    held_ref[...] = value[:half].reshape(held_ref.shape)
    moving_ref[...] = value[half:].reshape(held_ref.shape)


def first_grads(own, got, grads, got_grads, which, part, after=()):
    _, tokens, rows = own.shape
    _, chunks, _, width = grads.shape
    left = pl.BlockSpec((1, tokens, rows), lambda i: (part, 0, 0))
    right = pl.BlockSpec((1, 1, tokens, width), lambda i: (which, i, 0, 0))
    out = pl.BlockSpec((4, 1, rows // 8, width), lambda i: (0, i, 0, 0))
    dims = (4, chunks, rows // 8, width)
    return steps_call(
        first_kernel, (chunks,), [left, left, right, right], (own, got, grads, got_grads),
        [out, out], [dims, dims], after=after,
    )


def tower_kernel(tower_ref, own_ref, got_ref, grad_ref, got_grad_ref, *refs):
    held_ref, lent_ref = refs[-2:]
    value = both(own_ref[0], got_ref[0], grad_ref[0, 0], got_grad_ref[0, 0])
    value = value.reshape(held_ref.shape)
    here = pl.program_id(0) < pl.num_programs(0) // 2

    @pl.when(here)
    def _():
        held_ref[...] = value

    @pl.when(jnp.logical_not(here))
    def _():
        lent_ref[...] = value


def tower_grads(tower, own, got, grads, got_grads, which, chunks, first, part, after=()):
    _, tokens, rows = own.shape
    width = grads.shape[-1]
    half = chunks // 2
    left = pl.BlockSpec((1, tokens, rows), lambda i, t: (part, 0, 0))
    right = pl.BlockSpec(
        (1, 1, tokens, width), lambda i, t: (which, first + (i + half * t[0]) % chunks, 0, 0)
    )
    block = (2, 4, 1, rows // 8, width)
    dims = (2, 4, half, rows // 8, width)
    outs = [
        pl.BlockSpec(block, lambda i, t: (0, 0, jnp.minimum(i, half - 1), 0, 0)),
        pl.BlockSpec(block, lambda i, t: (0, 0, jnp.maximum(i - half, 0), 0, 0)),
    ]
    return steps_call(
        tower_kernel, (chunks,), [left, left, right, right], (own, got, grads, got_grads),
        outs, [dims, dims], scalars=tower, after=after,
    )


def rest_kernel(own_ref, got_ref, attn_ref, got_attn_ref, mixed_ref, got_mixed_ref, *refs):
    held_ref, moving_ref = refs[-2:]
    tokens, width = mixed_ref.shape[1:]
    half = width // 4
    pieces = [
        both(own_ref[1], got_ref[1], attn_ref[0:tokens, :], got_attn_ref[0:tokens, :]),
        both(own_ref[0], got_ref[0], mixed_ref[0], got_mixed_ref[0]),
    ]
    parts = attn_ref[tokens:, : width // 2].astype(F32)
    got = got_attn_ref[tokens:, width // 2 :].astype(F32)
    values = parts[0:4] + parts[4:8] + got[0:4] + got[4:8]
    upper = values.astype(BF16).astype(F32)
    blank = jnp.zeros((PAD - 2 * VECTORS, width // 2), F32)
    pieces.append(jnp.concatenate([upper, values - upper, blank], axis=0).T.astype(BF16))
    at = 0
    for piece in pieces:
        columns = piece.shape[1]
        for k, out_ref in enumerate((held_ref, moving_ref)):
            out_ref[:, :, at : at + columns] = piece[k * 2 * half // 2 : (k + 1) * half].reshape(
                4, -1, columns
            )
        at += columns


def rest_grads(own, got, attn, got_attn, mixed, got_mixed, after=()):
    _, tokens, rows = own.shape
    width = mixed.shape[2]
    full = lambda *dims: pl.BlockSpec(dims, lambda i: (0,) * len(dims))
    one = pl.BlockSpec((1, tokens, width), lambda i: (0, 0, 0))
    dims = (4, rows // 8, 2 * width + PAD)
    return steps_call(
        rest_kernel, (1,),
        [full(*own.shape), full(*own.shape), full(*attn.shape), full(*attn.shape), one, one],
        (own, got, attn, got_attn, mixed, got_mixed),
        [full(*dims)] * 2, [dims, dims], after=after,
    )


def reduce_digit(parts, sizes, place, digit):
    size = sizes[place]
    total = pick(parts, 0, digit).astype(F32)
    for shift in range(1, size):
        sent = pick(parts, 0, (digit + shift) % size).astype(BF16)
        total += lax.ppermute(sent, "dp", digit_shift(sizes, place, shift)).astype(F32)
    return total


def shared_sum(grad, sizes, digits, tower_index):
    rows, columns = grad.shape
    count = math.prod(sizes)
    per = rows // count
    tiles = columns // 128
    side = max(1, round(tiles * 0.3)) * 128
    middle = columns - 2 * side
    last = len(sizes) - 1
    blocks = grad.astype(BF16).reshape(count // sizes[last], sizes[last], per, columns)
    chip = reduce_digit(jnp.moveaxis(blocks, 1, 0), sizes, last, digits[last]).astype(BF16)
    lead = chip.shape[0]
    mine = lax.dynamic_slice(chip, (0, 0, tower_index * (columns - side)), (lead, per, side))
    other = lax.dynamic_slice(
        chip, (0, 0, (1 - tower_index) * (columns - side)), (lead, per, side)
    )
    mine = mine.astype(F32) + lax.ppermute(other, "tower", SWAP).astype(F32)
    part = jnp.concatenate([mine.astype(BF16), chip[:, :, side : side + middle]], axis=2)
    for place in range(last - 1, -1, -1):
        size = sizes[place]
        part = jnp.moveaxis(part.reshape(part.shape[0] // size, size, per, side + middle), 1, 0)
        part = reduce_digit(part, sizes, place, digits[place]).astype(BF16)
    part = part[0]
    back = lax.ppermute(part, "tower", SWAP).astype(F32)
    part = part.astype(F32)
    centre = part[:, side:] + back[:, side:]
    first = tower_index == 0
    return jnp.concatenate(
        [
            jnp.where(first, part[:, :side], back[:, :side]),
            centre,
            jnp.where(first, back[:, :side], part[:, :side]),
        ],
        axis=1,
    )


def plus_kernel(jobs, count, z_ref, *refs):
    for out_ref, (terms, vectors) in zip(refs[count:], jobs, strict=True):
        total = None
        for place, index in terms:
            piece = refs[place][index(z_ref[0]) if callable(index) else index].astype(F32)
            total = piece if total is None else total + piece
        total = total.reshape(out_ref.shape)
        if vectors:
            at = total.shape[-1] - PAD
            parts = total[..., at:].reshape(-1, PAD)
            lane = lax.broadcasted_iota(jnp.int32, parts.shape, 1)
            values = parts + pltpu.roll(parts, PAD - VECTORS, 1)
            upper = values.astype(BF16).astype(F32)
            lower = pltpu.roll(values - upper, VECTORS, 1)
            parts = jnp.where(lane < VECTORS, upper, jnp.where(lane < 2 * VECTORS, lower, 0.0))
            out_ref[..., :at] = total[..., :at].astype(BF16)
            out_ref[..., at:] = parts.astype(BF16).reshape(*out_ref.shape[:-1], PAD)
        else:
            out_ref[...] = total.astype(BF16)


def plus(jobs, z, after=()):
    inputs, outs, shapes = [], [], []
    for arrays, plan, dims, vectors in jobs:
        base = len(inputs)
        inputs += arrays
        outs += [([(base + place, index) for place, index in terms], vectors) for terms in plan]
        shapes += dims
    count = len(inputs)
    spec = lambda dims: pl.BlockSpec(dims, lambda i: (0,) * len(dims))
    return pl.pallas_call(
        lambda *refs: plus_kernel(
            outs, count, *refs[: 1 + count], *refs[1 + count + len(after) :]
        ),
        grid=(1,),
        in_specs=[pl.BlockSpec(memory_space=pltpu.SMEM)]
        + [spec(a.shape) for a in inputs]
        + [pl.BlockSpec(memory_space=pl.ANY)] * len(after),
        out_specs=[spec(dims) for dims in shapes],
        out_shape=[jax.ShapeDtypeStruct(dims, BF16) for dims in shapes],
        compiler_params=params(24),
        cost_estimate=SHORT,
    )(z, *inputs, *after)


class GradSum:
    def __init__(self, pair, sizes, z, by_tower, direct, vectors=False):
        self.sizes = sizes
        self.z = z
        self.direct = direct
        self.vectors = vectors
        self.by_tower = by_tower
        self.held, sent = pair
        self.got = lax.ppermute(sent, "tower", SWAP) if by_tower else self.shift_y(sent)
        self.steps = ["tower", "y", "z"] if by_tower else ["y", "z"]

    def shift_y(self, sent):
        return lax.ppermute(sent, "dp", digit_shift(self.sizes, 1, 1))

    def job(self):
        step = self.steps[0]
        if step == "tower":
            plan = [[(0, (k,)), (1, (k,))] for k in (1, 0)]
            return [self.held, self.got], plan, [self.held.shape[1:]] * 2, self.vectors
        depth = self.sizes[0]
        if step == "y" and self.direct:
            views = [lambda z, k=k: ((z + k) % depth,) for k in (1, 2, 3, 0)]
            plan = [[(0, view), (1, view)] for view in views]
            return [self.held, self.got], plan, [self.held.shape[1:]] * depth, self.vectors
        if step == "y":
            plan = [[(0, (Ellipsis,)), (1, (Ellipsis,))]]
            return [self.held, self.got], plan, [self.held.shape], self.vectors
        if self.direct:
            plan = [[(k, (Ellipsis,)) for k in range(depth)]]
            return [self.held, *self.got], plan, [self.held.shape], self.vectors
        plan = [[(0, (k,)) for k in range(depth)]]
        return [self.got], plan, [self.got.shape[1:]], self.vectors

    def take(self, outs):
        step = self.steps.pop(0)
        if step == "tower":
            moving, self.held = outs
            self.got = self.shift_y(moving)
        elif step == "y" and self.direct:
            *parts, self.held = outs
            self.got = [
                lax.ppermute(part, "dp", digit_shift(self.sizes, 0, k + 1))
                for k, part in enumerate(parts)
            ]
        elif step == "y":
            depth, rest = self.sizes[0], math.prod(self.sizes[1:])
            groups = [[z * rest + other for z in range(depth)] for other in range(rest)]
            self.got = lax.all_to_all(outs[0], "dp", 0, 0, axis_index_groups=groups, tiled=True)
        else:
            (self.held,) = outs
            self.got = lax.ppermute(self.held, "tower", SWAP)

    def result(self, tower_index):
        first = tower_index == 0
        return jnp.where(first, self.held, self.got), jnp.where(first, self.got, self.held)


def advance(order, *sums, done=()):
    jobs = [one.job() for one in sums]
    outs = plus(jobs, sums[0].z, (order, *(one.got for one in done)))
    last = outs[-1]
    for one, (_, plan, _, _) in zip(sums, jobs, strict=True):
        one.take(outs[: len(plan)])
        outs = outs[len(plan) :]
    return last


def sum_norms(sums_one, sums_two, dp_count):
    sums = jnp.concatenate([sums_one, sums_two], axis=0)
    sums = sums.reshape(4, dp_count, -1).transpose(1, 0, 2)
    sums = jnp.concatenate([sums, sums], axis=0)
    return jnp.sum(lax.all_to_all(sums, ("tower", "dp"), 0, 0, tiled=True), axis=0)


def finish_kernel(plan, count, *refs):
    for out_ref, terms in zip(refs[count:], plan, strict=True):
        for to, places, index in terms:
            total = refs[places[0]][index].astype(F32)
            for place in places[1:]:
                total += refs[place][index].astype(F32)
            out_ref[to] = total


def finish(inputs, plan, shapes, after=()):
    count = len(inputs)
    spec = lambda dims: pl.BlockSpec(dims, lambda i: (0,) * len(dims))
    return pl.pallas_call(
        lambda *refs: finish_kernel(plan, count, *refs[:count], *refs[count + len(after) :]),
        grid=(1,),
        in_specs=[spec(a.shape) for a in inputs]
        + [pl.BlockSpec(memory_space=pl.ANY)] * len(after),
        out_specs=[spec(dims) for dims in shapes],
        out_shape=[jax.ShapeDtypeStruct(dims, F32) for dims in shapes],
        compiler_params=params(24),
        cost_estimate=SHORT,
    )(*inputs, *after)


def beside(chunks):
    return jnp.concatenate(list(chunks), axis=1)


def column_orders(digits, per, spread, width):
    _, y, c = digits
    place = jnp.arange(width, dtype=jnp.int32)
    block, row = place // per, place % per
    core, dy, z = block // 8, block // 4 % 2, block % 4
    source = ((z * 4 + (dy + y) % 2 * 2 + (core + c) % 2)) * per + row
    device = (dy + y) % 2 * 2 + (core + c) % 2
    return source[None], ((device * spread + block % 4) * per + row)[None]


def body(
    tokens,
    lengths,
    pos_doc,
    w_qkv,
    w_out,
    w_gate,
    w_up,
    w_down,
    ln1_gain,
    ln1_bias,
    ln2_gain,
    ln2_bias,
):
    dp_count = lax.axis_size("dp")
    device_count = 2 * dp_count
    sizes = split_dp(dp_count)
    dp_index = lax.axis_index("dp")
    tower_index = lax.axis_index("tower")
    digits = digits_of(dp_index, sizes)
    per, narrow = w_out.shape
    wide = w_gate.shape[1]
    spread = wide // narrow

    own_pack = pack_own(w_gate, w_up, w_out, w_qkv, w_down)
    pack = lax.all_gather(own_pack, "dp", axis=0, tiled=True)
    pack = pack.reshape(dp_count, 4 * spread, per, narrow)
    if per % 16:
        front = pack[:, : 3 * spread].transpose(1, 0, 2, 3).reshape(3 * spread, narrow, narrow)
        back = pack[:, 3 * spread :].reshape(spread, narrow, narrow)
        pack = jnp.concatenate([front, back], axis=0)[None]
    vectors_own = jnp.stack([ln1_gain, ln1_bias, ln2_gain, ln2_bias])
    vectors = lax.all_to_all(
        jnp.broadcast_to(vectors_own[None], (dp_count, 4, per)), "dp", 0, 0, tiled=True
    )
    vectors = vectors.transpose(1, 0, 2).reshape(4, narrow).astype(F32)

    rows_in = tokens[0]
    row_count = rows_in.shape[0]
    pooling, labels, offsets = layout(lengths[0], row_count)
    pool_t = pooling.T
    cosine, sine = rotary_tables(offsets)

    fast = sizes == [4, 2, 2] and spread == 4 and per % 16 == 0
    source, source_down = column_orders(digits, per, spread, narrow) if fast else (
        jnp.zeros((1, narrow), jnp.int32),
    ) * 2
    core_swap = digit_shift(sizes, len(sizes) - 1, 1)
    swap_cores = lambda values: lax.ppermute(values, "dp", core_swap)
    (query, key, value, attended, first_low, unit_one, scale_one, unit_two, scale_two, pooled,
     unit_vectors, active, to_gate, to_up) = forward(
        rows_in, pack, cosine, sine, labels, vectors, pool_t
    )
    seq_count = unit_vectors.shape[0]
    everyone = lax.all_to_all(
        jnp.broadcast_to(unit_vectors[None], (device_count,) + unit_vectors.shape),
        ("tower", "dp"),
        0,
        0,
        tiled=True,
    ).reshape(device_count * seq_count, narrow)
    if fast:
        own, lent, own_active, lent_active = halves(
            rows_in, attended, first_low, active, source, source_down
        )
    loss_value, grad_mid, grad_branch, sums_two = loss_and_grad(
        everyone, pos_doc, tower_index, dp_index, unit_vectors, pooled, pool_t, unit_two, scale_two,
        vectors, (own,) if fast else (),
    )
    grad_feed, grad_hidden, grad_attn, sums_one = gates_back(
        fast, source, grad_branch, grad_mid, to_gate, to_up, unit_one, scale_one, vectors, sums_two,
        pack,
    )
    heads_args = (pack, cosine, sine, labels, query, key, value, grad_attn)
    if fast:
        got, got_active = swap_cores(lent), swap_cores(lent_active)
        got_branch = swap_cores(grad_branch)
        got_feed = swap_cores(grad_feed)
        got_attn = swap_cores(grad_attn)
        tower = tower_index.reshape(1).astype(jnp.int32)
        plain = lambda pair, **how: GradSum(pair, sizes, digits[0].reshape(1), **how)
        sums, order, late = {}, grad_hidden, []
        for step in ORDER:
            after = (order,)
            if step == "down":
                pair = down_grads(own_active, got_active, grad_branch, got_branch, after)
                sums["d"] = plain(pair, by_tower=False, direct="d" in DIRECT)
                order = pair[0]
            elif step == "heads":
                grad_mixed = attend_back(*heads_args, (order, got_attn))
                got_mixed = swap_cores(grad_mixed)
                order = grad_mixed
            elif step == "gate":
                pair = tower_grads(tower, own, got, grad_feed, got_feed, 0, 4, 0, 2, after)
                sums["g"] = plain(pair, by_tower=True, direct="g" in DIRECT)
                order = pair[0]
            elif step == "up":
                pair = first_grads(own, got, grad_feed, got_feed, 1, 2, after)
                sums["u"] = plain(pair, by_tower=False, direct="u" in DIRECT)
                order = pair[0]
            elif step == "rest":
                pair = rest_grads(own, got, grad_attn, got_attn, grad_mixed, got_mixed, after)
                sums["r"] = plain(pair, by_tower=False, direct="r" in DIRECT, vectors=True)
                order = pair[0]
            elif step == "last":
                pair = tower_grads(
                    tower, own, got, grad_mixed[None], got_mixed[None], 0, 2, 1, 0, after
                )
                sums["l"] = plain(pair, by_tower=True, direct="l" in DIRECT)
                order = pair[0]
            elif step == "tokens":
                grad_rows = order = tokens_back(grad_mixed, grad_hidden, pack, after)
            else:
                ready = [one for one in late if one.age > 0]
                late = [one for one in late if one.age == 0]
                for one in late:
                    one.age += 1
                moving = [sums[name] for name in step]
                order = advance(order, *moving, done=ready)
                for one in moving:
                    if not one.steps:
                        one.age = 0
                        late.append(one)
        down, gate, up, rest, last = (sums[name] for name in "dgurl")
        columns = lambda k: (slice(None), slice(k * narrow, (k + 1) * narrow))
        sum_down, sum_up = finish(
            [down.held, down.got, up.held, up.got],
            [
                [((Ellipsis,), (0, 1), (Ellipsis,))],
                [(columns(k), (2, 3), (k,)) for k in range(spread)],
            ],
            [down.held.shape, (per, wide)],
        )
        lower, upper = gate.result(tower_index)
        (sum_gate,) = finish(
            [lower, upper],
            [[(columns(k), (k // 2,), (k % 2,)) for k in range(spread)]],
            [(per, wide)],
        )
        key_value = last.result(tower_index)
        sum_out, sum_qkv, norms = finish(
            [rest.held, rest.got, *key_value],
            [
                [((Ellipsis,), (0, 1), columns(0))],
                [(columns(0), (0, 1), columns(1)), (columns(1), (2,), (0,)), (columns(2), (3,), (0,))],
                [((Ellipsis,), (0, 1), (slice(None), slice(2 * narrow, 2 * narrow + PAD)))],
            ],
            [(per, narrow), (per, 3 * narrow), (per, PAD)],
        )
        norms = norms.T
        sums = norms[:VECTORS] + norms[VECTORS : 2 * VECTORS]
    else:
        grad_mixed = attend_back(*heads_args)
        grad_rows = tokens_back(grad_mixed, grad_hidden, pack)
        grad_down = joined(active, grad_branch, 0, 0)
        down_rows = (
            grad_down.reshape(dp_count, spread, per, narrow)
            .transpose(0, 2, 1, 3)
            .reshape(narrow, wide)
        )
        share = lambda grad: shared_sum(grad, sizes, digits, tower_index)
        sum_down = share(down_rows).reshape(per, spread, narrow).transpose(1, 0, 2)
        sum_down = sum_down.reshape(wide // dp_count, narrow)
        sum_gate, sum_up = (
            share(joined(first_low, beside(grad_feed[k]), 0, 0)) for k in range(2)
        )
        sum_out = share(joined(attended, grad_attn, 0, 0))
        sum_qkv = share(joined(rows_in, beside(grad_mixed), 0, 0))
        sums = sum_norms(sums_one, sums_two, dp_count)
    return (
        loss_value.reshape(()),
        unit_vectors[None],
        grad_rows[None],
        sum_qkv,
        sum_out,
        sum_gate,
        sum_up,
        sum_down,
        sums[0],
        sums[1],
        sums[2],
        sums[3],
    )


def solution(mesh):
    placed = (
        P("tower", "dp", None),
        P("tower", "dp"),
        P(),
        P("dp", None),
        P("dp", None),
        P("dp", None),
        P("dp", None),
        P("dp", None),
        P("dp"),
        P("dp"),
        P("dp"),
        P("dp"),
    )
    return jax.shard_map(
        body,
        mesh=mesh,
        in_specs=placed,
        out_specs=(
            P(),
            P("tower", "dp", None),
            P("tower", "dp", None),
            P("dp", None),
            P("dp", None),
            P("dp", None),
            P("dp", None),
            P("dp", None),
            P("dp"),
            P("dp"),
            P("dp"),
            P("dp"),
        ),
        check_vma=False,
    )
```

```python
import math

import jax
import jax.numpy as jnp
from jax import lax
from jax.experimental import pallas as pl
from jax.experimental.pallas import tpu as pltpu
from jax.sharding import PartitionSpec as P

HD = 64
PAD = 128
VECTORS = 4
TEMPER = 0.05
EPS_NORM = 1e-05
EPS_UNIT = 1e-06
MASKED = -1e30
F32 = jnp.float32
BF16 = jnp.bfloat16
MIB = 1 << 20
ORDER = (
    "down", "heads", "gate", "up", "d", "rest", "last", "g",
    "tokens", "u", "l", "d", "r", "g", "u", "l",
    "r", "l", "g",
)
DIRECT = "gulr"
LONG = pl.CostEstimate(flops=100000000000, bytes_accessed=100000000, transcendentals=0)
SHORT = pl.CostEstimate(flops=100000000000, bytes_accessed=100000000, transcendentals=0)


def joined(left_arr, right_arr, left_dim, right_dim):
    return lax.dot_general(
        left_arr,
        right_arr,
        (((left_dim,), (right_dim,)), ((), ())),
        preferred_element_type=F32,
    )


def joined_high(left_arr, right_arr, left_dim, right_dim):
    return lax.dot_general(
        left_arr,
        right_arr,
        (((left_dim,), (right_dim,)), ((), ())),
        precision=lax.Precision.HIGHEST,
        preferred_element_type=F32,
    )


def split_dp(count):
    sizes = [2] if count % 2 == 0 else []
    rest = count // 2 if sizes else count
    front = []
    while rest > 1:
        step = 4 if rest % 4 == 0 else (2 if rest % 2 == 0 else rest)
        front.append(step)
        rest //= step
    return front + sizes


def digit_shift(sizes, place, shift):
    stride = math.prod(sizes[place + 1 :])
    size = sizes[place]
    pairs = []
    for index in range(math.prod(sizes)):
        digit = index // stride % size
        pairs.append((index, index + ((digit + shift) % size - digit) * stride))
    return pairs


def digits_of(index, sizes):
    found = []
    for size in reversed(sizes):
        found.append(index % size)
        index = index // size
    return found[::-1]


SWAP = [(0, 1), (1, 0)]


def pick(array, axis, place):
    return lax.dynamic_index_in_dim(array, place, axis, keepdims=False)


def layout(seq_spans, row_count):
    seq_total = seq_spans.shape[0]
    starts = jnp.cumsum(seq_spans) - seq_spans
    places = jnp.arange(row_count, dtype=jnp.int32)
    member = (
        (places[None, :] >= starts[:, None]) & (places[None, :] < (starts + seq_spans)[:, None])
    ).astype(jnp.int32)
    labels = jnp.sum(member * jnp.arange(seq_total, dtype=jnp.int32)[:, None], axis=0)
    offsets = places - jnp.sum(member * starts[:, None], axis=0)
    pooling = member.astype(F32) / seq_spans.astype(F32)[:, None]
    return (pooling, labels, offsets)


def rotary_tables(offsets):
    half_size = HD // 2
    frequency = 1000.0 ** (-jnp.arange(half_size, dtype=F32) / half_size)
    angles = offsets.astype(F32)[:, None] * frequency[None, :]
    cosine, sine = jnp.cos(angles), jnp.sin(angles)
    return (
        jnp.concatenate([cosine] * 4, axis=1),
        jnp.concatenate([-sine, sine, -sine, sine], axis=1),
    )


def partner(values):
    lane = lax.broadcasted_iota(jnp.int32, values.shape, 1)
    return jnp.where(
        lane % HD < HD // 2, pltpu.roll(values, 96, 1), pltpu.roll(values, 32, 1)
    )


def reorder(source):
    count = source.shape[1]
    rows = lax.broadcasted_iota(jnp.int32, (count, count), 0)
    return jnp.where(rows == source, 1.0, 0.0).astype(BF16)


def unit_rows(values):
    centered = values - jnp.mean(values, axis=-1, keepdims=True)
    scaling = lax.rsqrt(jnp.mean(centered * centered, axis=-1, keepdims=True) + EPS_NORM)
    return centered * scaling, scaling


def norm_back(grad_rows, units, scaling, gain_row):
    along = grad_rows * gain_row
    back_rows = scaling * (
        along
        - jnp.mean(along, axis=-1, keepdims=True)
        - units * jnp.mean(along * units, axis=-1, keepdims=True)
    )
    return (
        back_rows,
        jnp.sum(grad_rows * units, axis=0, keepdims=True),
        jnp.sum(grad_rows, axis=0, keepdims=True),
    )


def whole_spec():
    return pl.BlockSpec(memory_space=pltpu.VMEM)


def params(mib=60):
    return pltpu.CompilerParams(vmem_limit_bytes=mib * MIB)


def pack_kernel(*refs):
    *weight_refs, out_ref = refs
    rows, width = weight_refs[2].shape
    to = 0
    for ref in weight_refs:
        count = ref.shape[0]
        for at in range(0, ref.shape[1], width):
            out_ref[to : to + count, :] = ref[:, at : at + width]
            to += count


def pack_own(*weights):
    rows, width = weights[2].shape
    if rows % 16:
        parts = [
            w[:, at : at + width] for w in weights[:-1] for at in range(0, w.shape[1], width)
        ]
        return jnp.concatenate(parts + [weights[-1]], axis=0)
    total = sum(w.size for w in weights) // width
    full = lambda *dims: pl.BlockSpec(dims, lambda i: (0,) * len(dims))
    return pl.pallas_call(
        pack_kernel,
        grid=(1,),
        in_specs=[full(*w.shape) for w in weights],
        out_specs=full(total, width),
        out_shape=jax.ShapeDtypeStruct((total, width), BF16),
        compiler_params=params(),
    )(*weights)


def attend_kernel(
    rows_ref, wqkv_ref, wout_ref, cos_ref, sin_ref, mark_ref, markt_ref, vec_ref,
    q_ref, k_ref, v_ref, att_ref, low_ref, unit_ref, scale_ref, bias_ref,
):
    rows = rows_ref[...]
    tokens, width = rows.shape
    pair = 2 * HD
    cosine, sine = cos_ref[...], sin_ref[...]
    bias_ref[...] = jnp.where(mark_ref[...] == markt_ref[...], 0.0, MASKED)
    for part, out_ref in enumerate((q_ref, k_ref, v_ref)):
        mixed = joined(rows, wqkv_ref[:, part].reshape(width, width), 1, 0)
        if part == 2:
            out_ref[...] = mixed.astype(BF16)
        else:
            for at in range(0, width, pair):
                piece = mixed[:, at : at + pair]
                turned = piece * cosine + partner(piece) * sine
                out_ref[:, at : at + pair] = turned.astype(BF16)
    first_half = lax.broadcasted_iota(jnp.int32, (tokens, pair), 1) < HD
    for at in range(0, width, pair):
        query = q_ref[:, at : at + pair]
        key = k_ref[:, at : at + pair]
        value = v_ref[:, at : at + pair]
        outs = []
        for half in range(2):
            inside = first_half if half == 0 else jnp.logical_not(first_half)
            only = jnp.where(inside, query, jnp.zeros_like(query))
            scores = joined(only, key, 1, 1) * HD**-0.5 + bias_ref[...]
            raised = jnp.exp(scores - jnp.max(scores, axis=-1, keepdims=True))
            total = jnp.sum(raised, axis=-1, keepdims=True)
            weights = (raised * (1.0 / total)).astype(BF16)
            outs.append(joined(weights, value, 1, 0))
        att_ref[:, at : at + pair] = jnp.where(first_half, outs[0], outs[1]).astype(BF16)
    hidden = rows.astype(F32) + joined(att_ref[...], wout_ref[:, 0].reshape(width, width), 1, 0)
    units, scaling = unit_rows(hidden)
    unit_ref[...] = units
    scale_ref[...] = scaling
    low_ref[...] = (units * vec_ref[0:1, :] + vec_ref[1:2, :]).astype(BF16)


def forward_kernel(
    rows_ref, wqkv_ref, wout_ref, cos_ref, sin_ref, mark_ref, markt_ref, vec_ref, pool_ref, pack_ref,
    q_out, k_out, v_out, att_out, low_out, unit1_out, scale1_ref, unit_ref, scale_ref, pooled_ref,
    emb_ref, act_ref, togate_ref, toup_ref,
    bias_ref, wide_ref, deep_ref, made_ref, heads_ref, unit1_ref, in_sem, out_sem, heads_sem,
):
    tokens, width = rows_ref.shape
    blocks, deep = deep_ref.shape[0], deep_ref.shape[1:3]
    chunks = pack_ref.shape[1]
    arriving = []
    for j in range(blocks):
        if deep[0] * blocks == pack_ref.shape[0]:
            below = pack_ref.at[pl.ds(j * deep[0], deep[0]), pl.ds(chunks - deep[1], deep[1])]
        else:
            below = pack_ref.at[:, pl.ds(chunks - blocks + j, 1)]
        pairs = (
            (pack_ref.at[:, j], wide_ref.at[j]),
            (pack_ref.at[:, blocks + j], wide_ref.at[blocks + j]),
            (below, deep_ref.at[j]),
        )
        arriving.append(
            [pltpu.make_async_copy(*pair, in_sem.at[3 * j + k]) for k, pair in enumerate(pairs)]
        )
    for copies in arriving:
        for copy in copies:
            copy.start()
    attend_kernel(
        rows_ref, wqkv_ref, wout_ref, cos_ref, sin_ref, mark_ref, markt_ref, vec_ref,
        *(heads_ref.at[k] for k in range(5)), unit1_ref, scale1_ref, bias_ref,
    )
    leaving = [
        pltpu.make_async_copy(heads_ref.at[k], out_ref, heads_sem.at[k])
        for k, out_ref in enumerate((q_out, k_out, v_out, att_out, low_out))
    ]
    leaving.append(pltpu.make_async_copy(unit1_ref, unit1_out, heads_sem.at[5]))
    for copy in leaving:
        copy.start()
    low = heads_ref[4]
    total = unit1_ref[...] * vec_ref[0:1, :] + vec_ref[1:2, :]
    for j in range(blocks):
        for copy in arriving[j]:
            copy.wait()
        gate = joined(low, wide_ref[j].reshape(width, width), 1, 0)
        up = joined(low, wide_ref[blocks + j].reshape(width, width), 1, 0)
        sig = 1.0 / (1.0 + jnp.exp(-gate))
        silu = gate * sig
        active = (silu * up).astype(BF16)
        made_ref[j, 0] = active
        made_ref[j, 1] = silu.astype(BF16)
        made_ref[j, 2] = (up * sig * (1.0 + gate * (1.0 - sig))).astype(BF16)
        for k, out_ref in enumerate((act_ref, toup_ref, togate_ref)):
            copy = pltpu.make_async_copy(
                made_ref.at[j, k], out_ref.at[:, pl.ds(j * width, width)], out_sem.at[3 * j + k]
            )
            copy.start()
            leaving.append(copy)
        total += joined(active, deep_ref[j].reshape(width, width), 1, 0)
    units, scaling = unit_rows(total)
    unit_ref[...] = units
    scale_ref[...] = scaling
    second = units * vec_ref[2:3, :] + vec_ref[3:4, :]
    rows = [
        jnp.sum(second * pool_ref[:, s : s + 1], axis=0, keepdims=True)
        for s in range(pool_ref.shape[1])
    ]
    pooled = jnp.concatenate(rows, axis=0)
    pooled_ref[...] = pooled
    emb_ref[...] = pooled * lax.rsqrt(jnp.sum(pooled * pooled, axis=-1, keepdims=True) + EPS_UNIT)
    for copy in leaving:
        copy.wait()


def forward(rows, pack, cosine, sine, labels, vectors, pool_t):
    tokens, width = rows.shape
    lead, _, per, _ = pack.shape
    blocks = 4
    seqs = pool_t.shape[1]
    shape = jax.ShapeDtypeStruct
    full = lambda *dims: pl.BlockSpec(dims, lambda i: (0,) * len(dims))
    anywhere = pl.BlockSpec(memory_space=pl.ANY)
    mark = labels.astype(F32)
    deep = (lead // 4, 4) if lead > 1 else (1, 1)
    return pl.pallas_call(
        forward_kernel,
        grid=(1,),
        in_specs=[
            full(tokens, width),
            pl.BlockSpec((lead, 3, per, width), lambda i: (0, 3, 0, 0)),
            pl.BlockSpec((lead, 1, per, width), lambda i: (0, 8, 0, 0)),
            full(tokens, 2 * HD),
            full(tokens, 2 * HD),
            full(tokens, 1),
            full(1, tokens),
            full(4, width),
            full(tokens, seqs),
            anywhere,
        ],
        out_specs=[anywhere] * 6
        + [full(tokens, 1), full(tokens, width), full(tokens, 1)]
        + [full(seqs, width)] * 2
        + [anywhere] * 3,
        out_shape=[shape((tokens, width), BF16)] * 5
        + [shape((tokens, width), F32), shape((tokens, 1), F32)] * 2
        + [shape((seqs, width), F32)] * 2
        + [shape((tokens, blocks * width), BF16)] * 3,
        scratch_shapes=[
            pltpu.VMEM((tokens, tokens), F32),
            pltpu.VMEM((2 * blocks, lead, per, width), BF16),
            pltpu.VMEM((blocks, *deep, per, width), BF16),
            pltpu.VMEM((blocks, 3, tokens, width), BF16),
            pltpu.VMEM((5, tokens, width), BF16),
            pltpu.VMEM((tokens, width), F32),
            pltpu.SemaphoreType.DMA((3 * blocks,)),
            pltpu.SemaphoreType.DMA((3 * blocks,)),
            pltpu.SemaphoreType.DMA((6,)),
        ],
        compiler_params=params(),
        cost_estimate=LONG,
    )(rows, pack, pack, cosine, sine, mark[:, None], mark[None, :], vectors, pool_t, pack)


def down_spec(pack, first=0):
    lead, chunks, per, width = pack.shape
    if lead == 1:
        return pl.BlockSpec((1, 1, per, width), lambda i, *p: (0, chunks - 4 + first + i, 0, 0))
    return pl.BlockSpec((lead // 4, 4, per, width), lambda i, *p: (first + i, 3, 0, 0))


def halves_kernel(rows_ref, att_ref, low_ref, act_ref, source_ref, source_down_ref,
                  keep_ref, send_ref, act_keep_ref, act_send_ref):
    step = pl.program_id(0)
    half = rows_ref.shape[1] // 2
    moved = joined(act_ref[...], reorder(source_down_ref[...]), 1, 0).astype(BF16)
    act_keep_ref[0] = moved[:, :half]
    act_send_ref[0] = moved[:, half:]
    for part, ref in enumerate((rows_ref, att_ref, low_ref)):

        @pl.when(step == part)
        def _(ref=ref):
            moved = joined(ref[...], reorder(source_ref[...]), 1, 0).astype(BF16)
            keep_ref[0] = moved[:, :half]
            send_ref[0] = moved[:, half:]


def halves(rows, attended, low, active, source, source_down):
    tokens, width = rows.shape
    blocks = active.shape[1] // width
    full = lambda *dims: pl.BlockSpec(dims, lambda i: (0,) * len(dims))
    three = pl.BlockSpec((1, tokens, width // 2), lambda i: (jnp.minimum(i, 2), 0, 0))
    four = pl.BlockSpec((1, tokens, width // 2), lambda i: (i, 0, 0))
    shape = jax.ShapeDtypeStruct
    return pl.pallas_call(
        halves_kernel,
        grid=(blocks,),
        in_specs=[full(tokens, width)] * 3
        + [pl.BlockSpec((tokens, width), lambda i: (0, i)), full(1, width), full(1, width)],
        out_specs=[three, three, four, four],
        out_shape=[shape((3, tokens, width // 2), BF16)] * 2
        + [shape((blocks, tokens, width // 2), BF16)] * 2,
        compiler_params=params(),
        cost_estimate=LONG,
    )(rows, attended, low, active, source, source_down)


def lse(values, axis):
    top = jnp.max(values, axis=axis, keepdims=True)
    return top + jnp.log(jnp.sum(jnp.exp(values - top), axis=axis, keepdims=True))


def loss_kernel(
    every_ref, match_ref, own_match_ref, tower_ref, emb_ref, pooled_ref, pool_ref, unit_ref,
    scale_ref, vec_ref, *refs,
):
    loss_ref, mid_ref, low_ref, sums_ref = refs[-4:]
    total = every_ref.shape[0] // 2
    queries = every_ref[0:total, :]
    documents = every_ref[total : 2 * total, :]
    similar = joined_high(queries, documents, 1, 1) / TEMPER
    flipped = joined_high(documents, queries, 1, 1) / TEMPER
    row_log = lse(similar, 1)
    loss = (
        0.5 * (jnp.sum(row_log, keepdims=True) + jnp.sum(lse(similar, 0), keepdims=True))
        - jnp.sum(similar * match_ref[...], keepdims=True)
    ) / total
    loss_ref[...] = loss
    first = tower_ref[...] == 0
    others = jnp.where(first, documents, queries)
    other_log = jnp.where(first, lse(similar, 0), lse(flipped, 0))
    own = joined_high(emb_ref[...], others, 1, 1) / TEMPER
    grad_similar = (
        0.5 * (jnp.exp(own - lse(own, 1)) + jnp.exp(own - other_log)) - own_match_ref[...]
    ) / total
    grad_unit = joined_high(grad_similar, others, 1, 0) / TEMPER
    pooled = pooled_ref[...]
    inverse = lax.rsqrt(jnp.sum(pooled * pooled, axis=-1, keepdims=True) + EPS_UNIT)
    along = jnp.sum(pooled * grad_unit, axis=-1, keepdims=True)
    grad_pooled = inverse * grad_unit - inverse * inverse * inverse * pooled * along
    grad_second = sum(
        pool_ref[:, s : s + 1] * grad_pooled[s : s + 1, :] for s in range(grad_pooled.shape[0])
    )
    mid, gain, bias = norm_back(grad_second, unit_ref[...], scale_ref[...], vec_ref[2:3, :])
    mid_ref[...] = mid
    low_ref[...] = mid.astype(BF16)
    sums_ref[0:1, :] = gain
    sums_ref[1:2, :] = bias


def loss_and_grad(
    everyone, pos_doc, tower_index, dp_index, emb, pooled, pool_t, units, scaling, vectors, after
):
    tokens = units.shape[0]
    total = everyone.shape[0] // 2
    seqs, width = emb.shape
    match = (pos_doc[:, None] == jnp.arange(total, dtype=jnp.int32)[None, :]).astype(F32)
    oriented = jnp.where(tower_index == 0, match, match.T)
    own_match = lax.dynamic_slice_in_dim(oriented, dp_index * seqs, seqs, 0)
    shape = jax.ShapeDtypeStruct
    return pl.pallas_call(
        loss_kernel,
        in_specs=[whole_spec()] * 10 + [pl.BlockSpec(memory_space=pl.ANY)] * len(after),
        out_specs=[whole_spec()] * 4,
        out_shape=[shape((1, 1), F32), shape((tokens, width), F32), shape((tokens, width), BF16),
                   shape((2, width), F32)],
        compiler_params=params(30),
        cost_estimate=LONG,
    )(everyone, match, own_match, tower_index.reshape(1, 1), emb, pooled, pool_t, units, scaling,
      vectors, *after)


def gates_kernel(fast, branch_ref, mid_ref, act1_ref, act2_ref, unit_ref, scale_ref, vec_ref,
                 two_ref, source_ref, wgate_ref, wup_ref, wdown_ref,
                 grads_ref, hid_ref, attn_ref, sums_ref, *refs):
    acc_ref = refs[-1]
    step = pl.program_id(0)
    tokens, width = mid_ref.shape
    grad_active = joined(branch_ref[...], wdown_ref[...].reshape(width, width), 1, 1)
    grad_gate = (grad_active * act1_ref[...].astype(F32)).astype(BF16)
    grad_up = (grad_active * act2_ref[...].astype(F32)).astype(BF16)
    grads_ref[0, 0] = grad_gate
    grads_ref[1, 0] = grad_up
    back = joined(grad_gate, wgate_ref[:, 0].reshape(width, width), 1, 1) + joined(
        grad_up, wup_ref[:, 0].reshape(width, width), 1, 1
    )

    @pl.when(step == 0)
    def _():
        acc_ref[...] = mid_ref[...] + back

    @pl.when(step > 0)
    def _():
        acc_ref[...] += back

    @pl.when(step == pl.num_programs(0) - 1)
    def _():
        grad_hidden, gain, bias = norm_back(
            acc_ref[...], unit_ref[...], scale_ref[...], vec_ref[0:1, :]
        )
        hid_ref[...] = grad_hidden
        attn_ref[0:tokens, :] = grad_hidden.astype(BF16)
        if fast:
            values = jnp.concatenate([gain, bias, two_ref[...]], axis=0)
            upper = values.astype(BF16).astype(F32)
            blank = jnp.zeros((8, width), F32)
            parts = jnp.concatenate([upper, values - upper, blank], axis=0).astype(BF16)
            moved = joined(parts, reorder(source_ref[...]), 1, 0).astype(BF16)
            attn_ref[tokens:, :] = moved
        else:
            sums_ref[0:1, :] = gain
            sums_ref[1:2, :] = bias


def gates_back(fast, source, branch, mid, to_gate, to_up, units, scaling, vectors, sums_two, pack):
    tokens, width = mid.shape
    lead, _, per, _ = pack.shape
    blocks = 4
    shape = jax.ShapeDtypeStruct
    full = lambda *dims: pl.BlockSpec(dims, lambda i: (0,) * len(dims))
    flat = full(tokens, width)
    column = pl.BlockSpec((tokens, width), lambda i: (0, i))
    rows = tokens + (16 if fast else 0)
    return pl.pallas_call(
        lambda *refs: gates_kernel(fast, *refs),
        grid=(blocks,),
        in_specs=[flat, flat, column, column, flat, full(tokens, 1), full(4, width),
                  full(2, width), full(1, width),
                  pl.BlockSpec((lead, 1, per, width), lambda i: (0, i, 0, 0)),
                  pl.BlockSpec((lead, 1, per, width), lambda i: (0, 4 + i, 0, 0)),
                  down_spec(pack)],
        out_specs=[pl.BlockSpec((2, 1, tokens, width), lambda i: (0, i, 0, 0)), flat,
                   full(rows, width), full(2, width)],
        out_shape=[shape((2, blocks, tokens, width), BF16), shape((tokens, width), F32),
                   shape((rows, width), BF16), shape((2, width), F32)],
        scratch_shapes=[pltpu.VMEM((tokens, width), F32)],
        compiler_params=params(30),
        cost_estimate=LONG,
    )(branch, mid, to_gate, to_up, units, scaling, vectors, sums_two, source, pack, pack, pack)


def attend_back_kernel(
    wout_ref, cos_ref, sin_ref, mark_ref, markt_ref, q_ref, k_ref, v_ref, grad_ref, *refs
):
    mixed_ref, bias_ref, gatt_ref = refs[-3:]
    tokens, width = q_ref.shape
    pair = 2 * HD
    cosine, sine = cos_ref[...], sin_ref[...]
    bias_ref[...] = jnp.where(mark_ref[...] == markt_ref[...], 0.0, MASKED)
    gatt_ref[...] = joined(grad_ref[...], wout_ref[:, 0].reshape(width, width), 1, 1).astype(BF16)
    first_half = lax.broadcasted_iota(jnp.int32, (tokens, pair), 1) < HD
    for at in range(0, width, pair):
        query = q_ref[:, at : at + pair]
        key = k_ref[:, at : at + pair]
        value = v_ref[:, at : at + pair]
        grad_out = gatt_ref[:, at : at + pair]
        found = []
        for half in range(2):
            inside = first_half if half == 0 else jnp.logical_not(first_half)
            scores = (
                joined(jnp.where(inside, key, jnp.zeros_like(key)), query, 1, 1) * HD**-0.5
                + bias_ref[...]
            )
            raised = jnp.exp(scores - jnp.max(scores, axis=0, keepdims=True))
            probs = raised * (1.0 / jnp.sum(raised, axis=0, keepdims=True))
            grad_probs = joined(
                jnp.where(inside, value, jnp.zeros_like(value)), grad_out, 1, 1
            )
            delta = jnp.sum(probs * grad_probs, axis=0, keepdims=True)
            grad_scores = (probs * (grad_probs - delta)).astype(BF16)
            found.append(
                (
                    joined(grad_scores, key, 0, 0),
                    joined(grad_scores, query, 1, 0),
                    joined(probs.astype(BF16), grad_out, 1, 0),
                )
            )
        grad_query = jnp.where(first_half, found[0][0], found[1][0]) * HD**-0.5
        grad_key = jnp.where(first_half, found[0][1], found[1][1]) * HD**-0.5
        grad_value = jnp.where(first_half, found[0][2], found[1][2])
        mixed_ref[0, :, at : at + pair] = (
            grad_query * cosine - partner(grad_query) * sine
        ).astype(BF16)
        mixed_ref[1, :, at : at + pair] = (
            grad_key * cosine - partner(grad_key) * sine
        ).astype(BF16)
        mixed_ref[2, :, at : at + pair] = grad_value.astype(BF16)


def attend_back(pack, cosine, sine, labels, query, key, value, grad, after=()):
    tokens, width = query.shape
    lead, _, per, _ = pack.shape
    full = lambda *dims: pl.BlockSpec(dims, lambda i: (0,) * len(dims))
    flat = full(tokens, width)
    mark = labels.astype(F32)
    return pl.pallas_call(
        attend_back_kernel,
        grid=(1,),
        in_specs=[pl.BlockSpec((lead, 1, per, width), lambda i: (0, 8, 0, 0)),
                  full(tokens, 2 * HD), full(tokens, 2 * HD), full(tokens, 1), full(1, tokens)]
        + [flat] * 4 + [pl.BlockSpec(memory_space=pl.ANY)] * len(after),
        out_specs=full(3, tokens, width),
        out_shape=jax.ShapeDtypeStruct((3, tokens, width), BF16),
        scratch_shapes=[pltpu.VMEM((tokens, tokens), F32), pltpu.VMEM((tokens, width), BF16)],
        compiler_params=params(30),
        cost_estimate=LONG,
    )(pack, cosine, sine, mark[:, None], mark[None, :], query, key, value, grad, *after)


def tokens_kernel(mixed_ref, hid_ref, wqkv_ref, *refs):
    tokens, width = hid_ref.shape
    back = hid_ref[...]
    for part in range(3):
        back += joined(mixed_ref[part], wqkv_ref[:, part].reshape(width, width), 1, 1)
    refs[-1][...] = back


def tokens_back(mixed, hidden, pack, after=()):
    tokens, width = hidden.shape
    lead, _, per, _ = pack.shape
    full = lambda *dims: pl.BlockSpec(dims, lambda i: (0,) * len(dims))
    return pl.pallas_call(
        tokens_kernel,
        grid=(1,),
        in_specs=[full(3, tokens, width), full(tokens, width),
                  pl.BlockSpec((lead, 3, per, width), lambda i: (0, 3, 0, 0))]
        + [pl.BlockSpec(memory_space=pl.ANY)] * len(after),
        out_specs=full(tokens, width),
        out_shape=jax.ShapeDtypeStruct((tokens, width), F32),
        compiler_params=params(),
        cost_estimate=LONG,
    )(mixed, hidden, pack, *after)


def both(own_left, got_left, own_right, got_right):
    return (joined(own_left, own_right, 0, 0) + joined(got_left, got_right, 0, 0)).astype(BF16)


def steps_call(kernel, grid, ins, args, outs, shapes, scalars=None, after=()):
    ins = ins + [pl.BlockSpec(memory_space=pl.ANY)] * len(after)
    shapes = [jax.ShapeDtypeStruct(dims, BF16) for dims in shapes]
    more = dict(out_shape=shapes, compiler_params=params(30), cost_estimate=LONG)
    if scalars is None:
        return pl.pallas_call(
            kernel, grid=grid, in_specs=ins, out_specs=outs, **more
        )(*args, *after)
    return pl.pallas_call(
        kernel,
        grid_spec=pltpu.PrefetchScalarGridSpec(
            num_scalar_prefetch=1, grid=grid, in_specs=ins, out_specs=outs
        ),
        **more,
    )(scalars, *args, *after)


def down_kernel(own_ref, got_ref, grad_ref, got_grad_ref, *refs):
    held_ref, moving_ref = refs[-2:]
    value = both(own_ref[0], got_ref[0], grad_ref[...], got_grad_ref[...])
    half = value.shape[0] // 2
    held_ref[0] = value[:half]
    moving_ref[0] = value[half:]


def down_grads(own, got, grad, got_grad, after=()):
    blocks, tokens, rows = own.shape
    width = grad.shape[1]
    left = pl.BlockSpec((1, tokens, rows), lambda i: (i, 0, 0))
    right = pl.BlockSpec((tokens, width), lambda i: (0, 0))
    out = pl.BlockSpec((1, rows // 2, width), lambda i: (i, 0, 0))
    dims = (blocks, rows // 2, width)
    return steps_call(
        down_kernel, (blocks,), [left, left, right, right], (own, got, grad, got_grad),
        [out, out], [dims, dims], after=after,
    )


def first_kernel(own_ref, got_ref, grad_ref, got_grad_ref, *refs):
    held_ref, moving_ref = refs[-2:]
    value = both(own_ref[0], got_ref[0], grad_ref[0, 0], got_grad_ref[0, 0])
    half = value.shape[0] // 2
    held_ref[...] = value[:half].reshape(held_ref.shape)
    moving_ref[...] = value[half:].reshape(held_ref.shape)


def first_grads(own, got, grads, got_grads, which, part, after=()):
    _, tokens, rows = own.shape
    _, chunks, _, width = grads.shape
    left = pl.BlockSpec((1, tokens, rows), lambda i: (part, 0, 0))
    right = pl.BlockSpec((1, 1, tokens, width), lambda i: (which, i, 0, 0))
    out = pl.BlockSpec((4, 1, rows // 8, width), lambda i: (0, i, 0, 0))
    dims = (4, chunks, rows // 8, width)
    return steps_call(
        first_kernel, (chunks,), [left, left, right, right], (own, got, grads, got_grads),
        [out, out], [dims, dims], after=after,
    )


def tower_kernel(tower_ref, own_ref, got_ref, grad_ref, got_grad_ref, *refs):
    held_ref, lent_ref = refs[-2:]
    value = both(own_ref[0], got_ref[0], grad_ref[0, 0], got_grad_ref[0, 0])
    value = value.reshape(held_ref.shape)
    here = pl.program_id(0) < pl.num_programs(0) // 2

    @pl.when(here)
    def _():
        held_ref[...] = value

    @pl.when(jnp.logical_not(here))
    def _():
        lent_ref[...] = value


def tower_grads(tower, own, got, grads, got_grads, which, chunks, first, part, after=()):
    _, tokens, rows = own.shape
    width = grads.shape[-1]
    half = chunks // 2
    left = pl.BlockSpec((1, tokens, rows), lambda i, t: (part, 0, 0))
    right = pl.BlockSpec(
        (1, 1, tokens, width), lambda i, t: (which, first + (i + half * t[0]) % chunks, 0, 0)
    )
    block = (2, 4, 1, rows // 8, width)
    dims = (2, 4, half, rows // 8, width)
    outs = [
        pl.BlockSpec(block, lambda i, t: (0, 0, jnp.minimum(i, half - 1), 0, 0)),
        pl.BlockSpec(block, lambda i, t: (0, 0, jnp.maximum(i - half, 0), 0, 0)),
    ]
    return steps_call(
        tower_kernel, (chunks,), [left, left, right, right], (own, got, grads, got_grads),
        outs, [dims, dims], scalars=tower, after=after,
    )


def rest_kernel(own_ref, got_ref, attn_ref, got_attn_ref, mixed_ref, got_mixed_ref, *refs):
    held_ref, moving_ref = refs[-2:]
    tokens, width = mixed_ref.shape[1:]
    half = width // 4
    pieces = [
        both(own_ref[1], got_ref[1], attn_ref[0:tokens, :], got_attn_ref[0:tokens, :]),
        both(own_ref[0], got_ref[0], mixed_ref[0], got_mixed_ref[0]),
    ]
    parts = attn_ref[tokens:, : width // 2].astype(F32)
    got = got_attn_ref[tokens:, width // 2 :].astype(F32)
    values = parts[0:4] + parts[4:8] + got[0:4] + got[4:8]
    upper = values.astype(BF16).astype(F32)
    blank = jnp.zeros((PAD - 2 * VECTORS, width // 2), F32)
    pieces.append(jnp.concatenate([upper, values - upper, blank], axis=0).T.astype(BF16))
    at = 0
    for piece in pieces:
        columns = piece.shape[1]
        for k, out_ref in enumerate((held_ref, moving_ref)):
            out_ref[:, :, at : at + columns] = piece[k * 2 * half // 2 : (k + 1) * half].reshape(
                4, -1, columns
            )
        at += columns


def rest_grads(own, got, attn, got_attn, mixed, got_mixed, after=()):
    _, tokens, rows = own.shape
    width = mixed.shape[2]
    full = lambda *dims: pl.BlockSpec(dims, lambda i: (0,) * len(dims))
    one = pl.BlockSpec((1, tokens, width), lambda i: (0, 0, 0))
    dims = (4, rows // 8, 2 * width + PAD)
    return steps_call(
        rest_kernel, (1,),
        [full(*own.shape), full(*own.shape), full(*attn.shape), full(*attn.shape), one, one],
        (own, got, attn, got_attn, mixed, got_mixed),
        [full(*dims)] * 2, [dims, dims], after=after,
    )


def reduce_digit(parts, sizes, place, digit):
    size = sizes[place]
    total = pick(parts, 0, digit).astype(F32)
    for shift in range(1, size):
        sent = pick(parts, 0, (digit + shift) % size).astype(BF16)
        total += lax.ppermute(sent, "dp", digit_shift(sizes, place, shift)).astype(F32)
    return total


def shared_sum(grad, sizes, digits, tower_index):
    rows, columns = grad.shape
    count = math.prod(sizes)
    per = rows // count
    tiles = columns // 128
    side = max(1, round(tiles * 0.3)) * 128
    middle = columns - 2 * side
    last = len(sizes) - 1
    blocks = grad.astype(BF16).reshape(count // sizes[last], sizes[last], per, columns)
    chip = reduce_digit(jnp.moveaxis(blocks, 1, 0), sizes, last, digits[last]).astype(BF16)
    lead = chip.shape[0]
    mine = lax.dynamic_slice(chip, (0, 0, tower_index * (columns - side)), (lead, per, side))
    other = lax.dynamic_slice(
        chip, (0, 0, (1 - tower_index) * (columns - side)), (lead, per, side)
    )
    mine = mine.astype(F32) + lax.ppermute(other, "tower", SWAP).astype(F32)
    part = jnp.concatenate([mine.astype(BF16), chip[:, :, side : side + middle]], axis=2)
    for place in range(last - 1, -1, -1):
        size = sizes[place]
        part = jnp.moveaxis(part.reshape(part.shape[0] // size, size, per, side + middle), 1, 0)
        part = reduce_digit(part, sizes, place, digits[place]).astype(BF16)
    part = part[0]
    back = lax.ppermute(part, "tower", SWAP).astype(F32)
    part = part.astype(F32)
    centre = part[:, side:] + back[:, side:]
    first = tower_index == 0
    return jnp.concatenate(
        [
            jnp.where(first, part[:, :side], back[:, :side]),
            centre,
            jnp.where(first, back[:, :side], part[:, :side]),
        ],
        axis=1,
    )


def plus_kernel(jobs, count, z_ref, *refs):
    for out_ref, (terms, vectors) in zip(refs[count:], jobs, strict=True):
        total = None
        for place, index in terms:
            piece = refs[place][index(z_ref[0]) if callable(index) else index].astype(F32)
            total = piece if total is None else total + piece
        total = total.reshape(out_ref.shape)
        if vectors:
            at = total.shape[-1] - PAD
            parts = total[..., at:].reshape(-1, PAD)
            lane = lax.broadcasted_iota(jnp.int32, parts.shape, 1)
            values = parts + pltpu.roll(parts, PAD - VECTORS, 1)
            upper = values.astype(BF16).astype(F32)
            lower = pltpu.roll(values - upper, VECTORS, 1)
            parts = jnp.where(lane < VECTORS, upper, jnp.where(lane < 2 * VECTORS, lower, 0.0))
            out_ref[..., :at] = total[..., :at].astype(BF16)
            out_ref[..., at:] = parts.astype(BF16).reshape(*out_ref.shape[:-1], PAD)
        else:
            out_ref[...] = total.astype(BF16)


def plus(jobs, z, after=()):
    inputs, outs, shapes = [], [], []
    for arrays, plan, dims, vectors in jobs:
        base = len(inputs)
        inputs += arrays
        outs += [([(base + place, index) for place, index in terms], vectors) for terms in plan]
        shapes += dims
    count = len(inputs)
    spec = lambda dims: pl.BlockSpec(dims, lambda i: (0,) * len(dims))
    return pl.pallas_call(
        lambda *refs: plus_kernel(
            outs, count, *refs[: 1 + count], *refs[1 + count + len(after) :]
        ),
        grid=(1,),
        in_specs=[pl.BlockSpec(memory_space=pltpu.SMEM)]
        + [spec(a.shape) for a in inputs]
        + [pl.BlockSpec(memory_space=pl.ANY)] * len(after),
        out_specs=[spec(dims) for dims in shapes],
        out_shape=[jax.ShapeDtypeStruct(dims, BF16) for dims in shapes],
        compiler_params=params(24),
        cost_estimate=SHORT,
    )(z, *inputs, *after)


class GradSum:
    def __init__(self, pair, sizes, z, by_tower, direct, vectors=False):
        self.sizes = sizes
        self.z = z
        self.direct = direct
        self.vectors = vectors
        self.by_tower = by_tower
        self.held, sent = pair
        self.got = lax.ppermute(sent, "tower", SWAP) if by_tower else self.shift_y(sent)
        self.steps = ["tower", "y", "z"] if by_tower else ["y", "z"]

    def shift_y(self, sent):
        return lax.ppermute(sent, "dp", digit_shift(self.sizes, 1, 1))

    def job(self):
        step = self.steps[0]
        if step == "tower":
            plan = [[(0, (k,)), (1, (k,))] for k in (1, 0)]
            return [self.held, self.got], plan, [self.held.shape[1:]] * 2, self.vectors
        depth = self.sizes[0]
        if step == "y" and self.direct:
            views = [lambda z, k=k: ((z + k) % depth,) for k in (1, 2, 3, 0)]
            plan = [[(0, view), (1, view)] for view in views]
            return [self.held, self.got], plan, [self.held.shape[1:]] * depth, self.vectors
        if step == "y":
            plan = [[(0, (Ellipsis,)), (1, (Ellipsis,))]]
            return [self.held, self.got], plan, [self.held.shape], self.vectors
        if self.direct:
            plan = [[(k, (Ellipsis,)) for k in range(depth)]]
            return [self.held, *self.got], plan, [self.held.shape], self.vectors
        plan = [[(0, (k,)) for k in range(depth)]]
        return [self.got], plan, [self.got.shape[1:]], self.vectors

    def take(self, outs):
        step = self.steps.pop(0)
        if step == "tower":
            moving, self.held = outs
            self.got = self.shift_y(moving)
        elif step == "y" and self.direct:
            *parts, self.held = outs
            self.got = [
                lax.ppermute(part, "dp", digit_shift(self.sizes, 0, k + 1))
                for k, part in enumerate(parts)
            ]
        elif step == "y":
            depth, rest = self.sizes[0], math.prod(self.sizes[1:])
            groups = [[z * rest + other for z in range(depth)] for other in range(rest)]
            self.got = lax.all_to_all(outs[0], "dp", 0, 0, axis_index_groups=groups, tiled=True)
        else:
            (self.held,) = outs
            self.got = lax.ppermute(self.held, "tower", SWAP)

    def result(self, tower_index):
        first = tower_index == 0
        return jnp.where(first, self.held, self.got), jnp.where(first, self.got, self.held)


def advance(order, *sums, done=()):
    jobs = [one.job() for one in sums]
    outs = plus(jobs, sums[0].z, (order, *(one.got for one in done)))
    last = outs[-1]
    for one, (_, plan, _, _) in zip(sums, jobs, strict=True):
        one.take(outs[: len(plan)])
        outs = outs[len(plan) :]
    return last


def sum_norms(sums_one, sums_two, dp_count):
    sums = jnp.concatenate([sums_one, sums_two], axis=0)
    sums = sums.reshape(4, dp_count, -1).transpose(1, 0, 2)
    sums = jnp.concatenate([sums, sums], axis=0)
    return jnp.sum(lax.all_to_all(sums, ("tower", "dp"), 0, 0, tiled=True), axis=0)


def finish_kernel(plan, count, *refs):
    for out_ref, terms in zip(refs[count:], plan, strict=True):
        for to, places, index in terms:
            total = refs[places[0]][index].astype(F32)
            for place in places[1:]:
                total += refs[place][index].astype(F32)
            out_ref[to] = total


def finish(inputs, plan, shapes, after=()):
    count = len(inputs)
    spec = lambda dims: pl.BlockSpec(dims, lambda i: (0,) * len(dims))
    return pl.pallas_call(
        lambda *refs: finish_kernel(plan, count, *refs[:count], *refs[count + len(after) :]),
        grid=(1,),
        in_specs=[spec(a.shape) for a in inputs]
        + [pl.BlockSpec(memory_space=pl.ANY)] * len(after),
        out_specs=[spec(dims) for dims in shapes],
        out_shape=[jax.ShapeDtypeStruct(dims, F32) for dims in shapes],
        compiler_params=params(24),
        cost_estimate=SHORT,
    )(*inputs, *after)


def beside(chunks):
    return jnp.concatenate(list(chunks), axis=1)


def column_orders(digits, per, spread, width):
    _, y, c = digits
    place = jnp.arange(width, dtype=jnp.int32)
    block, row = place // per, place % per
    core, dy, z = block // 8, block // 4 % 2, block % 4
    source = ((z * 4 + (dy + y) % 2 * 2 + (core + c) % 2)) * per + row
    device = (dy + y) % 2 * 2 + (core + c) % 2
    return source[None], ((device * spread + block % 4) * per + row)[None]


def body(
    tokens,
    lengths,
    pos_doc,
    w_qkv,
    w_out,
    w_gate,
    w_up,
    w_down,
    ln1_gain,
    ln1_bias,
    ln2_gain,
    ln2_bias,
):
    dp_count = lax.axis_size("dp")
    device_count = 2 * dp_count
    sizes = split_dp(dp_count)
    dp_index = lax.axis_index("dp")
    tower_index = lax.axis_index("tower")
    digits = digits_of(dp_index, sizes)
    per, narrow = w_out.shape
    wide = w_gate.shape[1]
    spread = wide // narrow

    own_pack = pack_own(w_gate, w_up, w_out, w_qkv, w_down)
    pack = lax.all_gather(own_pack, "dp", axis=0, tiled=True)
    pack = pack.reshape(dp_count, 4 * spread, per, narrow)
    if per % 16:
        front = pack[:, : 3 * spread].transpose(1, 0, 2, 3).reshape(3 * spread, narrow, narrow)
        back = pack[:, 3 * spread :].reshape(spread, narrow, narrow)
        pack = jnp.concatenate([front, back], axis=0)[None]
    vectors_own = jnp.stack([ln1_gain, ln1_bias, ln2_gain, ln2_bias])
    vectors = lax.all_to_all(
        jnp.broadcast_to(vectors_own[None], (dp_count, 4, per)), "dp", 0, 0, tiled=True
    )
    vectors = vectors.transpose(1, 0, 2).reshape(4, narrow).astype(F32)

    rows_in = tokens[0]
    row_count = rows_in.shape[0]
    pooling, labels, offsets = layout(lengths[0], row_count)
    pool_t = pooling.T
    cosine, sine = rotary_tables(offsets)

    fast = sizes == [4, 2, 2] and spread == 4 and per % 16 == 0
    source, source_down = column_orders(digits, per, spread, narrow) if fast else (
        jnp.zeros((1, narrow), jnp.int32),
    ) * 2
    core_swap = digit_shift(sizes, len(sizes) - 1, 1)
    swap_cores = lambda values: lax.ppermute(values, "dp", core_swap)
    (query, key, value, attended, first_low, unit_one, scale_one, unit_two, scale_two, pooled,
     unit_vectors, active, to_gate, to_up) = forward(
        rows_in, pack, cosine, sine, labels, vectors, pool_t
    )
    seq_count = unit_vectors.shape[0]
    everyone = lax.all_to_all(
        jnp.broadcast_to(unit_vectors[None], (device_count,) + unit_vectors.shape),
        ("tower", "dp"),
        0,
        0,
        tiled=True,
    ).reshape(device_count * seq_count, narrow)
    if fast:
        own, lent, own_active, lent_active = halves(
            rows_in, attended, first_low, active, source, source_down
        )
    loss_value, grad_mid, grad_branch, sums_two = loss_and_grad(
        everyone, pos_doc, tower_index, dp_index, unit_vectors, pooled, pool_t, unit_two, scale_two,
        vectors, (own,) if fast else (),
    )
    grad_feed, grad_hidden, grad_attn, sums_one = gates_back(
        fast, source, grad_branch, grad_mid, to_gate, to_up, unit_one, scale_one, vectors, sums_two,
        pack,
    )
    heads_args = (pack, cosine, sine, labels, query, key, value, grad_attn)
    if fast:
        got, got_active = swap_cores(lent), swap_cores(lent_active)
        got_branch = swap_cores(grad_branch)
        got_feed = swap_cores(grad_feed)
        got_attn = swap_cores(grad_attn)
        tower = tower_index.reshape(1).astype(jnp.int32)
        plain = lambda pair, **how: GradSum(pair, sizes, digits[0].reshape(1), **how)
        sums, order, late = {}, grad_hidden, []
        for step in ORDER:
            after = (order,)
            if step == "down":
                pair = down_grads(own_active, got_active, grad_branch, got_branch, after)
                sums["d"] = plain(pair, by_tower=False, direct="d" in DIRECT)
                order = pair[0]
            elif step == "heads":
                grad_mixed = attend_back(*heads_args, (order, got_attn))
                got_mixed = swap_cores(grad_mixed)
                order = grad_mixed
            elif step == "gate":
                pair = tower_grads(tower, own, got, grad_feed, got_feed, 0, 4, 0, 2, after)
                sums["g"] = plain(pair, by_tower=True, direct="g" in DIRECT)
                order = pair[0]
            elif step == "up":
                pair = first_grads(own, got, grad_feed, got_feed, 1, 2, after)
                sums["u"] = plain(pair, by_tower=False, direct="u" in DIRECT)
                order = pair[0]
            elif step == "rest":
                pair = rest_grads(own, got, grad_attn, got_attn, grad_mixed, got_mixed, after)
                sums["r"] = plain(pair, by_tower=False, direct="r" in DIRECT, vectors=True)
                order = pair[0]
            elif step == "last":
                pair = tower_grads(
                    tower, own, got, grad_mixed[None], got_mixed[None], 0, 2, 1, 0, after
                )
                sums["l"] = plain(pair, by_tower=True, direct="l" in DIRECT)
                order = pair[0]
            elif step == "tokens":
                grad_rows = order = tokens_back(grad_mixed, grad_hidden, pack, after)
            else:
                ready = [one for one in late if one.age > 0]
                late = [one for one in late if one.age == 0]
                for one in late:
                    one.age += 1
                moving = [sums[name] for name in step]
                order = advance(order, *moving, done=ready)
                for one in moving:
                    if not one.steps:
                        one.age = 0
                        late.append(one)
        down, gate, up, rest, last = (sums[name] for name in "dgurl")
        columns = lambda k: (slice(None), slice(k * narrow, (k + 1) * narrow))
        sum_down, sum_up = finish(
            [down.held, down.got, up.held, up.got],
            [
                [((Ellipsis,), (0, 1), (Ellipsis,))],
                [(columns(k), (2, 3), (k,)) for k in range(spread)],
            ],
            [down.held.shape, (per, wide)],
        )
        lower, upper = gate.result(tower_index)
        (sum_gate,) = finish(
            [lower, upper],
            [[(columns(k), (k // 2,), (k % 2,)) for k in range(spread)]],
            [(per, wide)],
        )
        key_value = last.result(tower_index)
        sum_out, sum_qkv, norms = finish(
            [rest.held, rest.got, *key_value],
            [
                [((Ellipsis,), (0, 1), columns(0))],
                [(columns(0), (0, 1), columns(1)), (columns(1), (2,), (0,)), (columns(2), (3,), (0,))],
                [((Ellipsis,), (0, 1), (slice(None), slice(2 * narrow, 2 * narrow + PAD)))],
            ],
            [(per, narrow), (per, 3 * narrow), (per, PAD)],
        )
        norms = norms.T
        sums = norms[:VECTORS] + norms[VECTORS : 2 * VECTORS]
    else:
        grad_mixed = attend_back(*heads_args)
        grad_rows = tokens_back(grad_mixed, grad_hidden, pack)
        grad_down = joined(active, grad_branch, 0, 0)
        down_rows = (
            grad_down.reshape(dp_count, spread, per, narrow)
            .transpose(0, 2, 1, 3)
            .reshape(narrow, wide)
        )
        share = lambda grad: shared_sum(grad, sizes, digits, tower_index)
        sum_down = share(down_rows).reshape(per, spread, narrow).transpose(1, 0, 2)
        sum_down = sum_down.reshape(wide // dp_count, narrow)
        sum_gate, sum_up = (
            share(joined(first_low, beside(grad_feed[k]), 0, 0)) for k in range(2)
        )
        sum_out = share(joined(attended, grad_attn, 0, 0))
        sum_qkv = share(joined(rows_in, beside(grad_mixed), 0, 0))
        sums = sum_norms(sums_one, sums_two, dp_count)
    return (
        loss_value.reshape(()),
        unit_vectors[None],
        grad_rows[None],
        sum_qkv,
        sum_out,
        sum_gate,
        sum_up,
        sum_down,
        sums[0],
        sums[1],
        sums[2],
        sums[3],
    )


def solution(mesh):
    placed = (
        P("tower", "dp", None),
        P("tower", "dp"),
        P(),
        P("dp", None),
        P("dp", None),
        P("dp", None),
        P("dp", None),
        P("dp", None),
        P("dp"),
        P("dp"),
        P("dp"),
        P("dp"),
    )
    return jax.shard_map(
        body,
        mesh=mesh,
        in_specs=placed,
        out_specs=(
            P(),
            P("tower", "dp", None),
            P("tower", "dp", None),
            P("dp", None),
            P("dp", None),
            P("dp", None),
            P("dp", None),
            P("dp", None),
            P("dp"),
            P("dp"),
            P("dp"),
            P("dp"),
        ),
        check_vma=False,
    )
```

```python
import math

import jax
import jax.numpy as jnp
from jax import lax
from jax.experimental import pallas as pl
from jax.experimental.pallas import tpu as pltpu
from jax.sharding import PartitionSpec as P

HD = 64
PAD = 128
VECTORS = 4
TEMPER = 0.05
EPS_NORM = 1e-05
EPS_UNIT = 1e-06
MASKED = -1e30
F32 = jnp.float32
BF16 = jnp.bfloat16
MIB = 1 << 20
ORDER = (
    "down", "heads", "gate", "up", "d", "rest", "last", "g",
    "tokens", "u", "l", "d", "r", "g", "u", "l",
    "r", "l", "g",
)
DIRECT = "gulr"
LONG = pl.CostEstimate(flops=100000000000, bytes_accessed=100000000, transcendentals=0)
SHORT = pl.CostEstimate(flops=100000000000, bytes_accessed=100000000, transcendentals=0)


def joined(left_arr, right_arr, left_dim, right_dim):
    return lax.dot_general(
        left_arr,
        right_arr,
        (((left_dim,), (right_dim,)), ((), ())),
        preferred_element_type=F32,
    )


def joined_high(left_arr, right_arr, left_dim, right_dim):
    return lax.dot_general(
        left_arr,
        right_arr,
        (((left_dim,), (right_dim,)), ((), ())),
        precision=lax.Precision.HIGHEST,
        preferred_element_type=F32,
    )


def split_dp(count):
    sizes = [2] if count % 2 == 0 else []
    rest = count // 2 if sizes else count
    front = []
    while rest > 1:
        step = 4 if rest % 4 == 0 else (2 if rest % 2 == 0 else rest)
        front.append(step)
        rest //= step
    return front + sizes


def digit_shift(sizes, place, shift):
    stride = math.prod(sizes[place + 1 :])
    size = sizes[place]
    pairs = []
    for index in range(math.prod(sizes)):
        digit = index // stride % size
        pairs.append((index, index + ((digit + shift) % size - digit) * stride))
    return pairs


def digits_of(index, sizes):
    found = []
    for size in reversed(sizes):
        found.append(index % size)
        index = index // size
    return found[::-1]


SWAP = [(0, 1), (1, 0)]


def pick(array, axis, place):
    return lax.dynamic_index_in_dim(array, place, axis, keepdims=False)


def layout(seq_spans, row_count):
    seq_total = seq_spans.shape[0]
    starts = jnp.cumsum(seq_spans) - seq_spans
    places = jnp.arange(row_count, dtype=jnp.int32)
    member = (
        (places[None, :] >= starts[:, None]) & (places[None, :] < (starts + seq_spans)[:, None])
    ).astype(jnp.int32)
    labels = jnp.sum(member * jnp.arange(seq_total, dtype=jnp.int32)[:, None], axis=0)
    offsets = places - jnp.sum(member * starts[:, None], axis=0)
    pooling = member.astype(F32) / seq_spans.astype(F32)[:, None]
    return (pooling, labels, offsets)


def rotary_tables(offsets):
    half_size = HD // 2
    frequency = 1000.0 ** (-jnp.arange(half_size, dtype=F32) / half_size)
    angles = offsets.astype(F32)[:, None] * frequency[None, :]
    cosine, sine = jnp.cos(angles), jnp.sin(angles)
    return (
        jnp.concatenate([cosine] * 4, axis=1),
        jnp.concatenate([-sine, sine, -sine, sine], axis=1),
    )


def partner(values):
    lane = lax.broadcasted_iota(jnp.int32, values.shape, 1)
    return jnp.where(
        lane % HD < HD // 2, pltpu.roll(values, 96, 1), pltpu.roll(values, 32, 1)
    )


def reorder(source):
    count = source.shape[1]
    rows = lax.broadcasted_iota(jnp.int32, (count, count), 0)
    return jnp.where(rows == source, 1.0, 0.0).astype(BF16)


def unit_rows(values):
    centered = values - jnp.mean(values, axis=-1, keepdims=True)
    scaling = lax.rsqrt(jnp.mean(centered * centered, axis=-1, keepdims=True) + EPS_NORM)
    return centered * scaling, scaling


def norm_back(grad_rows, units, scaling, gain_row):
    along = grad_rows * gain_row
    back_rows = scaling * (
        along
        - jnp.mean(along, axis=-1, keepdims=True)
        - units * jnp.mean(along * units, axis=-1, keepdims=True)
    )
    return (
        back_rows,
        jnp.sum(grad_rows * units, axis=0, keepdims=True),
        jnp.sum(grad_rows, axis=0, keepdims=True),
    )


def whole_spec():
    return pl.BlockSpec(memory_space=pltpu.VMEM)


def params(mib=60):
    return pltpu.CompilerParams(vmem_limit_bytes=mib * MIB)


def pack_kernel(*refs):
    *weight_refs, out_ref = refs
    rows, width = weight_refs[2].shape
    to = 0
    for ref in weight_refs:
        count = ref.shape[0]
        for at in range(0, ref.shape[1], width):
            out_ref[to : to + count, :] = ref[:, at : at + width]
            to += count


def pack_own(*weights):
    rows, width = weights[2].shape
    if rows % 16:
        parts = [
            w[:, at : at + width] for w in weights[:-1] for at in range(0, w.shape[1], width)
        ]
        return jnp.concatenate(parts + [weights[-1]], axis=0)
    total = sum(w.size for w in weights) // width
    full = lambda *dims: pl.BlockSpec(dims, lambda i: (0,) * len(dims))
    return pl.pallas_call(
        pack_kernel,
        grid=(1,),
        in_specs=[full(*w.shape) for w in weights],
        out_specs=full(total, width),
        out_shape=jax.ShapeDtypeStruct((total, width), BF16),
        compiler_params=params(),
    )(*weights)


def attend_kernel(
    rows_ref, wqkv_ref, wout_ref, cos_ref, sin_ref, mark_ref, markt_ref, vec_ref,
    q_ref, k_ref, v_ref, att_ref, low_ref, unit_ref, scale_ref, bias_ref,
):
    rows = rows_ref[...]
    tokens, width = rows.shape
    pair = 2 * HD
    cosine, sine = cos_ref[...], sin_ref[...]
    bias_ref[...] = jnp.where(mark_ref[...] == markt_ref[...], 0.0, MASKED)
    for part, out_ref in enumerate((q_ref, k_ref, v_ref)):
        mixed = joined(rows, wqkv_ref[:, part].reshape(width, width), 1, 0)
        if part == 2:
            out_ref[...] = mixed.astype(BF16)
        else:
            for at in range(0, width, pair):
                piece = mixed[:, at : at + pair]
                turned = piece * cosine + partner(piece) * sine
                out_ref[:, at : at + pair] = turned.astype(BF16)
    first_half = lax.broadcasted_iota(jnp.int32, (tokens, pair), 1) < HD
    for at in range(0, width, pair):
        query = q_ref[:, at : at + pair]
        key = k_ref[:, at : at + pair]
        value = v_ref[:, at : at + pair]
        outs = []
        for half in range(2):
            inside = first_half if half == 0 else jnp.logical_not(first_half)
            only = jnp.where(inside, query, jnp.zeros_like(query))
            scores = joined(only, key, 1, 1) * HD**-0.5 + bias_ref[...]
            raised = jnp.exp(scores - jnp.max(scores, axis=-1, keepdims=True))
            total = jnp.sum(raised, axis=-1, keepdims=True)
            weights = (raised * (1.0 / total)).astype(BF16)
            outs.append(joined(weights, value, 1, 0))
        att_ref[:, at : at + pair] = jnp.where(first_half, outs[0], outs[1]).astype(BF16)
    hidden = rows.astype(F32) + joined(att_ref[...], wout_ref[:, 0].reshape(width, width), 1, 0)
    units, scaling = unit_rows(hidden)
    unit_ref[...] = units
    scale_ref[...] = scaling
    low_ref[...] = (units * vec_ref[0:1, :] + vec_ref[1:2, :]).astype(BF16)


def forward_kernel(
    rows_ref, wqkv_ref, wout_ref, cos_ref, sin_ref, mark_ref, markt_ref, vec_ref, pool_ref, pack_ref,
    q_out, k_out, v_out, att_out, low_out, unit1_out, scale1_ref, unit_ref, scale_ref, pooled_ref,
    emb_ref, act_ref, togate_ref, toup_ref,
    bias_ref, wide_ref, deep_ref, made_ref, heads_ref, unit1_ref, in_sem, out_sem, heads_sem,
):
    tokens, width = rows_ref.shape
    blocks, deep = deep_ref.shape[0], deep_ref.shape[1:3]
    chunks = pack_ref.shape[1]
    arriving = []
    for j in range(blocks):
        if deep[0] * blocks == pack_ref.shape[0]:
            below = pack_ref.at[pl.ds(j * deep[0], deep[0]), pl.ds(chunks - deep[1], deep[1])]
        else:
            below = pack_ref.at[:, pl.ds(chunks - blocks + j, 1)]
        pairs = (
            (pack_ref.at[:, j], wide_ref.at[j]),
            (pack_ref.at[:, blocks + j], wide_ref.at[blocks + j]),
            (below, deep_ref.at[j]),
        )
        arriving.append(
            [pltpu.make_async_copy(*pair, in_sem.at[3 * j + k]) for k, pair in enumerate(pairs)]
        )
    for copies in arriving:
        for copy in copies:
            copy.start()
    attend_kernel(
        rows_ref, wqkv_ref, wout_ref, cos_ref, sin_ref, mark_ref, markt_ref, vec_ref,
        *(heads_ref.at[k] for k in range(5)), unit1_ref, scale1_ref, bias_ref,
    )
    leaving = [
        pltpu.make_async_copy(heads_ref.at[k], out_ref, heads_sem.at[k])
        for k, out_ref in enumerate((q_out, k_out, v_out, att_out, low_out))
    ]
    leaving.append(pltpu.make_async_copy(unit1_ref, unit1_out, heads_sem.at[5]))
    for copy in leaving:
        copy.start()
    low = heads_ref[4]
    total = unit1_ref[...] * vec_ref[0:1, :] + vec_ref[1:2, :]
    for j in range(blocks):
        for copy in arriving[j]:
            copy.wait()
        gate = joined(low, wide_ref[j].reshape(width, width), 1, 0)
        up = joined(low, wide_ref[blocks + j].reshape(width, width), 1, 0)
        sig = 1.0 / (1.0 + jnp.exp(-gate))
        silu = gate * sig
        active = (silu * up).astype(BF16)
        made_ref[j, 0] = active
        made_ref[j, 1] = silu.astype(BF16)
        made_ref[j, 2] = (up * sig * (1.0 + gate * (1.0 - sig))).astype(BF16)
        for k, out_ref in enumerate((act_ref, toup_ref, togate_ref)):
            copy = pltpu.make_async_copy(
                made_ref.at[j, k], out_ref.at[:, pl.ds(j * width, width)], out_sem.at[3 * j + k]
            )
            copy.start()
            leaving.append(copy)
        total += joined(active, deep_ref[j].reshape(width, width), 1, 0)
    units, scaling = unit_rows(total)
    unit_ref[...] = units
    scale_ref[...] = scaling
    second = units * vec_ref[2:3, :] + vec_ref[3:4, :]
    rows = [
        jnp.sum(second * pool_ref[:, s : s + 1], axis=0, keepdims=True)
        for s in range(pool_ref.shape[1])
    ]
    pooled = jnp.concatenate(rows, axis=0)
    pooled_ref[...] = pooled
    emb_ref[...] = pooled * lax.rsqrt(jnp.sum(pooled * pooled, axis=-1, keepdims=True) + EPS_UNIT)
    for copy in leaving:
        copy.wait()


def forward(rows, pack, cosine, sine, labels, vectors, pool_t):
    tokens, width = rows.shape
    lead, _, per, _ = pack.shape
    blocks = 4
    seqs = pool_t.shape[1]
    shape = jax.ShapeDtypeStruct
    full = lambda *dims: pl.BlockSpec(dims, lambda i: (0,) * len(dims))
    anywhere = pl.BlockSpec(memory_space=pl.ANY)
    mark = labels.astype(F32)
    deep = (lead // 4, 4) if lead > 1 else (1, 1)
    return pl.pallas_call(
        forward_kernel,
        grid=(1,),
        in_specs=[
            full(tokens, width),
            pl.BlockSpec((lead, 3, per, width), lambda i: (0, 3, 0, 0)),
            pl.BlockSpec((lead, 1, per, width), lambda i: (0, 8, 0, 0)),
            full(tokens, 2 * HD),
            full(tokens, 2 * HD),
            full(tokens, 1),
            full(1, tokens),
            full(4, width),
            full(tokens, seqs),
            anywhere,
        ],
        out_specs=[anywhere] * 6
        + [full(tokens, 1), full(tokens, width), full(tokens, 1)]
        + [full(seqs, width)] * 2
        + [anywhere] * 3,
        out_shape=[shape((tokens, width), BF16)] * 5
        + [shape((tokens, width), F32), shape((tokens, 1), F32)] * 2
        + [shape((seqs, width), F32)] * 2
        + [shape((tokens, blocks * width), BF16)] * 3,
        scratch_shapes=[
            pltpu.VMEM((tokens, tokens), F32),
            pltpu.VMEM((2 * blocks, lead, per, width), BF16),
            pltpu.VMEM((blocks, *deep, per, width), BF16),
            pltpu.VMEM((blocks, 3, tokens, width), BF16),
            pltpu.VMEM((5, tokens, width), BF16),
            pltpu.VMEM((tokens, width), F32),
            pltpu.SemaphoreType.DMA((3 * blocks,)),
            pltpu.SemaphoreType.DMA((3 * blocks,)),
            pltpu.SemaphoreType.DMA((6,)),
        ],
        compiler_params=params(),
        cost_estimate=LONG,
    )(rows, pack, pack, cosine, sine, mark[:, None], mark[None, :], vectors, pool_t, pack)


def down_spec(pack, first=0):
    lead, chunks, per, width = pack.shape
    if lead == 1:
        return pl.BlockSpec((1, 1, per, width), lambda i, *p: (0, chunks - 4 + first + i, 0, 0))
    return pl.BlockSpec((lead // 4, 4, per, width), lambda i, *p: (first + i, 3, 0, 0))


def halves_kernel(rows_ref, att_ref, low_ref, act_ref, source_ref, source_down_ref,
                  keep_ref, send_ref, act_keep_ref, act_send_ref):
    step = pl.program_id(0)
    half = rows_ref.shape[1] // 2
    moved = joined(act_ref[...], reorder(source_down_ref[...]), 1, 0).astype(BF16)
    act_keep_ref[0] = moved[:, :half]
    act_send_ref[0] = moved[:, half:]
    for part, ref in enumerate((rows_ref, att_ref, low_ref)):

        @pl.when(step == part)
        def _(ref=ref):
            moved = joined(ref[...], reorder(source_ref[...]), 1, 0).astype(BF16)
            keep_ref[0] = moved[:, :half]
            send_ref[0] = moved[:, half:]


def halves(rows, attended, low, active, source, source_down):
    tokens, width = rows.shape
    blocks = active.shape[1] // width
    full = lambda *dims: pl.BlockSpec(dims, lambda i: (0,) * len(dims))
    three = pl.BlockSpec((1, tokens, width // 2), lambda i: (jnp.minimum(i, 2), 0, 0))
    four = pl.BlockSpec((1, tokens, width // 2), lambda i: (i, 0, 0))
    shape = jax.ShapeDtypeStruct
    return pl.pallas_call(
        halves_kernel,
        grid=(blocks,),
        in_specs=[full(tokens, width)] * 3
        + [pl.BlockSpec((tokens, width), lambda i: (0, i)), full(1, width), full(1, width)],
        out_specs=[three, three, four, four],
        out_shape=[shape((3, tokens, width // 2), BF16)] * 2
        + [shape((blocks, tokens, width // 2), BF16)] * 2,
        compiler_params=params(30),
        cost_estimate=LONG,
    )(rows, attended, low, active, source, source_down)


def lse(values, axis):
    top = jnp.max(values, axis=axis, keepdims=True)
    return top + jnp.log(jnp.sum(jnp.exp(values - top), axis=axis, keepdims=True))


def loss_kernel(
    every_ref, match_ref, own_match_ref, tower_ref, emb_ref, pooled_ref, pool_ref, unit_ref,
    scale_ref, vec_ref, *refs,
):
    loss_ref, mid_ref, low_ref, sums_ref = refs[-4:]
    total = every_ref.shape[0] // 2
    queries = every_ref[0:total, :]
    documents = every_ref[total : 2 * total, :]
    similar = joined_high(queries, documents, 1, 1) / TEMPER
    flipped = joined_high(documents, queries, 1, 1) / TEMPER
    row_log = lse(similar, 1)
    loss = (
        0.5 * (jnp.sum(row_log, keepdims=True) + jnp.sum(lse(similar, 0), keepdims=True))
        - jnp.sum(similar * match_ref[...], keepdims=True)
    ) / total
    loss_ref[...] = loss
    first = tower_ref[...] == 0
    others = jnp.where(first, documents, queries)
    other_log = jnp.where(first, lse(similar, 0), lse(flipped, 0))
    own = joined_high(emb_ref[...], others, 1, 1) / TEMPER
    grad_similar = (
        0.5 * (jnp.exp(own - lse(own, 1)) + jnp.exp(own - other_log)) - own_match_ref[...]
    ) / total
    grad_unit = joined_high(grad_similar, others, 1, 0) / TEMPER
    pooled = pooled_ref[...]
    inverse = lax.rsqrt(jnp.sum(pooled * pooled, axis=-1, keepdims=True) + EPS_UNIT)
    along = jnp.sum(pooled * grad_unit, axis=-1, keepdims=True)
    grad_pooled = inverse * grad_unit - inverse * inverse * inverse * pooled * along
    grad_second = sum(
        pool_ref[:, s : s + 1] * grad_pooled[s : s + 1, :] for s in range(grad_pooled.shape[0])
    )
    mid, gain, bias = norm_back(grad_second, unit_ref[...], scale_ref[...], vec_ref[2:3, :])
    mid_ref[...] = mid
    low_ref[...] = mid.astype(BF16)
    sums_ref[0:1, :] = gain
    sums_ref[1:2, :] = bias


def loss_and_grad(
    everyone, pos_doc, tower_index, dp_index, emb, pooled, pool_t, units, scaling, vectors, after
):
    tokens = units.shape[0]
    total = everyone.shape[0] // 2
    seqs, width = emb.shape
    match = (pos_doc[:, None] == jnp.arange(total, dtype=jnp.int32)[None, :]).astype(F32)
    oriented = jnp.where(tower_index == 0, match, match.T)
    own_match = lax.dynamic_slice_in_dim(oriented, dp_index * seqs, seqs, 0)
    shape = jax.ShapeDtypeStruct
    return pl.pallas_call(
        loss_kernel,
        in_specs=[whole_spec()] * 10 + [pl.BlockSpec(memory_space=pl.ANY)] * len(after),
        out_specs=[whole_spec()] * 4,
        out_shape=[shape((1, 1), F32), shape((tokens, width), F32), shape((tokens, width), BF16),
                   shape((2, width), F32)],
        compiler_params=params(30),
        cost_estimate=LONG,
    )(everyone, match, own_match, tower_index.reshape(1, 1), emb, pooled, pool_t, units, scaling,
      vectors, *after)


def gates_kernel(fast, branch_ref, mid_ref, act1_ref, act2_ref, unit_ref, scale_ref, vec_ref,
                 two_ref, source_ref, wgate_ref, wup_ref, wdown_ref,
                 grads_ref, hid_ref, attn_ref, sums_ref, *refs):
    acc_ref = refs[-1]
    step = pl.program_id(0)
    tokens, width = mid_ref.shape
    grad_active = joined(branch_ref[...], wdown_ref[...].reshape(width, width), 1, 1)
    grad_gate = (grad_active * act1_ref[...].astype(F32)).astype(BF16)
    grad_up = (grad_active * act2_ref[...].astype(F32)).astype(BF16)
    grads_ref[0, 0] = grad_gate
    grads_ref[1, 0] = grad_up
    back = joined(grad_gate, wgate_ref[:, 0].reshape(width, width), 1, 1) + joined(
        grad_up, wup_ref[:, 0].reshape(width, width), 1, 1
    )

    @pl.when(step == 0)
    def _():
        acc_ref[...] = mid_ref[...] + back

    @pl.when(step > 0)
    def _():
        acc_ref[...] += back

    @pl.when(step == pl.num_programs(0) - 1)
    def _():
        grad_hidden, gain, bias = norm_back(
            acc_ref[...], unit_ref[...], scale_ref[...], vec_ref[0:1, :]
        )
        hid_ref[...] = grad_hidden
        attn_ref[0:tokens, :] = grad_hidden.astype(BF16)
        if fast:
            values = jnp.concatenate([gain, bias, two_ref[...]], axis=0)
            upper = values.astype(BF16).astype(F32)
            blank = jnp.zeros((8, width), F32)
            parts = jnp.concatenate([upper, values - upper, blank], axis=0).astype(BF16)
            moved = joined(parts, reorder(source_ref[...]), 1, 0).astype(BF16)
            attn_ref[tokens:, :] = moved
        else:
            sums_ref[0:1, :] = gain
            sums_ref[1:2, :] = bias


def gates_back(fast, source, branch, mid, to_gate, to_up, units, scaling, vectors, sums_two, pack):
    tokens, width = mid.shape
    lead, _, per, _ = pack.shape
    blocks = 4
    shape = jax.ShapeDtypeStruct
    full = lambda *dims: pl.BlockSpec(dims, lambda i: (0,) * len(dims))
    flat = full(tokens, width)
    column = pl.BlockSpec((tokens, width), lambda i: (0, i))
    rows = tokens + (16 if fast else 0)
    return pl.pallas_call(
        lambda *refs: gates_kernel(fast, *refs),
        grid=(blocks,),
        in_specs=[flat, flat, column, column, flat, full(tokens, 1), full(4, width),
                  full(2, width), full(1, width),
                  pl.BlockSpec((lead, 1, per, width), lambda i: (0, i, 0, 0)),
                  pl.BlockSpec((lead, 1, per, width), lambda i: (0, 4 + i, 0, 0)),
                  down_spec(pack)],
        out_specs=[pl.BlockSpec((2, 1, tokens, width), lambda i: (0, i, 0, 0)), flat,
                   full(rows, width), full(2, width)],
        out_shape=[shape((2, blocks, tokens, width), BF16), shape((tokens, width), F32),
                   shape((rows, width), BF16), shape((2, width), F32)],
        scratch_shapes=[pltpu.VMEM((tokens, width), F32)],
        compiler_params=params(30),
        cost_estimate=LONG,
    )(branch, mid, to_gate, to_up, units, scaling, vectors, sums_two, source, pack, pack, pack)


def attend_back_kernel(
    wout_ref, cos_ref, sin_ref, mark_ref, markt_ref, q_ref, k_ref, v_ref, grad_ref, *refs
):
    mixed_ref, bias_ref, gatt_ref = refs[-3:]
    tokens, width = q_ref.shape
    pair = 2 * HD
    cosine, sine = cos_ref[...], sin_ref[...]
    bias_ref[...] = jnp.where(mark_ref[...] == markt_ref[...], 0.0, MASKED)
    gatt_ref[...] = joined(grad_ref[...], wout_ref[:, 0].reshape(width, width), 1, 1).astype(BF16)
    first_half = lax.broadcasted_iota(jnp.int32, (tokens, pair), 1) < HD
    for at in range(0, width, pair):
        query = q_ref[:, at : at + pair]
        key = k_ref[:, at : at + pair]
        value = v_ref[:, at : at + pair]
        grad_out = gatt_ref[:, at : at + pair]
        found = []
        for half in range(2):
            inside = first_half if half == 0 else jnp.logical_not(first_half)
            scores = (
                joined(jnp.where(inside, key, jnp.zeros_like(key)), query, 1, 1) * HD**-0.5
                + bias_ref[...]
            )
            raised = jnp.exp(scores - jnp.max(scores, axis=0, keepdims=True))
            probs = raised * (1.0 / jnp.sum(raised, axis=0, keepdims=True))
            grad_probs = joined(
                jnp.where(inside, value, jnp.zeros_like(value)), grad_out, 1, 1
            )
            delta = jnp.sum(probs * grad_probs, axis=0, keepdims=True)
            grad_scores = (probs * (grad_probs - delta)).astype(BF16)
            found.append(
                (
                    joined(grad_scores, key, 0, 0),
                    joined(grad_scores, query, 1, 0),
                    joined(probs.astype(BF16), grad_out, 1, 0),
                )
            )
        grad_query = jnp.where(first_half, found[0][0], found[1][0]) * HD**-0.5
        grad_key = jnp.where(first_half, found[0][1], found[1][1]) * HD**-0.5
        grad_value = jnp.where(first_half, found[0][2], found[1][2])
        mixed_ref[0, :, at : at + pair] = (
            grad_query * cosine - partner(grad_query) * sine
        ).astype(BF16)
        mixed_ref[1, :, at : at + pair] = (
            grad_key * cosine - partner(grad_key) * sine
        ).astype(BF16)
        mixed_ref[2, :, at : at + pair] = grad_value.astype(BF16)


def attend_back(pack, cosine, sine, labels, query, key, value, grad, after=()):
    tokens, width = query.shape
    lead, _, per, _ = pack.shape
    full = lambda *dims: pl.BlockSpec(dims, lambda i: (0,) * len(dims))
    flat = full(tokens, width)
    mark = labels.astype(F32)
    return pl.pallas_call(
        attend_back_kernel,
        grid=(1,),
        in_specs=[pl.BlockSpec((lead, 1, per, width), lambda i: (0, 8, 0, 0)),
                  full(tokens, 2 * HD), full(tokens, 2 * HD), full(tokens, 1), full(1, tokens)]
        + [flat] * 4 + [pl.BlockSpec(memory_space=pl.ANY)] * len(after),
        out_specs=full(3, tokens, width),
        out_shape=jax.ShapeDtypeStruct((3, tokens, width), BF16),
        scratch_shapes=[pltpu.VMEM((tokens, tokens), F32), pltpu.VMEM((tokens, width), BF16)],
        compiler_params=params(30),
        cost_estimate=LONG,
    )(pack, cosine, sine, mark[:, None], mark[None, :], query, key, value, grad, *after)


def tokens_kernel(mixed_ref, hid_ref, wqkv_ref, *refs):
    tokens, width = hid_ref.shape
    back = hid_ref[...]
    for part in range(3):
        back += joined(mixed_ref[part], wqkv_ref[:, part].reshape(width, width), 1, 1)
    refs[-1][...] = back


def tokens_back(mixed, hidden, pack, after=()):
    tokens, width = hidden.shape
    lead, _, per, _ = pack.shape
    full = lambda *dims: pl.BlockSpec(dims, lambda i: (0,) * len(dims))
    return pl.pallas_call(
        tokens_kernel,
        grid=(1,),
        in_specs=[full(3, tokens, width), full(tokens, width),
                  pl.BlockSpec((lead, 3, per, width), lambda i: (0, 3, 0, 0))]
        + [pl.BlockSpec(memory_space=pl.ANY)] * len(after),
        out_specs=full(tokens, width),
        out_shape=jax.ShapeDtypeStruct((tokens, width), F32),
        compiler_params=params(),
        cost_estimate=LONG,
    )(mixed, hidden, pack, *after)


def both(own_left, got_left, own_right, got_right):
    return (joined(own_left, own_right, 0, 0) + joined(got_left, got_right, 0, 0)).astype(BF16)


def steps_call(kernel, grid, ins, args, outs, shapes, scalars=None, after=()):
    ins = ins + [pl.BlockSpec(memory_space=pl.ANY)] * len(after)
    shapes = [jax.ShapeDtypeStruct(dims, BF16) for dims in shapes]
    more = dict(out_shape=shapes, compiler_params=params(30), cost_estimate=LONG)
    if scalars is None:
        return pl.pallas_call(
            kernel, grid=grid, in_specs=ins, out_specs=outs, **more
        )(*args, *after)
    return pl.pallas_call(
        kernel,
        grid_spec=pltpu.PrefetchScalarGridSpec(
            num_scalar_prefetch=1, grid=grid, in_specs=ins, out_specs=outs
        ),
        **more,
    )(scalars, *args, *after)


def down_kernel(own_ref, got_ref, grad_ref, got_grad_ref, *refs):
    held_ref, moving_ref = refs[-2:]
    value = both(own_ref[0], got_ref[0], grad_ref[...], got_grad_ref[...])
    half = value.shape[0] // 2
    held_ref[0] = value[:half]
    moving_ref[0] = value[half:]


def down_grads(own, got, grad, got_grad, after=()):
    blocks, tokens, rows = own.shape
    width = grad.shape[1]
    left = pl.BlockSpec((1, tokens, rows), lambda i: (i, 0, 0))
    right = pl.BlockSpec((tokens, width), lambda i: (0, 0))
    out = pl.BlockSpec((1, rows // 2, width), lambda i: (i, 0, 0))
    dims = (blocks, rows // 2, width)
    return steps_call(
        down_kernel, (blocks,), [left, left, right, right], (own, got, grad, got_grad),
        [out, out], [dims, dims], after=after,
    )


def first_kernel(own_ref, got_ref, grad_ref, got_grad_ref, *refs):
    held_ref, moving_ref = refs[-2:]
    value = both(own_ref[0], got_ref[0], grad_ref[0, 0], got_grad_ref[0, 0])
    half = value.shape[0] // 2
    held_ref[...] = value[:half].reshape(held_ref.shape)
    moving_ref[...] = value[half:].reshape(held_ref.shape)


def first_grads(own, got, grads, got_grads, which, part, after=()):
    _, tokens, rows = own.shape
    _, chunks, _, width = grads.shape
    left = pl.BlockSpec((1, tokens, rows), lambda i: (part, 0, 0))
    right = pl.BlockSpec((1, 1, tokens, width), lambda i: (which, i, 0, 0))
    out = pl.BlockSpec((4, 1, rows // 8, width), lambda i: (0, i, 0, 0))
    dims = (4, chunks, rows // 8, width)
    return steps_call(
        first_kernel, (chunks,), [left, left, right, right], (own, got, grads, got_grads),
        [out, out], [dims, dims], after=after,
    )


def tower_kernel(tower_ref, own_ref, got_ref, grad_ref, got_grad_ref, *refs):
    held_ref, lent_ref = refs[-2:]
    value = both(own_ref[0], got_ref[0], grad_ref[0, 0], got_grad_ref[0, 0])
    value = value.reshape(held_ref.shape)
    here = pl.program_id(0) < pl.num_programs(0) // 2

    @pl.when(here)
    def _():
        held_ref[...] = value

    @pl.when(jnp.logical_not(here))
    def _():
        lent_ref[...] = value


def tower_grads(tower, own, got, grads, got_grads, which, chunks, first, part, after=()):
    _, tokens, rows = own.shape
    width = grads.shape[-1]
    half = chunks // 2
    left = pl.BlockSpec((1, tokens, rows), lambda i, t: (part, 0, 0))
    right = pl.BlockSpec(
        (1, 1, tokens, width), lambda i, t: (which, first + (i + half * t[0]) % chunks, 0, 0)
    )
    block = (2, 4, 1, rows // 8, width)
    dims = (2, 4, half, rows // 8, width)
    outs = [
        pl.BlockSpec(block, lambda i, t: (0, 0, jnp.minimum(i, half - 1), 0, 0)),
        pl.BlockSpec(block, lambda i, t: (0, 0, jnp.maximum(i - half, 0), 0, 0)),
    ]
    return steps_call(
        tower_kernel, (chunks,), [left, left, right, right], (own, got, grads, got_grads),
        outs, [dims, dims], scalars=tower, after=after,
    )


def rest_kernel(own_ref, got_ref, attn_ref, got_attn_ref, mixed_ref, got_mixed_ref, *refs):
    held_ref, moving_ref = refs[-2:]
    tokens, width = mixed_ref.shape[1:]
    half = width // 4
    pieces = [
        both(own_ref[1], got_ref[1], attn_ref[0:tokens, :], got_attn_ref[0:tokens, :]),
        both(own_ref[0], got_ref[0], mixed_ref[0], got_mixed_ref[0]),
    ]
    parts = attn_ref[tokens:, : width // 2].astype(F32)
    got = got_attn_ref[tokens:, width // 2 :].astype(F32)
    values = parts[0:4] + parts[4:8] + got[0:4] + got[4:8]
    upper = values.astype(BF16).astype(F32)
    blank = jnp.zeros((PAD - 2 * VECTORS, width // 2), F32)
    pieces.append(jnp.concatenate([upper, values - upper, blank], axis=0).T.astype(BF16))
    at = 0
    for piece in pieces:
        columns = piece.shape[1]
        for k, out_ref in enumerate((held_ref, moving_ref)):
            out_ref[:, :, at : at + columns] = piece[k * 2 * half // 2 : (k + 1) * half].reshape(
                4, -1, columns
            )
        at += columns


def rest_grads(own, got, attn, got_attn, mixed, got_mixed, after=()):
    _, tokens, rows = own.shape
    width = mixed.shape[2]
    full = lambda *dims: pl.BlockSpec(dims, lambda i: (0,) * len(dims))
    one = pl.BlockSpec((1, tokens, width), lambda i: (0, 0, 0))
    dims = (4, rows // 8, 2 * width + PAD)
    return steps_call(
        rest_kernel, (1,),
        [full(*own.shape), full(*own.shape), full(*attn.shape), full(*attn.shape), one, one],
        (own, got, attn, got_attn, mixed, got_mixed),
        [full(*dims)] * 2, [dims, dims], after=after,
    )


def reduce_digit(parts, sizes, place, digit):
    size = sizes[place]
    total = pick(parts, 0, digit).astype(F32)
    for shift in range(1, size):
        sent = pick(parts, 0, (digit + shift) % size).astype(BF16)
        total += lax.ppermute(sent, "dp", digit_shift(sizes, place, shift)).astype(F32)
    return total


def shared_sum(grad, sizes, digits, tower_index):
    rows, columns = grad.shape
    count = math.prod(sizes)
    per = rows // count
    tiles = columns // 128
    side = max(1, round(tiles * 0.3)) * 128
    middle = columns - 2 * side
    last = len(sizes) - 1
    blocks = grad.astype(BF16).reshape(count // sizes[last], sizes[last], per, columns)
    chip = reduce_digit(jnp.moveaxis(blocks, 1, 0), sizes, last, digits[last]).astype(BF16)
    lead = chip.shape[0]
    mine = lax.dynamic_slice(chip, (0, 0, tower_index * (columns - side)), (lead, per, side))
    other = lax.dynamic_slice(
        chip, (0, 0, (1 - tower_index) * (columns - side)), (lead, per, side)
    )
    mine = mine.astype(F32) + lax.ppermute(other, "tower", SWAP).astype(F32)
    part = jnp.concatenate([mine.astype(BF16), chip[:, :, side : side + middle]], axis=2)
    for place in range(last - 1, -1, -1):
        size = sizes[place]
        part = jnp.moveaxis(part.reshape(part.shape[0] // size, size, per, side + middle), 1, 0)
        part = reduce_digit(part, sizes, place, digits[place]).astype(BF16)
    part = part[0]
    back = lax.ppermute(part, "tower", SWAP).astype(F32)
    part = part.astype(F32)
    centre = part[:, side:] + back[:, side:]
    first = tower_index == 0
    return jnp.concatenate(
        [
            jnp.where(first, part[:, :side], back[:, :side]),
            centre,
            jnp.where(first, back[:, :side], part[:, :side]),
        ],
        axis=1,
    )


def plus_kernel(jobs, count, z_ref, *refs):
    for out_ref, (terms, vectors) in zip(refs[count:], jobs, strict=True):
        total = None
        for place, index in terms:
            piece = refs[place][index(z_ref[0]) if callable(index) else index].astype(F32)
            total = piece if total is None else total + piece
        total = total.reshape(out_ref.shape)
        if vectors:
            at = total.shape[-1] - PAD
            parts = total[..., at:].reshape(-1, PAD)
            lane = lax.broadcasted_iota(jnp.int32, parts.shape, 1)
            values = parts + pltpu.roll(parts, PAD - VECTORS, 1)
            upper = values.astype(BF16).astype(F32)
            lower = pltpu.roll(values - upper, VECTORS, 1)
            parts = jnp.where(lane < VECTORS, upper, jnp.where(lane < 2 * VECTORS, lower, 0.0))
            out_ref[..., :at] = total[..., :at].astype(BF16)
            out_ref[..., at:] = parts.astype(BF16).reshape(*out_ref.shape[:-1], PAD)
        else:
            out_ref[...] = total.astype(BF16)


def plus(jobs, z, after=()):
    inputs, outs, shapes = [], [], []
    for arrays, plan, dims, vectors in jobs:
        base = len(inputs)
        inputs += arrays
        outs += [([(base + place, index) for place, index in terms], vectors) for terms in plan]
        shapes += dims
    count = len(inputs)
    spec = lambda dims: pl.BlockSpec(dims, lambda i: (0,) * len(dims))
    return pl.pallas_call(
        lambda *refs: plus_kernel(
            outs, count, *refs[: 1 + count], *refs[1 + count + len(after) :]
        ),
        grid=(1,),
        in_specs=[pl.BlockSpec(memory_space=pltpu.SMEM)]
        + [spec(a.shape) for a in inputs]
        + [pl.BlockSpec(memory_space=pl.ANY)] * len(after),
        out_specs=[spec(dims) for dims in shapes],
        out_shape=[jax.ShapeDtypeStruct(dims, BF16) for dims in shapes],
        compiler_params=params(24),
        cost_estimate=SHORT,
    )(z, *inputs, *after)


class GradSum:
    def __init__(self, pair, sizes, z, by_tower, direct, vectors=False):
        self.sizes = sizes
        self.z = z
        self.direct = direct
        self.vectors = vectors
        self.by_tower = by_tower
        self.held, sent = pair
        self.got = lax.ppermute(sent, "tower", SWAP) if by_tower else self.shift_y(sent)
        self.steps = ["tower", "y", "z"] if by_tower else ["y", "z"]

    def shift_y(self, sent):
        return lax.ppermute(sent, "dp", digit_shift(self.sizes, 1, 1))

    def job(self):
        step = self.steps[0]
        if step == "tower":
            plan = [[(0, (k,)), (1, (k,))] for k in (1, 0)]
            return [self.held, self.got], plan, [self.held.shape[1:]] * 2, self.vectors
        depth = self.sizes[0]
        if step == "y" and self.direct:
            views = [lambda z, k=k: ((z + k) % depth,) for k in (1, 2, 3, 0)]
            plan = [[(0, view), (1, view)] for view in views]
            return [self.held, self.got], plan, [self.held.shape[1:]] * depth, self.vectors
        if step == "y":
            plan = [[(0, (Ellipsis,)), (1, (Ellipsis,))]]
            return [self.held, self.got], plan, [self.held.shape], self.vectors
        if self.direct:
            plan = [[(k, (Ellipsis,)) for k in range(depth)]]
            return [self.held, *self.got], plan, [self.held.shape], self.vectors
        plan = [[(0, (k,)) for k in range(depth)]]
        return [self.got], plan, [self.got.shape[1:]], self.vectors

    def take(self, outs):
        step = self.steps.pop(0)
        if step == "tower":
            moving, self.held = outs
            self.got = self.shift_y(moving)
        elif step == "y" and self.direct:
            *parts, self.held = outs
            self.got = [
                lax.ppermute(part, "dp", digit_shift(self.sizes, 0, k + 1))
                for k, part in enumerate(parts)
            ]
        elif step == "y":
            depth, rest = self.sizes[0], math.prod(self.sizes[1:])
            groups = [[z * rest + other for z in range(depth)] for other in range(rest)]
            self.got = lax.all_to_all(outs[0], "dp", 0, 0, axis_index_groups=groups, tiled=True)
        else:
            (self.held,) = outs
            self.got = lax.ppermute(self.held, "tower", SWAP)

    def result(self, tower_index):
        first = tower_index == 0
        return jnp.where(first, self.held, self.got), jnp.where(first, self.got, self.held)


def advance(order, *sums, done=()):
    jobs = [one.job() for one in sums]
    outs = plus(jobs, sums[0].z, (order, *(one.got for one in done)))
    last = outs[-1]
    for one, (_, plan, _, _) in zip(sums, jobs, strict=True):
        one.take(outs[: len(plan)])
        outs = outs[len(plan) :]
    return last


def sum_norms(sums_one, sums_two, dp_count):
    sums = jnp.concatenate([sums_one, sums_two], axis=0)
    sums = sums.reshape(4, dp_count, -1).transpose(1, 0, 2)
    sums = jnp.concatenate([sums, sums], axis=0)
    return jnp.sum(lax.all_to_all(sums, ("tower", "dp"), 0, 0, tiled=True), axis=0)


def finish_kernel(plan, count, *refs):
    for out_ref, terms in zip(refs[count:], plan, strict=True):
        for to, places, index in terms:
            total = refs[places[0]][index].astype(F32)
            for place in places[1:]:
                total += refs[place][index].astype(F32)
            out_ref[to] = total


def finish(inputs, plan, shapes, after=()):
    count = len(inputs)
    spec = lambda dims: pl.BlockSpec(dims, lambda i: (0,) * len(dims))
    return pl.pallas_call(
        lambda *refs: finish_kernel(plan, count, *refs[:count], *refs[count + len(after) :]),
        grid=(1,),
        in_specs=[spec(a.shape) for a in inputs]
        + [pl.BlockSpec(memory_space=pl.ANY)] * len(after),
        out_specs=[spec(dims) for dims in shapes],
        out_shape=[jax.ShapeDtypeStruct(dims, F32) for dims in shapes],
        compiler_params=params(24),
        cost_estimate=SHORT,
    )(*inputs, *after)


def beside(chunks):
    return jnp.concatenate(list(chunks), axis=1)


def column_orders(digits, per, spread, width):
    _, y, c = digits
    place = jnp.arange(width, dtype=jnp.int32)
    block, row = place // per, place % per
    core, dy, z = block // 8, block // 4 % 2, block % 4
    source = ((z * 4 + (dy + y) % 2 * 2 + (core + c) % 2)) * per + row
    device = (dy + y) % 2 * 2 + (core + c) % 2
    return source[None], ((device * spread + block % 4) * per + row)[None]


def body(
    tokens,
    lengths,
    pos_doc,
    w_qkv,
    w_out,
    w_gate,
    w_up,
    w_down,
    ln1_gain,
    ln1_bias,
    ln2_gain,
    ln2_bias,
):
    dp_count = lax.axis_size("dp")
    device_count = 2 * dp_count
    sizes = split_dp(dp_count)
    dp_index = lax.axis_index("dp")
    tower_index = lax.axis_index("tower")
    digits = digits_of(dp_index, sizes)
    per, narrow = w_out.shape
    wide = w_gate.shape[1]
    spread = wide // narrow

    own_pack = pack_own(w_gate, w_up, w_out, w_qkv, w_down)
    pack = lax.all_gather(own_pack, "dp", axis=0, tiled=True)
    pack = pack.reshape(dp_count, 4 * spread, per, narrow)
    if per % 16:
        front = pack[:, : 3 * spread].transpose(1, 0, 2, 3).reshape(3 * spread, narrow, narrow)
        back = pack[:, 3 * spread :].reshape(spread, narrow, narrow)
        pack = jnp.concatenate([front, back], axis=0)[None]
    vectors_own = jnp.stack([ln1_gain, ln1_bias, ln2_gain, ln2_bias])
    vectors = lax.all_to_all(
        jnp.broadcast_to(vectors_own[None], (dp_count, 4, per)), "dp", 0, 0, tiled=True
    )
    vectors = vectors.transpose(1, 0, 2).reshape(4, narrow).astype(F32)

    rows_in = tokens[0]
    row_count = rows_in.shape[0]
    pooling, labels, offsets = layout(lengths[0], row_count)
    pool_t = pooling.T
    cosine, sine = rotary_tables(offsets)

    fast = sizes == [4, 2, 2] and spread == 4 and per % 16 == 0
    source, source_down = column_orders(digits, per, spread, narrow) if fast else (
        jnp.zeros((1, narrow), jnp.int32),
    ) * 2
    core_swap = digit_shift(sizes, len(sizes) - 1, 1)
    swap_cores = lambda values: lax.ppermute(values, "dp", core_swap)
    (query, key, value, attended, first_low, unit_one, scale_one, unit_two, scale_two, pooled,
     unit_vectors, active, to_gate, to_up) = forward(
        rows_in, pack, cosine, sine, labels, vectors, pool_t
    )
    seq_count = unit_vectors.shape[0]
    everyone = lax.all_to_all(
        jnp.broadcast_to(unit_vectors[None], (device_count,) + unit_vectors.shape),
        ("tower", "dp"),
        0,
        0,
        tiled=True,
    ).reshape(device_count * seq_count, narrow)
    if fast:
        own, lent, own_active, lent_active = halves(
            rows_in, attended, first_low, active, source, source_down
        )
    loss_value, grad_mid, grad_branch, sums_two = loss_and_grad(
        everyone, pos_doc, tower_index, dp_index, unit_vectors, pooled, pool_t, unit_two, scale_two,
        vectors, (own,) if fast else (),
    )
    grad_feed, grad_hidden, grad_attn, sums_one = gates_back(
        fast, source, grad_branch, grad_mid, to_gate, to_up, unit_one, scale_one, vectors, sums_two,
        pack,
    )
    heads_args = (pack, cosine, sine, labels, query, key, value, grad_attn)
    if fast:
        got, got_active = swap_cores(lent), swap_cores(lent_active)
        got_branch = swap_cores(grad_branch)
        got_feed = swap_cores(grad_feed)
        got_attn = swap_cores(grad_attn)
        tower = tower_index.reshape(1).astype(jnp.int32)
        plain = lambda pair, **how: GradSum(pair, sizes, digits[0].reshape(1), **how)
        sums, order, late = {}, grad_hidden, []
        for step in ORDER:
            after = (order,)
            if step == "down":
                pair = down_grads(own_active, got_active, grad_branch, got_branch, after)
                sums["d"] = plain(pair, by_tower=False, direct="d" in DIRECT)
                order = pair[0]
            elif step == "heads":
                grad_mixed = attend_back(*heads_args, (order, got_attn))
                got_mixed = swap_cores(grad_mixed)
                order = grad_mixed
            elif step == "gate":
                pair = tower_grads(tower, own, got, grad_feed, got_feed, 0, 4, 0, 2, after)
                sums["g"] = plain(pair, by_tower=True, direct="g" in DIRECT)
                order = pair[0]
            elif step == "up":
                pair = first_grads(own, got, grad_feed, got_feed, 1, 2, after)
                sums["u"] = plain(pair, by_tower=False, direct="u" in DIRECT)
                order = pair[0]
            elif step == "rest":
                pair = rest_grads(own, got, grad_attn, got_attn, grad_mixed, got_mixed, after)
                sums["r"] = plain(pair, by_tower=False, direct="r" in DIRECT, vectors=True)
                order = pair[0]
            elif step == "last":
                pair = tower_grads(
                    tower, own, got, grad_mixed[None], got_mixed[None], 0, 2, 1, 0, after
                )
                sums["l"] = plain(pair, by_tower=True, direct="l" in DIRECT)
                order = pair[0]
            elif step == "tokens":
                grad_rows = order = tokens_back(grad_mixed, grad_hidden, pack, after)
            else:
                ready = [one for one in late if one.age > 0]
                late = [one for one in late if one.age == 0]
                for one in late:
                    one.age += 1
                moving = [sums[name] for name in step]
                order = advance(order, *moving, done=ready)
                for one in moving:
                    if not one.steps:
                        one.age = 0
                        late.append(one)
        down, gate, up, rest, last = (sums[name] for name in "dgurl")
        columns = lambda k: (slice(None), slice(k * narrow, (k + 1) * narrow))
        sum_down, sum_up = finish(
            [down.held, down.got, up.held, up.got],
            [
                [((Ellipsis,), (0, 1), (Ellipsis,))],
                [(columns(k), (2, 3), (k,)) for k in range(spread)],
            ],
            [down.held.shape, (per, wide)],
        )
        lower, upper = gate.result(tower_index)
        (sum_gate,) = finish(
            [lower, upper],
            [[(columns(k), (k // 2,), (k % 2,)) for k in range(spread)]],
            [(per, wide)],
        )
        key_value = last.result(tower_index)
        sum_out, sum_qkv, norms = finish(
            [rest.held, rest.got, *key_value],
            [
                [((Ellipsis,), (0, 1), columns(0))],
                [(columns(0), (0, 1), columns(1)), (columns(1), (2,), (0,)), (columns(2), (3,), (0,))],
                [((Ellipsis,), (0, 1), (slice(None), slice(2 * narrow, 2 * narrow + PAD)))],
            ],
            [(per, narrow), (per, 3 * narrow), (per, PAD)],
        )
        norms = norms.T
        sums = norms[:VECTORS] + norms[VECTORS : 2 * VECTORS]
    else:
        grad_mixed = attend_back(*heads_args)
        grad_rows = tokens_back(grad_mixed, grad_hidden, pack)
        grad_down = joined(active, grad_branch, 0, 0)
        down_rows = (
            grad_down.reshape(dp_count, spread, per, narrow)
            .transpose(0, 2, 1, 3)
            .reshape(narrow, wide)
        )
        share = lambda grad: shared_sum(grad, sizes, digits, tower_index)
        sum_down = share(down_rows).reshape(per, spread, narrow).transpose(1, 0, 2)
        sum_down = sum_down.reshape(wide // dp_count, narrow)
        sum_gate, sum_up = (
            share(joined(first_low, beside(grad_feed[k]), 0, 0)) for k in range(2)
        )
        sum_out = share(joined(attended, grad_attn, 0, 0))
        sum_qkv = share(joined(rows_in, beside(grad_mixed), 0, 0))
        sums = sum_norms(sums_one, sums_two, dp_count)
    return (
        loss_value.reshape(()),
        unit_vectors[None],
        grad_rows[None],
        sum_qkv,
        sum_out,
        sum_gate,
        sum_up,
        sum_down,
        sums[0],
        sums[1],
        sums[2],
        sums[3],
    )


def solution(mesh):
    placed = (
        P("tower", "dp", None),
        P("tower", "dp"),
        P(),
        P("dp", None),
        P("dp", None),
        P("dp", None),
        P("dp", None),
        P("dp", None),
        P("dp"),
        P("dp"),
        P("dp"),
        P("dp"),
    )
    return jax.shard_map(
        body,
        mesh=mesh,
        in_specs=placed,
        out_specs=(
            P(),
            P("tower", "dp", None),
            P("tower", "dp", None),
            P("dp", None),
            P("dp", None),
            P("dp", None),
            P("dp", None),
            P("dp", None),
            P("dp"),
            P("dp"),
            P("dp"),
            P("dp"),
        ),
        check_vma=False,
    )
```
